256 devices in a mesh: grp: 8 (over y, core), col: 32 (over z, x).
Axes of the slice: x: 4, y: 4, z: 8, core: 2. Of those that a mesh axis runs over, the one named last changes fastest.
Arguments:
- conductance: float32 [4, 128, 8192], P(None, 'grp', 'col'), may hold values from 0.1 to 10
- shift: float32 [128, 8192], P('grp', 'col'), may hold values from 0.05 to 1
- lanczos_vector: float32 [8, 128, 8192], P(None, 'grp', 'col'), may hold values from -6 to 6
- previous: float32 [8, 128, 8192], P(None, 'grp', 'col'), may hold values from -4 to 4
Outputs:
- next_vector: float32 [8, 128, 8192], P(None, 'grp', 'col')
- coefficients: float32 [2, 8], replicated
The draws below stay inside these ranges and needn't reach their ends.
All inputs are finite; a program needn't handle non-finite values.
Results may differ from the reference program's by a relative error of at most 0.000043.
Values sent between devices are 32-bit elements; how exact they have to be, the bound alone decides.
A program may use at most 128 MiB of HBM per device.

```python
import math
import jax
import jax.numpy as jnp
from jax import lax

PROBES = 8
LEVELS = 4
SWEEPS = 2
NX = 128
NY = 8192


def block_levels(own_key, dims, shards, least, top_value):
    factor_of = 1.0
    for dim, shards_of in shards:
        draws = jax.random.uniform(jax.random.fold_in(jax.random.fold_in(own_key, 6), dim), (shards_of,), jnp.float32, least / len(shards), top_value / len(shards))
        factor_of = factor_of * jnp.repeat(jnp.exp(draws), dims[dim] // shards_of).reshape((-1,) + (1,) * (len(dims) - 1 - dim))
    return factor_of


def gaussian(own_key, dims, width, bound, cuts=(), kind=jnp.bfloat16):
    array = jax.random.normal(own_key, dims, jnp.float32) * width
    if len(cuts) > 0:
        array = block_levels(own_key, dims, cuts, -0.22, 0.18) * array
    return jnp.clip(array, min=-bound, max=bound).astype(kind)


def setup_inputs(seed: int = 0) -> dict:
    key_of = jax.random.split(jax.random.key(seed), 5)
    conductance = jnp.clip(jnp.exp(math.log(10.0) - 4.6051702 * jax.random.uniform(key_of[0], (4, NX, NY), jnp.float32) ** block_levels(key_of[0], (4, NX, NY), ((1, 8), (2, 32)), -0.2, 0.2)), 0.1, 10.0)
    shift = jnp.clip(jnp.exp(math.log(1.0) - 2.9957323 * jax.random.uniform(key_of[1], (NX, NY), jnp.float32) ** block_levels(key_of[1], (NX, NY), ((0, 8), (1, 32)), -0.2, 0.2)), 0.05, 1.0)
    lanczos_vector = gaussian(key_of[2], (PROBES, NX, NY), 1.0, 6.0, ((1, 8), (2, 32)), jnp.float32)
    previous = gaussian(key_of[3], (PROBES, NX, NY), 0.5, 4.0, ((1, 8), (2, 32)), jnp.float32)
    return {"conductance": conductance, "shift": shift, "lanczos_vector": lanczos_vector, "previous": previous}


OFFSETS = tuple(((row_step, col_step) for row_step in (-1, 0, 1) for col_step in (-1, 0, 1)))
EPSILON = 1e-06

def slot(row_step, col_step):
    return (row_step + 1) * 3 + col_step + 1

def zero_pad(field):
    return jnp.pad(field, ((0, 0), (1, 1), (1, 1)))

def window(beside_all, row_step, col_step, rows, cols):
    return beside_all[:, 1 + row_step:1 + row_step + rows, 1 + col_step:1 + col_step + cols]

def apply_stencil(stencil, beside_all):
    rows, cols = (stencil.shape[1], stencil.shape[2])
    total = stencil[4] * window(beside_all, 0, 0, rows, cols)
    for offset_index, (row_step, col_step) in enumerate(OFFSETS):
        if offset_index != 4:
            total = total + stencil[offset_index] * window(beside_all, row_step, col_step, rows, cols)
    return total

def grid_index(rows, cols, row_start, col_start):
    row_index = jnp.broadcast_to(row_start + jnp.arange(rows, dtype=jnp.int32)[:, None], (rows, cols))
    col_index = jnp.broadcast_to(col_start + jnp.arange(cols, dtype=jnp.int32)[None, :], (rows, cols))
    return (row_index, col_index)

def fine_stencil(conductance, shift, padder, row_start, col_start, total_rows, total_cols):
    rows, cols = shift.shape
    row_index, col_index = grid_index(rows, cols, row_start, col_start)
    south_ok = row_index < total_rows - 1
    east_ok = col_index < total_cols - 1
    west_ok = col_index > 0
    masks = jnp.stack([east_ok, south_ok, south_ok & east_ok, south_ok & west_ok]).astype(jnp.float32)
    owned = conductance * masks
    beside_all = padder(owned)
    pieces = [None] * 9
    pieces[slot(0, 1)] = -owned[0]
    pieces[slot(0, -1)] = -window(beside_all, 0, -1, rows, cols)[0]
    pieces[slot(1, 0)] = -owned[1]
    pieces[slot(-1, 0)] = -window(beside_all, -1, 0, rows, cols)[1]
    pieces[slot(1, 1)] = -owned[2]
    pieces[slot(-1, -1)] = -window(beside_all, -1, -1, rows, cols)[2]
    pieces[slot(1, -1)] = -owned[3]
    pieces[slot(-1, 1)] = -window(beside_all, -1, 1, rows, cols)[3]
    center = shift
    for offset_index in range(9):
        if offset_index != 4:
            center = center - pieces[offset_index]
    pieces[4] = center
    return jnp.stack(pieces)

def dendy(stencil, padder):
    vert = stencil[:, 1::2, 0::2]
    up_sum = vert[slot(-1, -1)] + vert[slot(-1, 0)] + vert[slot(-1, 1)]
    down_sum = vert[slot(1, -1)] + vert[slot(1, 0)] + vert[slot(1, 1)]
    vert_mid = vert[slot(0, -1)] + vert[4] + vert[slot(0, 1)]
    weight_up = -up_sum / vert_mid
    weight_down = -down_sum / vert_mid
    horiz = stencil[:, 0::2, 1::2]
    left_sum = horiz[slot(-1, -1)] + horiz[slot(0, -1)] + horiz[slot(1, -1)]
    right_sum = horiz[slot(-1, 1)] + horiz[slot(0, 1)] + horiz[slot(1, 1)]
    horiz_mid = horiz[slot(-1, 0)] + horiz[4] + horiz[slot(1, 0)]
    weight_left = -left_sum / horiz_mid
    weight_right = -right_sum / horiz_mid
    edges = jnp.stack([weight_up, weight_down, weight_left, weight_right])
    rows, cols = weight_up.shape
    beside_all = padder(edges)
    east_edges = window(beside_all, 0, 1, rows, cols)
    south_edges = window(beside_all, 1, 0, rows, cols)
    cell = stencil[:, 1::2, 1::2]
    corner_here = -(cell[slot(-1, -1)] + cell[slot(0, -1)] * weight_up + cell[slot(-1, 0)] * weight_left) / cell[4]
    corner_down = -(cell[slot(1, -1)] + cell[slot(0, -1)] * weight_down + cell[slot(1, 0)] * south_edges[2]) / cell[4]
    corner_right = -(cell[slot(-1, 1)] + cell[slot(0, 1)] * east_edges[0] + cell[slot(-1, 0)] * weight_right) / cell[4]
    corner_both = -(cell[slot(1, 1)] + cell[slot(0, 1)] * east_edges[1] + cell[slot(1, 0)] * south_edges[3]) / cell[4]
    return jnp.stack([weight_up, weight_down, weight_left, weight_right, corner_here, corner_down, corner_right, corner_both])

def prolong(coarse, weights, padder):
    count, rows, cols = coarse.shape
    beside_all = padder(coarse)
    below = window(beside_all, 1, 0, rows, cols)
    beside = window(beside_all, 0, 1, rows, cols)
    diagonal = window(beside_all, 1, 1, rows, cols)
    bottom_left = weights[0] * coarse + weights[1] * below
    top_right = weights[2] * coarse + weights[3] * beside
    bottom_right = weights[4] * coarse + weights[5] * below + weights[6] * beside + weights[7] * diagonal
    upper = jnp.stack([coarse, top_right], axis=-1)
    lower = jnp.stack([bottom_left, bottom_right], axis=-1)
    return jnp.stack([upper, lower], axis=2).reshape(count, 2 * rows, 2 * cols)

def restrict(fine, weights, padder):
    count = fine.shape[0]
    even_even = fine[:, 0::2, 0::2]
    odd_even = fine[:, 1::2, 0::2]
    even_odd = fine[:, 0::2, 1::2]
    odd_odd = fine[:, 1::2, 1::2]
    rows, cols = (even_even.shape[1], even_even.shape[2])
    coarse = even_even + weights[0] * odd_even + weights[2] * even_odd + weights[4] * odd_odd
    outgoing = jnp.concatenate([weights[1] * odd_even + weights[5] * odd_odd, weights[3] * even_odd + weights[6] * odd_odd, weights[7] * odd_odd], axis=0)
    beside_all = padder(outgoing)
    coarse = coarse + window(beside_all, -1, 0, rows, cols)[:count]
    coarse = coarse + window(beside_all, 0, -1, rows, cols)[count:2 * count]
    coarse = coarse + window(beside_all, -1, -1, rows, cols)[2 * count:]
    return coarse

def galerkin(stencil, weights, padder, row_start, col_start, colors):
    rows, cols = (stencil.shape[1] // 2, stencil.shape[2] // 2)
    row_index, col_index = grid_index(rows, cols, row_start, col_start)
    color_map = row_index % 3 * 3 + col_index % 3
    probes = jnp.stack([(color_map == color).astype(jnp.float32) for color in colors])
    lifted = prolong(probes, weights, padder)
    image = restrict(apply_stencil(stencil, padder(lifted)), weights, padder)
    entries = []
    for row_step, col_step in OFFSETS:
        target = (row_index + row_step) % 3 * 3 + (col_index + col_step) % 3
        entry = jnp.zeros((rows, cols), jnp.float32)
        for position, color in enumerate(colors):
            entry = entry + image[position] * (target == color).astype(jnp.float32)
        entries.append(entry)
    return jnp.stack(entries)

def parity(rows, cols, row_start, col_start):
    row_index, col_index = grid_index(rows, cols, row_start, col_start)
    red_mask = ((row_index + col_index) % 2 == 0).astype(jnp.float32)
    return (red_mask, 1.0 - red_mask)

def relax(field, right, stencil, color_mask, padder):
    return field + color_mask * (right - apply_stencil(stencil, padder(field))) / stencil[4]

def smooth_from_zero(right, stencil, masks, padder):
    red_mask, black_mask = masks
    field = red_mask * right / stencil[4]
    field = relax(field, right, stencil, black_mask, padder)
    for sweep_index in range(SWEEPS - 1):
        field = relax(field, right, stencil, red_mask, padder)
        field = relax(field, right, stencil, black_mask, padder)
    return field

def smooth_from(field, right, stencil, masks, padder):
    red_mask, black_mask = masks
    for sweep_index in range(SWEEPS):
        field = relax(field, right, stencil, red_mask, padder)
        field = relax(field, right, stencil, black_mask, padder)
    return field

def vcycle(level_index, right, stencils, weights_list, masks, padder, coarsest):
    if level_index == LEVELS - 1:
        return coarsest(right)
    stencil = stencils[level_index]
    field = smooth_from_zero(right, stencil, masks[level_index], padder)
    residual = right - apply_stencil(stencil, padder(field))
    coarse_right = restrict(residual, weights_list[level_index], padder)
    correction = vcycle(level_index + 1, coarse_right, stencils, weights_list, masks, padder, coarsest)
    field = field + prolong(correction, weights_list[level_index], padder)
    return smooth_from(field, right, stencil, masks[level_index], padder)

def reference(conductance, shift, lanczos_vector, previous):
    total_rows, total_cols = shift.shape
    stencils = [fine_stencil(conductance, shift, zero_pad, 0, 0, total_rows, total_cols)]
    masks = [parity(total_rows, total_cols, 0, 0)]
    weights_list = []
    rows, cols = (total_rows, total_cols)
    for level_index in range(LEVELS - 1):
        weights = dendy(stencils[-1], zero_pad)
        weights_list.append(weights)
        rows, cols = (rows // 2, cols // 2)
        coarse = galerkin(stencils[-1], weights, zero_pad, 0, 0, [0])
        for color in range(1, 9):
            coarse = coarse + galerkin(stencils[-1], weights, zero_pad, 0, 0, [color])
        stencils.append(coarse)
        masks.append(parity(rows, cols, 0, 0))

    def coarsest(right):
        return smooth_from_zero(right, stencils[-1], masks[-1], zero_pad)
    image = apply_stencil(stencils[0], zero_pad(lanczos_vector))
    solved = vcycle(0, image, stencils, weights_list, masks, zero_pad, coarsest)
    alpha = lax.optimization_barrier(jnp.mean(lanczos_vector * solved, axis=(1, 2)))
    rest = solved - alpha[:, None, None] * lanczos_vector - previous
    scale = jnp.sqrt(lax.optimization_barrier(jnp.mean(rest * rest, axis=(1, 2))) + EPSILON)
    return (rest / scale[:, None, None], jnp.stack([alpha, scale]))
```

```python
import jax
import jax.numpy as jnp
from jax import lax
from jax.experimental import pallas as pl
from jax.experimental.pallas import tpu as pltpu
from jax.sharding import PartitionSpec as P

F32 = jnp.float32
BF16 = jnp.bfloat16
EPSILON = 1e-06
LANES = 128
SUB = 8
ROWS = 16
COLS = 256
MESH = pl.DeviceIdType.MESH

LEVEL_ROWS = (16, 8, 4, 2)
LEVEL_PHASES = (4, 2, 2, 2)
LEVEL_STRIDE = (1, 1, 2, 4)
AROUND = ((-1, 0), (1, 0), (0, -1), (0, 1), (-1, -1), (-1, 1), (1, -1), (1, 1))
PLACE = {offset: index for index, offset in enumerate(AROUND)}


def turn_lanes(x, by):
    return pltpu.roll(x, by % LANES, 1)


def turn_strips(x, by):
    return pltpu.roll(x, by % SUB, 0)


def rows(count, body, per):
    if per >= count:
        for index in range(count):
            body(index)
    else:

        def step(index, carry):
            for inner in range(per):
                body(index * per + inner)
            return carry

        lax.fori_loop(0, count // per, step, 0)


class Grid:
    def __init__(self, rows_, phases, stride):
        self.rows, self.phases, self.stride = rows_, phases, stride

    @property
    def ghosted(self):
        return (self.rows + 2, self.phases + 2, SUB, LANES)

    @property
    def bare(self):
        return (self.rows, self.phases, SUB, LANES)

    def put(self, ref, t, r, x):
        ref[t + 1, r + 1] = x
        if r == 0:
            ref[t + 1, self.phases + 1] = turn_lanes(x, -self.stride)
        if r == self.phases - 1:
            ref[t + 1, 0] = turn_lanes(x, self.stride)

    def wrap(self, ref, colour=None):
        for r in range(-1, self.phases + 1):
            if colour is None or (self.rows - 1 + r) % 2 == colour:
                ref[0, r + 1] = turn_strips(ref[self.rows, r + 1], 1)
            if colour is None or r % 2 == colour:
                ref[self.rows + 1, r + 1] = turn_strips(ref[1, r + 1], -1)


GRIDS = tuple(Grid(*sizes) for sizes in zip(LEVEL_ROWS, LEVEL_PHASES, LEVEL_STRIDE))
DENSE = tuple(Grid(g.rows // 2, g.phases // 2, g.stride) for g in GRIDS[:3])


def level_scratch():
    shapes = []
    for index, grid in enumerate(GRIDS):
        entry = {
            "own": (4,) + grid.ghosted,
            "dia": grid.bare,
            "inv": grid.bare,
            "near": (8,) + grid.bare,
            "right": grid.ghosted,
            "red0": grid.ghosted,
            "red1": grid.ghosted,
            "black0": grid.ghosted,
            "black1": grid.ghosted,
        }
        if index < 3:
            dense = DENSE[index]
            entry["weights"] = (8,) + dense.ghosted
            entry["passed"] = (6,) + dense.ghosted
            entry["kept"] = (5,) + dense.bare
            entry["residual"] = grid.ghosted
            entry["lifted"] = dense.ghosted
        shapes.append({name: pltpu.VMEM(shape, F32) for name, shape in entry.items()})
    return shapes


class Level:
    def __init__(self, index, refs, per):
        self.index, self.grid, self.per = index, GRIDS[index], per
        for name, ref in refs.items():
            setattr(self, name, ref)
        self.buffers = ((self.red0, self.red1), (self.black0, self.black1))
        self.now = [self.right, None]

    def pairs(self, body):
        rows(self.grid.rows // 2, body, self.per)

    def edge(self, a, b, t, r):
        own = self.own
        if (a, b) == (0, 1):
            return own[0, t + 1, r + 1]
        if (a, b) == (0, -1):
            return own[0, t + 1, r]
        if (a, b) == (1, 0):
            return own[1, t + 1, r + 1]
        if (a, b) == (-1, 0):
            return own[1, t, r + 1]
        if (a, b) == (1, 1):
            return own[2, t + 1, r + 1]
        if (a, b) == (-1, -1):
            return own[2, t, r]
        if (a, b) == (1, -1):
            return own[3, t + 1, r + 1]
        return own[3, t, r + 2]

    def scale_edges(self, t, r, edges, diagonal):
        inverse = 1.0 / diagonal
        self.dia[t, r] = diagonal
        self.inv[t, r] = inverse
        for index, edge in enumerate(edges):
            self.near[index, t, r] = edge * inverse

    def gathered(self, t, r, offsets, source, start=None):
        terms = [
            self.near[PLACE[a, b], t, r] * source(a, b)[t + 1 + a, r + 1 + b] for a, b in offsets
        ]
        if start is not None:
            terms.append(start)
        while len(terms) > 1:
            terms = [
                terms[i] + terms[i + 1] if i + 1 < len(terms) else terms[i]
                for i in range(0, len(terms), 2)
            ]
        return terms[0]

    def spare(self, colour):
        first, second = self.buffers[colour]
        return second if self.now[colour] is first else first

    def half_sweep(self, colour):
        grid, other, same = self.grid, self.now[1 - colour], self.now[colour]
        out = self.spare(colour)
        offsets = AROUND if same is not None else AROUND[:4]

        def body(u):
            for odd in (0, 1):
                for r in range(grid.phases):
                    if (odd + r) % 2 == colour:
                        t = 2 * u + odd
                        x = self.gathered(
                            t,
                            r,
                            offsets,
                            lambda a, b: other if (a + b) % 2 else same,
                            self.right[t + 1, r + 1],
                        )
                        grid.put(out, t, r, x)

        self.pairs(body)
        grid.wrap(out, colour)
        self.now[colour] = out

    def smooth_from_zero(self):
        self.now = [self.right, None]
        for colour in (1, 0, 1):
            self.half_sweep(colour)

    def smooth(self):
        for colour in (0, 1, 0, 1):
            self.half_sweep(colour)

    def find_residual(self):
        grid = self.grid

        def body(u):
            for odd in (0, 1):
                for r in range(grid.phases):
                    t = 2 * u + odd
                    colour = (odd + r) % 2
                    x = self.gathered(
                        t,
                        r,
                        AROUND,
                        lambda a, b: self.now[(colour + a + b) % 2],
                        self.right[t + 1, r + 1] - self.now[colour][t + 1, r + 1],
                    )
                    grid.put(self.residual, t, r, self.dia[t, r] * x)

        self.pairs(body)
        grid.wrap(self.residual)

    def find_weights(self):
        grid, dense, edge = self.grid, DENSE[self.index], self.edge

        def edges(i):
            for p in range(dense.phases):
                t, r = 2 * i + 1, 2 * p
                middle = 1.0 / (self.dia[t, r] - edge(0, -1, t, r) - edge(0, 1, t, r))
                up = edge(-1, 0, t, r) + edge(-1, -1, t, r) + edge(-1, 1, t, r)
                down = edge(1, 0, t, r) + edge(1, -1, t, r) + edge(1, 1, t, r)
                dense.put(self.weights.at[0], i, p, up * middle)
                dense.put(self.weights.at[1], i, p, down * middle)
                t, r = 2 * i, 2 * p + 1
                middle = 1.0 / (self.dia[t, r] - edge(-1, 0, t, r) - edge(1, 0, t, r))
                left = edge(0, -1, t, r) + edge(-1, -1, t, r) + edge(1, -1, t, r)
                right = edge(0, 1, t, r) + edge(-1, 1, t, r) + edge(1, 1, t, r)
                dense.put(self.weights.at[2], i, p, left * middle)
                dense.put(self.weights.at[3], i, p, right * middle)

        rows(dense.rows, edges, self.per)
        for index in range(4):
            dense.wrap(self.weights.at[index])
        w = self.weight

        def corners(i):
            for p in range(dense.phases):
                n = lambda a, b: self.near[PLACE[a, b], 2 * i + 1, 2 * p + 1]
                here = n(-1, -1) + n(0, -1) * w(0, i, p) + n(-1, 0) * w(2, i, p)
                down = n(1, -1) + n(0, -1) * w(1, i, p) + n(1, 0) * w(2, i + 1, p)
                right = n(-1, 1) + n(0, 1) * w(0, i, p + 1) + n(-1, 0) * w(3, i, p)
                both = n(1, 1) + n(0, 1) * w(1, i, p + 1) + n(1, 0) * w(3, i + 1, p)
                for index, x in enumerate((here, down, right, both)):
                    dense.put(self.weights.at[4 + index], i, p, x)

        rows(dense.rows, corners, self.per)
        for index in range(4, 8):
            dense.wrap(self.weights.at[index])

    def weight(self, index, i, p):
        return self.weights[index, i + 1, p + 1]

    def find_product(self):
        dense, w = DENSE[self.index], self.weight
        up, down, left, right, here, below, beside, both = range(8)

        def body(i):
            for p in range(dense.phases):
                t, r = 2 * i, 2 * p
                c = lambda a, b: self.edge(a, b, t, r)
                center = (
                    self.dia[t, r]
                    - c(-1, 0) * w(down, i - 1, p)
                    - c(1, 0) * w(up, i, p)
                    - c(0, -1) * w(right, i, p - 1)
                    - c(0, 1) * w(left, i, p)
                ) - (
                    c(-1, -1) * w(both, i - 1, p - 1)
                    + c(-1, 1) * w(below, i - 1, p)
                    + c(1, -1) * w(beside, i, p - 1)
                    + c(1, 1) * w(here, i, p)
                )
                east = -(
                    c(0, 1) * w(right, i, p)
                    + c(-1, 1) * w(both, i - 1, p)
                    + c(1, 1) * w(beside, i, p)
                )
                south = -(
                    c(1, 0) * w(down, i, p)
                    + c(1, 1) * w(below, i, p)
                    + c(1, -1) * w(both, i, p - 1)
                )
                south_east = -c(1, 1) * w(both, i, p)
                south_west = -c(1, -1) * w(below, i, p - 1)
                t, r = 2 * i + 1, 2 * p
                v = lambda a, b: self.edge(a, b, t, r)
                d = self.dia[t, r]
                v00 = (
                    d * w(up, i, p)
                    - v(-1, 0)
                    - v(-1, -1) * w(right, i, p - 1)
                    - v(-1, 1) * w(left, i, p)
                    - v(0, -1) * w(beside, i, p - 1)
                    - v(0, 1) * w(here, i, p)
                )
                v10 = (
                    d * w(down, i, p)
                    - v(1, 0)
                    - v(1, -1) * w(right, i + 1, p - 1)
                    - v(1, 1) * w(left, i + 1, p)
                    - v(0, -1) * w(both, i, p - 1)
                    - v(0, 1) * w(below, i, p)
                )
                v01 = -v(-1, 1) * w(right, i, p) - v(0, 1) * w(beside, i, p)
                v11 = -v(1, 1) * w(right, i + 1, p) - v(0, 1) * w(both, i, p)
                v1m = -v(1, -1) * w(left, i + 1, p - 1) - v(0, -1) * w(below, i, p - 1)
                t, r = 2 * i, 2 * p + 1
                h = lambda a, b: self.edge(a, b, t, r)
                d = self.dia[t, r]
                h00 = (
                    d * w(left, i, p)
                    - h(0, -1)
                    - h(-1, -1) * w(down, i - 1, p)
                    - h(1, -1) * w(up, i, p)
                    - h(-1, 0) * w(below, i - 1, p)
                    - h(1, 0) * w(here, i, p)
                )
                h01 = (
                    d * w(right, i, p)
                    - h(0, 1)
                    - h(-1, 1) * w(down, i - 1, p + 1)
                    - h(1, 1) * w(up, i, p + 1)
                    - h(-1, 0) * w(both, i - 1, p)
                    - h(1, 0) * w(beside, i, p)
                )
                h10 = -h(1, -1) * w(down, i, p) - h(1, 0) * w(below, i, p)
                h11 = -h(1, 1) * w(down, i, p + 1) - h(1, 0) * w(both, i, p)
                t, r = 2 * i + 1, 2 * p + 1
                k = lambda a, b: self.edge(a, b, t, r)
                d = self.dia[t, r]
                k00 = (
                    d * w(here, i, p)
                    - k(-1, -1)
                    - k(-1, 0) * w(left, i, p)
                    - k(0, -1) * w(up, i, p)
                )
                k10 = (
                    d * w(below, i, p)
                    - k(1, -1)
                    - k(1, 0) * w(left, i + 1, p)
                    - k(0, -1) * w(down, i, p)
                )
                k01 = (
                    d * w(beside, i, p)
                    - k(-1, 1)
                    - k(-1, 0) * w(right, i, p)
                    - k(0, 1) * w(up, i, p + 1)
                )
                k11 = (
                    d * w(both, i, p)
                    - k(1, 1)
                    - k(1, 0) * w(right, i + 1, p)
                    - k(0, 1) * w(down, i, p + 1)
                )
                wu, wd, wl, wr = (w(index, i, p) for index in (up, down, left, right))
                ch, cd, cr, cb = (w(index, i, p) for index in (here, below, beside, both))
                self.kept[0, i, p] = center + (wu * v00 + wl * h00) + ch * k00
                self.kept[1, i, p] = east + (wu * v01 + wl * h01) + ch * k01
                self.kept[2, i, p] = south + (wu * v10 + wl * h10) + ch * k10
                self.kept[3, i, p] = south_east + (wu * v11 + wl * h11) + ch * k11
                self.kept[4, i, p] = south_west + wu * v1m
                passed = (
                    wd * v10 + cd * k10,
                    wd * v11 + cd * k11,
                    wr * h01 + cr * k01,
                    wr * h11 + cr * k11,
                    wr * h10 + cr * k10,
                    cb * k11,
                )
                for index, x in enumerate(passed):
                    dense.put(self.passed.at[index], i, p, x)

        rows(dense.rows, body, self.per)
        for index in range(6):
            dense.wrap(self.passed.at[index])

    def give_product(self, coarse):
        dense, grid = DENSE[self.index], coarse.grid

        def body(i):
            for p in range(dense.phases):
                sent = lambda index, di, dp: self.passed[index, i + 1 + di, p + 1 + dp]
                center = (
                    self.kept[0, i, p] + sent(0, -1, 0) + sent(2, 0, -1) + sent(5, -1, -1)
                )
                entries = (
                    self.kept[1, i, p] + sent(1, -1, 0),
                    self.kept[2, i, p] + sent(3, 0, -1),
                    self.kept[3, i, p],
                    self.kept[4, i, p] + sent(4, 0, -1),
                )
                for phase, by in coarse.places(p, dense):
                    coarse.dia[i, phase] = center if by == 0 else turn_lanes(center, by)
                    for index, x in enumerate(entries):
                        x = -x if by == 0 else turn_lanes(-x, by)
                        grid.put(coarse.own.at[index], i, phase, x)

        rows(dense.rows, body, coarse.per)
        for index in range(4):
            grid.wrap(coarse.own.at[index])

        def scaled(u):
            for odd in (0, 1):
                for r in range(grid.phases):
                    t = 2 * u + odd
                    coarse.scale_edges(
                        t, r, [coarse.edge(a, b, t, r) for a, b in AROUND], coarse.dia[t, r]
                    )

        coarse.pairs(scaled)

    def places(self, p, dense):
        if dense.phases == self.grid.phases:
            return ((p, 0),)
        return ((0, 0), (1, -dense.stride))

    def restrict(self, coarse):
        dense, w, res = DENSE[self.index], self.weight, self.residual

        def body(i):
            for p in range(dense.phases):
                f = lambda a, b: res[2 * i + a + 1, 2 * p + b + 1]
                x = (
                    (f(0, 0) + w(0, i, p) * f(1, 0))
                    + (w(1, i - 1, p) * f(-1, 0) + w(2, i, p) * f(0, 1))
                ) + (
                    (w(3, i, p - 1) * f(0, -1) + w(4, i, p) * f(1, 1))
                    + (
                        (w(5, i - 1, p) * f(-1, 1) + w(6, i, p - 1) * f(1, -1))
                        + w(7, i - 1, p - 1) * f(-1, -1)
                    )
                )
                for phase, by in coarse.places(p, dense):
                    y = x if by == 0 else turn_lanes(x, by)
                    coarse.grid.put(coarse.right, i, phase, y * coarse.inv[i, phase])

        rows(dense.rows, body, coarse.per)
        coarse.grid.wrap(coarse.right)

    def prolong(self, coarse):
        grid, dense, w = self.grid, DENSE[self.index], self.weight
        if dense.phases == coarse.grid.phases:
            e = lambda i, p, parity: coarse.now[parity % 2][i + 1, p + 1]
        else:
            lane = lax.broadcasted_iota(jnp.int32, (SUB, LANES), 1)
            even = (lane & dense.stride) == 0
            for i in range(dense.rows):
                first = coarse.now[i % 2][i + 1, 1]
                second = turn_lanes(coarse.now[(i + 1) % 2][i + 1, 2], dense.stride)
                dense.put(self.lifted, i, 0, jnp.where(even, first, second))
            dense.wrap(self.lifted)
            e = lambda i, p, parity: self.lifted[i + 1, p + 1]
        outs = [self.spare(0), self.spare(1)]

        def body(v):
            for odd in (0, 1):
                i = 2 * v + odd
                for p in range(dense.phases):
                    here = e(i, p, odd + p)
                    below = e(i + 1, p, odd + p + 1)
                    beside = e(i, p + 1, odd + p + 1)
                    both = e(i + 1, p + 1, odd + p)
                    changes = (
                        (0, 0, here),
                        (1, 0, w(0, i, p) * here + w(1, i, p) * below),
                        (0, 1, w(2, i, p) * here + w(3, i, p) * beside),
                        (
                            1,
                            1,
                            (w(4, i, p) * here + w(5, i, p) * below)
                            + (w(6, i, p) * beside + w(7, i, p) * both),
                        ),
                    )
                    for a, b, change in changes:
                        colour = (a + b) % 2
                        t, r = 2 * i + a, 2 * p + b
                        grid.put(outs[colour], t, r, self.now[colour][t + 1, r + 1] + change)

        rows(dense.rows // 2, body, self.per)
        for colour in (0, 1):
            grid.wrap(outs[colour], colour)
            self.now[colour] = outs[colour]


def reorder(x, order):
    high = x.astype(BF16)
    rest = x - high.astype(F32)
    middle = rest.astype(BF16)
    low = (rest - middle.astype(F32)).astype(BF16)
    moved = [jnp.dot(part, order, preferred_element_type=F32) for part in (low, middle, high)]
    return (moved[0] + moved[1]) + moved[2]


def phase_matrix(swap, inverse):
    natural = lax.broadcasted_iota(jnp.int32, (COLS, COLS), 1 if inverse else 0)
    phased = lax.broadcasted_iota(jnp.int32, (COLS, COLS), 0 if inverse else 1)
    phase = natural & 3
    if swap:
        phase = phase ^ 1
    target = phase * 64 + (natural >> 2)
    return jnp.where(phased == target, 1.0, 0.0).astype(BF16)


def spread(field, own, halo, own_order, halo_order, own_out, halo_out):
    for out, x in ((own_out, reorder(own, own_order)), (halo_out, reorder(halo, halo_order))):
        for pair in (0, 1):
            out[field, pair] = x[:, pair * LANES : (pair + 1) * LANES]


def phases_of(field, t, own_out, halo_out, low):
    found = []
    for pair in (0, 1):
        window = (pl.ds(t, SUB, stride=ROWS), slice(None))
        own, halo = own_out.at[field, pair][window], halo_out.at[field, pair][window]
        found.append(jnp.where(low, own, halo))
        found.append(turn_lanes(jnp.where(low, halo, own), 64))
    return found


def fill_edges(level, col_place, own_out, halo_out):
    grid = level.grid
    lane = lax.broadcasted_iota(jnp.int32, (SUB, LANES), 1)
    strip = lax.broadcasted_iota(jnp.int32, (SUB, LANES), 0)
    low = lane < 64
    lane_start = col_place * 64 + jnp.where(lane < 96, lane, lane - LANES)
    count = lax.axis_size("col") * 64
    east_ok = jnp.where((lane_start == count - 1) | (lane_start == -1), 0.0, 1.0)
    west_ok = jnp.where((lane_start == 0) | (lane_start == count), 0.0, 1.0)
    last_strip = strip == SUB - 1

    def body(t):
        south_ok = jnp.where(last_strip & (t == ROWS - 1), 0.0, 1.0)
        for index in range(4):
            phases = phases_of(index, t, own_out, halo_out, low)
            for r, x in enumerate(phases):
                if index != 0:
                    x = x * south_ok
                if index in (0, 2) and r == 3:
                    x = x * east_ok
                if index == 3 and r == 0:
                    x = x * west_ok
                grid.put(level.own.at[index], t, r, x)

    rows(ROWS, body, 2)
    for index in range(4):
        grid.wrap(level.own.at[index])

    def scaled(t):
        shift = phases_of(4, t, own_out, halo_out, low)
        for r in range(4):
            edges = [level.edge(a, b, t, r) for a, b in AROUND]
            pairs = [edges[i] + edges[i + 1] for i in range(0, 8, 2)]
            total = (pairs[0] + pairs[1]) + (pairs[2] + pairs[3])
            level.scale_edges(t, r, edges, shift[r] + total)

    rows(ROWS, scaled, 2)


def fill_right(level, own_out, halo_out):
    grid = level.grid
    vector = level.residual
    lane = lax.broadcasted_iota(jnp.int32, (SUB, LANES), 1)
    low = lane < 64

    def body(t):
        for r, x in enumerate(phases_of(5, t, own_out, halo_out, low)):
            grid.put(vector, t, r, x)

    rows(ROWS, body, 4)
    grid.wrap(vector)

    def image(u):
        for odd in (0, 1):
            for r in range(4):
                t = 2 * u + odd
                x = vector[t + 1, r + 1] - level.gathered(t, r, AROUND, lambda a, b: vector)
                grid.put(level.right, t, r, x)

    level.pairs(image)
    grid.wrap(level.right)


def setup(levels):
    for index in range(3):
        levels[index].find_weights()
        levels[index].find_product()
        levels[index].give_product(levels[index + 1])


def cycle(levels, index):
    level = levels[index]
    level.smooth_from_zero()
    if index == 3:
        return
    level.find_residual()
    level.restrict(levels[index + 1])
    cycle(levels, index + 1)
    level.prolong(levels[index + 1])
    level.smooth()


def total(x):
    return jnp.sum(jnp.sum(x, axis=0, keepdims=True), axis=1, keepdims=True)


def tell(solved, vector, previous):
    target = solved - previous
    length = total(vector * vector)
    projected = total(vector * target)
    near_alpha = jnp.where(length > 0.0, projected / jnp.where(length > 0.0, length, 1.0), 0.0)
    rest = target - near_alpha * vector
    squares = total(rest * rest)
    cross = total(vector * rest)
    inner = total(vector * solved)
    lane = lax.broadcasted_iota(jnp.int32, (1, LANES), 1)
    row = jnp.where(lane < 3, near_alpha, 0.0)
    for place, x in ((3, inner), (64, squares), (65, cross), (66, length)):
        row = jnp.where(lane == place, x, row)
    return row


def conclude(told, cells):
    lane = lax.broadcasted_iota(jnp.int32, told.shape, 1)
    alpha = total(jnp.where(lane == 3, told, 0.0)) / cells
    delta = alpha - told
    sums = pltpu.roll(told, 64, 1)
    weight = jnp.where(lane == 0, 1.0, jnp.where(lane == 1, -2.0 * delta, delta * delta))
    squares = total(jnp.where(lane < 3, weight * sums, 0.0)) / cells
    scale = jnp.sqrt(jnp.maximum(squares, 0.0) + EPSILON)
    return alpha, scale


def compute(col_place, own, halo, vector, vector_halo, previous, solved, told, levels_refs, own_out, halo_out, phased):
    levels = [Level(index, refs, 2 if index == 0 else 99) for index, refs in enumerate(levels_refs)]
    own_order = phase_matrix(False, False)
    halo_order = phase_matrix(True, False)
    whole = (SUB * ROWS, COLS)
    half = (SUB * ROWS, LANES)
    for field in range(5):
        sides = [halo[:, side, field].reshape(half) for side in (0, 1)]
        spread(
            field,
            own[:, field].reshape(whole),
            jnp.concatenate(sides, axis=1),
            own_order,
            halo_order,
            own_out,
            halo_out,
        )
    sides = [vector_halo[side].reshape(half) for side in (0, 1)]
    spread(
        5,
        vector[...].reshape(whole),
        jnp.concatenate(sides, axis=1),
        own_order,
        halo_order,
        own_out,
        halo_out,
    )
    fill_edges(levels[0], col_place, own_out, halo_out)
    fill_right(levels[0], own_out, halo_out)
    setup(levels)
    cycle(levels, 0)
    lane = lax.broadcasted_iota(jnp.int32, (SUB, LANES), 1)
    low = lane < 64

    def gather(u):
        for odd in (0, 1):
            t = 2 * u + odd
            x = [levels[0].now[(odd + r) % 2][t + 1, r + 1] for r in range(4)]
            for pair in (0, 1):
                y = jnp.where(low, x[2 * pair], turn_lanes(x[2 * pair + 1], 64))
                phased.at[pair][pl.ds(t, SUB, stride=ROWS), :] = y

    rows(ROWS // 2, gather, 2)
    result = reorder(jnp.concatenate([phased[0], phased[1]], axis=1), phase_matrix(False, True))
    solved[...] = result.reshape(SUB, ROWS, COLS)
    told[...] = tell(result, vector[...].reshape(whole), previous[...].reshape(whole))


def copy_out(source, target, send, receive, grp, col):
    return pltpu.make_async_remote_copy(
        src_ref=source,
        dst_ref=target,
        send_sem=send,
        recv_sem=receive,
        device_id=(grp, col),
        device_id_type=MESH,
    )


def greet(partners):
    barrier = pltpu.get_barrier_semaphore()
    for grp, col in partners:
        pl.semaphore_signal(barrier, inc=1, device_id=(grp, col), device_id_type=MESH)
    pl.semaphore_wait(barrier, len(partners))


def gather_semaphores():
    dma = pltpu.SemaphoreType.DMA
    return [dma((2, 3)), dma((2, 7)), dma((2, 7)), dma((2, 8)), dma((2, 2)), dma((2, 4)), dma((2, 8))]


def gather_sources(g, conductance, shift, vector_in, previous_in, own, vector, previous):
    own[g, 0:4] = conductance[...]
    own[g, 4] = shift[...]
    vector[g] = vector_in[g]
    previous[g] = previous_in[g]


def gather(g, c, vector_in, previous_in, own, halo, vector, vector_halo, previous, semaphores):
    along, of_vector, of_previous, beside, vector_beside, across, halo_across = semaphores
    n_grp, n_col = 8, lax.axis_size("col")
    y, core = g // 2, g % 2
    twin = y * 2 + 1 - core
    mates = [(g + step) % n_grp for step in range(1, n_grp)]
    east, west = (c + 1) % n_col, (c + n_col - 1) % n_col
    started = []

    def start(copy):
        copy.start()
        started.append(copy)
        return copy

    def place(back):
        return ((y + 4 - back) % 4) * 2 + core

    def send_sides(back):
        rows_ = place(back)
        return [
            start(
                copy_out(
                    own.at[rows_, :, :, pl.ds(LANES, LANES)],
                    halo.at[rows_, 1],
                    beside.at[0, back],
                    beside.at[1, back],
                    g,
                    east,
                )
            ),
            start(
                copy_out(
                    own.at[rows_, :, :, pl.ds(0, LANES)],
                    halo.at[rows_, 0],
                    beside.at[0, 4 + back],
                    beside.at[1, 4 + back],
                    g,
                    west,
                )
            ),
        ]

    def send_across(back):
        rows_ = place(back)
        return start(
            copy_out(own.at[rows_], own.at[rows_], across.at[0, back], across.at[1, back], twin, c)
        )

    arriving = []
    for step in range(1, 4):
        to = ((y + step) % 4) * 2 + core
        arriving.append(
            start(
                copy_out(own.at[g], own.at[g], along.at[0, step - 1], along.at[1, step - 1], to, c)
            )
        )
    from_sides = [send_sides(0)]
    from_twin = [send_across(0)]
    vectors = [
        start(
            copy_out(
                vector_in.at[to], vector.at[g], of_vector.at[0, i], of_vector.at[1, i], to, c
            )
        )
        for i, to in enumerate(mates)
    ]
    for back in (1, 3, 2):
        arriving[back - 1].wait_recv()
        from_sides.append(send_sides(back))
        from_twin.append(send_across(back))
    for copy in vectors:
        copy.wait_recv()
    side_vectors = []
    for side, to in ((1, east), (0, west)):
        side_vectors.append(
            start(
                copy_out(
                    vector.at[:, :, pl.ds(side * LANES, LANES)],
                    vector_halo.at[side],
                    vector_beside.at[0, side],
                    vector_beside.at[1, side],
                    g,
                    to,
                )
            )
        )
    previouses = [
        start(
            copy_out(
                previous_in.at[to],
                previous.at[g],
                of_previous.at[0, i],
                of_previous.at[1, i],
                to,
                c,
            )
        )
        for i, to in enumerate(mates)
    ]
    halves = []
    for order, back in enumerate((0, 1, 3, 2)):
        for side in (1, 0):
            from_sides[order][1 - side].wait_recv()
            rows_ = place(back)
            at = side * 4 + back
            halves.append(
                start(
                    copy_out(
                        halo.at[rows_, side],
                        halo.at[rows_, side],
                        halo_across.at[0, at],
                        halo_across.at[1, at],
                        twin,
                        c,
                    )
                )
            )
    for copy in from_twin + halves + side_vectors:
        copy.wait_recv()

    def finish():
        for copy in previouses:
            copy.wait_recv()
        for copy in started:
            copy.wait_send()

    return finish


def finish_semaphores():
    dma = pltpu.SemaphoreType.DMA
    return [dma((2,)), dma((2, 7)), dma((2,))]


def finish_scratch(n_col):
    return [
        pltpu.VMEM((8, ROWS, COLS), F32),
        pltpu.VMEM((n_col, 1, LANES), F32),
        pltpu.VMEM((8, 2, LANES), F32),
    ]


def conclude_all(g, c, vector_in, previous_in, solved, told, got, heard, verdicts, out, coefficients, semaphores):
    spread_sem, back_sem, verdict_sem = semaphores
    n_grp, n_col = 8, lax.axis_size("col")
    mates = [(g + step) % n_grp for step in range(1, n_grp)]
    heard[c] = told[...]
    telling = []
    for step in range(1, n_col):
        to = (c + step) % n_col
        telling.append(copy_out(told, heard.at[c], spread_sem.at[0], spread_sem.at[1], g, to))
        telling[-1].start()
    back = []
    for i, to in enumerate(mates):
        back.append(copy_out(solved.at[to], got.at[g], back_sem.at[0, i], back_sem.at[1, i], to, c))
        back[-1].start()
    got[g] = solved[g]
    several = heard.at[pl.ds(0, n_col - 1)]
    pltpu.make_async_copy(several, several, spread_sem.at[1]).wait()
    alpha, scale = conclude(heard[...].reshape(n_col, LANES), float(n_grp * ROWS * n_col * COLS))
    which = lax.broadcasted_iota(jnp.int32, (2, LANES), 0)
    verdicts[g] = jnp.where(which == 0, alpha, scale)
    deciding = []
    for to in mates:
        deciding.append(
            copy_out(verdicts.at[g], verdicts.at[g], verdict_sem.at[0], verdict_sem.at[1], to, c)
        )
        deciding[-1].start()
    for copy in back:
        copy.wait_recv()
    others = verdicts.at[pl.ds(0, n_grp - 1)]
    pltpu.make_async_copy(others, others, verdict_sem.at[1]).wait()
    lane = lax.broadcasted_iota(jnp.int32, (2, LANES), 1)
    summary = jnp.zeros((2, LANES), F32)
    for probe in range(n_grp):
        pair = verdicts[probe]
        summary = jnp.where(lane == probe, pair, summary)
        rest = got[probe] - pair[0:1, 0:1] * vector_in[probe] - previous_in[probe]
        out[probe] = rest * (1.0 / pair[1:2, 0:1])
    coefficients[...] = summary[:, 0:n_grp]
    pltpu.make_async_copy(several, several, spread_sem.at[0]).wait()
    pltpu.make_async_copy(others, others, verdict_sem.at[0]).wait()
    for copy in back:
        copy.wait_send()


def flat_levels():
    return jax.tree.flatten(level_scratch())


def spread_scratch():
    return [pltpu.VMEM((6, 2, 8 * ROWS, LANES), F32)] * 2 + [pltpu.VMEM((2, 8 * ROWS, LANES), F32)]


VMEM = pl.BlockSpec(memory_space=pltpu.VMEM)
LIMIT = 48 * 1024 * 1024


def shape(*dims):
    return jax.ShapeDtypeStruct(dims, F32)


def gather_kernel(conductance, shift, vector_in, previous_in, own, halo, vector, vector_halo, previous, *semaphores):
    g, c = lax.axis_index("grp"), lax.axis_index("col")
    n_col = lax.axis_size("col")
    gather_sources(g, conductance, shift, vector_in, previous_in, own, vector, previous)
    greet(
        [((g + step) % 8, c) for step in range(1, 8)]
        + [(g, (c + 1) % n_col), (g, (c + n_col - 1) % n_col)]
    )
    gather(g, c, vector_in, previous_in, own, halo, vector, vector_halo, previous, semaphores)()


def compute_kernel(own, halo, vector, vector_halo, previous, solved, told, *scratch):
    leaves, tree = flat_levels()
    count = len(leaves)
    levels_refs = jax.tree.unflatten(tree, scratch[:count])
    own_out, halo_out, phased = scratch[count:]
    c = lax.axis_index("col")
    compute(c, own, halo, vector, vector_halo, previous, solved, told, levels_refs, own_out, halo_out, phased)


def finish_kernel(vector_in, previous_in, solved, told, out, coefficients, got, heard, verdicts, *semaphores):
    g, c = lax.axis_index("grp"), lax.axis_index("col")
    n_col = lax.axis_size("col")
    greet(
        [((g + step) % 8, c) for step in range(1, 8)]
        + [(g, (c + step) % n_col) for step in range(1, n_col)]
    )
    conclude_all(g, c, vector_in, previous_in, solved, told, got, heard, verdicts, out, coefficients, semaphores)


def local(conductance, shift, vector_in, previous_in):
    n_col = lax.axis_size("col")
    gathered = pl.pallas_call(
        gather_kernel,
        out_shape=(
            shape(8, 5, ROWS, COLS),
            shape(8, 2, 5, ROWS, LANES),
            shape(8, ROWS, COLS),
            shape(2, 8, ROWS, LANES),
            shape(8, ROWS, COLS),
        ),
        in_specs=[VMEM] * 4,
        out_specs=(VMEM,) * 5,
        scratch_shapes=gather_semaphores(),
        compiler_params=pltpu.CompilerParams(collective_id=0, has_side_effects=True, vmem_limit_bytes=LIMIT),
    )(conductance, shift, vector_in, previous_in)
    leaves, _ = flat_levels()
    solved, told = pl.pallas_call(
        compute_kernel,
        out_shape=(shape(8, ROWS, COLS), shape(1, LANES)),
        in_specs=[VMEM] * 5,
        out_specs=(VMEM,) * 2,
        scratch_shapes=leaves + spread_scratch(),
        compiler_params=pltpu.CompilerParams(vmem_limit_bytes=LIMIT),
    )(*gathered)
    return pl.pallas_call(
        finish_kernel,
        out_shape=(shape(8, ROWS, COLS), shape(2, 8)),
        in_specs=[VMEM] * 4,
        out_specs=(VMEM,) * 2,
        scratch_shapes=finish_scratch(n_col) + finish_semaphores(),
        compiler_params=pltpu.CompilerParams(collective_id=1, has_side_effects=True, vmem_limit_bytes=LIMIT),
    )(vector_in, previous_in, solved, told)


def solution(mesh):
    in_specs = (
        P(None, "grp", "col"),
        P("grp", "col"),
        P(None, "grp", "col"),
        P(None, "grp", "col"),
    )
    out_specs = (P(None, "grp", "col"), P())
    return jax.shard_map(local, mesh=mesh, in_specs=in_specs, out_specs=out_specs, check_vma=False)
```

```python
import jax
import jax.numpy as jnp
from jax import lax
from jax.experimental import pallas as pl
from jax.experimental.pallas import tpu as pltpu
from jax.sharding import PartitionSpec as P

F32 = jnp.float32
BF16 = jnp.bfloat16
EPSILON = 1e-06
LANES = 128
SUB = 8
WHOLE = 99
ROWS = 16
COLS = 256
MESH = pl.DeviceIdType.MESH

LEVEL_ROWS = (16, 8, 4, 2)
LEVEL_PHASES = (4, 2, 2, 2)
LEVEL_STRIDE = (1, 1, 2, 4)
AROUND = ((-1, 0), (1, 0), (0, -1), (0, 1), (-1, -1), (-1, 1), (1, -1), (1, 1))
PLACE = {offset: index for index, offset in enumerate(AROUND)}


def turn_lanes(x, by):
    return pltpu.roll(x, by % LANES, 1)


def turn_strips(x, by):
    return pltpu.roll(x, by % SUB, 0)


def rows(count, body, per):
    if per >= count:
        for index in range(count):
            body(index)
    else:

        def step(index, carry):
            for inner in range(per):
                body(index * per + inner)
            return carry

        lax.fori_loop(0, count // per, step, 0)


class Grid:
    def __init__(self, rows_, phases, stride):
        self.rows, self.phases, self.stride = rows_, phases, stride

    @property
    def ghosted(self):
        return (self.rows + 2, self.phases + 2, SUB, LANES)

    @property
    def bare(self):
        return (self.rows, self.phases, SUB, LANES)

    def put(self, ref, t, r, x):
        places = [(r + 1, x)]
        if r == 0:
            places.append((self.phases + 1, turn_lanes(x, -self.stride)))
        if r == self.phases - 1:
            places.append((0, turn_lanes(x, self.stride)))
        for place, y in places:
            ref[t + 1, place] = y
            if isinstance(t, int) and t == 0:
                ref[self.rows + 1, place] = turn_strips(y, -1)
            if isinstance(t, int) and t == self.rows - 1:
                ref[0, place] = turn_strips(y, 1)

    def wrap(self, ref, per, colour=None):
        if per >= self.rows:
            return
        for r in range(-1, self.phases + 1):
            if colour is None or (self.rows - 1 + r) % 2 == colour:
                ref[0, r + 1] = turn_strips(ref[self.rows, r + 1], 1)
            if colour is None or r % 2 == colour:
                ref[self.rows + 1, r + 1] = turn_strips(ref[1, r + 1], -1)


GRIDS = tuple(Grid(*sizes) for sizes in zip(LEVEL_ROWS, LEVEL_PHASES, LEVEL_STRIDE))
DENSE = tuple(Grid(g.rows // 2, g.phases // 2, g.stride) for g in GRIDS[:3])


def level_scratch():
    shapes = []
    for index, grid in enumerate(GRIDS):
        entry = {
            "own": (4,) + grid.ghosted,
            "dia": grid.bare,
            "inv": grid.bare,
            "near": (8,) + grid.bare,
            "right": grid.ghosted,
            "red0": grid.ghosted,
            "red1": grid.ghosted,
            "black0": grid.ghosted,
            "black1": grid.ghosted,
        }
        if index < 3:
            dense = DENSE[index]
            entry["weights"] = (8,) + dense.ghosted
            entry["passed"] = (6,) + dense.ghosted
            entry["kept"] = (5,) + dense.bare
            entry["residual"] = grid.ghosted
            entry["lifted"] = dense.ghosted
        shapes.append({name: pltpu.VMEM(shape, F32) for name, shape in entry.items()})
    return shapes


class Level:
    def __init__(self, index, refs, per):
        self.index, self.grid, self.per = index, GRIDS[index], per
        for name, ref in refs.items():
            setattr(self, name, ref)
        self.buffers = ((self.red0, self.red1), (self.black0, self.black1))
        self.now = [self.right, None]

    def pairs(self, body):
        rows(self.grid.rows // 2, body, self.per)

    def edge(self, a, b, t, r):
        own = self.own
        if (a, b) == (0, 1):
            return own[0, t + 1, r + 1]
        if (a, b) == (0, -1):
            return own[0, t + 1, r]
        if (a, b) == (1, 0):
            return own[1, t + 1, r + 1]
        if (a, b) == (-1, 0):
            return own[1, t, r + 1]
        if (a, b) == (1, 1):
            return own[2, t + 1, r + 1]
        if (a, b) == (-1, -1):
            return own[2, t, r]
        if (a, b) == (1, -1):
            return own[3, t + 1, r + 1]
        return own[3, t, r + 2]

    def scale_edges(self, t, r, edges, diagonal):
        inverse = 1.0 / diagonal
        self.dia[t, r] = diagonal
        self.inv[t, r] = inverse
        for index, edge in enumerate(edges):
            self.near[index, t, r] = edge * inverse

    def gathered(self, t, r, offsets, source, start=None):
        terms = [
            self.near[PLACE[a, b], t, r] * source(a, b)[t + 1 + a, r + 1 + b] for a, b in offsets
        ]
        if start is not None:
            terms.append(start)
        while len(terms) > 1:
            terms = [
                terms[i] + terms[i + 1] if i + 1 < len(terms) else terms[i]
                for i in range(0, len(terms), 2)
            ]
        return terms[0]

    def spare(self, colour):
        first, second = self.buffers[colour]
        return second if self.now[colour] is first else first

    def half_sweep(self, colour):
        grid, other, same = self.grid, self.now[1 - colour], self.now[colour]
        out = self.spare(colour)
        offsets = AROUND if same is not None else AROUND[:4]

        def body(u):
            for odd in (0, 1):
                for r in range(grid.phases):
                    if (odd + r) % 2 == colour:
                        t = 2 * u + odd
                        x = self.gathered(
                            t,
                            r,
                            offsets,
                            lambda a, b: other if (a + b) % 2 else same,
                            self.right[t + 1, r + 1],
                        )
                        grid.put(out, t, r, x)

        self.pairs(body)
        grid.wrap(out, self.per, colour)
        self.now[colour] = out

    def smooth_from_zero(self):
        self.now = [self.right, None]
        for colour in (1, 0, 1):
            self.half_sweep(colour)

    def smooth(self):
        for colour in (0, 1, 0, 1):
            self.half_sweep(colour)

    def find_residual(self):
        grid = self.grid

        def body(u):
            for odd in (0, 1):
                for r in range(grid.phases):
                    t = 2 * u + odd
                    colour = (odd + r) % 2
                    x = self.gathered(
                        t,
                        r,
                        AROUND,
                        lambda a, b: self.now[(colour + a + b) % 2],
                        self.right[t + 1, r + 1] - self.now[colour][t + 1, r + 1],
                    )
                    grid.put(self.residual, t, r, self.dia[t, r] * x)

        self.pairs(body)
        grid.wrap(self.residual, self.per)

    def find_weights(self):
        grid, dense, edge = self.grid, DENSE[self.index], self.edge

        def edges(i):
            for p in range(dense.phases):
                t, r = 2 * i + 1, 2 * p
                middle = 1.0 / (self.dia[t, r] - edge(0, -1, t, r) - edge(0, 1, t, r))
                up = edge(-1, 0, t, r) + edge(-1, -1, t, r) + edge(-1, 1, t, r)
                down = edge(1, 0, t, r) + edge(1, -1, t, r) + edge(1, 1, t, r)
                dense.put(self.weights.at[0], i, p, up * middle)
                dense.put(self.weights.at[1], i, p, down * middle)
                t, r = 2 * i, 2 * p + 1
                middle = 1.0 / (self.dia[t, r] - edge(-1, 0, t, r) - edge(1, 0, t, r))
                left = edge(0, -1, t, r) + edge(-1, -1, t, r) + edge(1, -1, t, r)
                right = edge(0, 1, t, r) + edge(-1, 1, t, r) + edge(1, 1, t, r)
                dense.put(self.weights.at[2], i, p, left * middle)
                dense.put(self.weights.at[3], i, p, right * middle)

        rows(dense.rows, edges, self.per)
        for index in range(4):
            dense.wrap(self.weights.at[index], self.per)
        w = self.weight

        def corners(i):
            for p in range(dense.phases):
                n = lambda a, b: self.near[PLACE[a, b], 2 * i + 1, 2 * p + 1]
                here = n(-1, -1) + n(0, -1) * w(0, i, p) + n(-1, 0) * w(2, i, p)
                down = n(1, -1) + n(0, -1) * w(1, i, p) + n(1, 0) * w(2, i + 1, p)
                right = n(-1, 1) + n(0, 1) * w(0, i, p + 1) + n(-1, 0) * w(3, i, p)
                both = n(1, 1) + n(0, 1) * w(1, i, p + 1) + n(1, 0) * w(3, i + 1, p)
                for index, x in enumerate((here, down, right, both)):
                    dense.put(self.weights.at[4 + index], i, p, x)

        rows(dense.rows, corners, self.per)
        for index in range(4, 8):
            dense.wrap(self.weights.at[index], self.per)

    def weight(self, index, i, p):
        return self.weights[index, i + 1, p + 1]

    def find_product(self):
        dense, w = DENSE[self.index], self.weight
        up, down, left, right, here, below, beside, both = range(8)

        def body(i):
            for p in range(dense.phases):
                t, r = 2 * i, 2 * p
                c = lambda a, b: self.edge(a, b, t, r)
                center = (
                    self.dia[t, r]
                    - c(-1, 0) * w(down, i - 1, p)
                    - c(1, 0) * w(up, i, p)
                    - c(0, -1) * w(right, i, p - 1)
                    - c(0, 1) * w(left, i, p)
                ) - (
                    c(-1, -1) * w(both, i - 1, p - 1)
                    + c(-1, 1) * w(below, i - 1, p)
                    + c(1, -1) * w(beside, i, p - 1)
                    + c(1, 1) * w(here, i, p)
                )
                east = -(
                    c(0, 1) * w(right, i, p)
                    + c(-1, 1) * w(both, i - 1, p)
                    + c(1, 1) * w(beside, i, p)
                )
                south = -(
                    c(1, 0) * w(down, i, p)
                    + c(1, 1) * w(below, i, p)
                    + c(1, -1) * w(both, i, p - 1)
                )
                south_east = -c(1, 1) * w(both, i, p)
                south_west = -c(1, -1) * w(below, i, p - 1)
                t, r = 2 * i + 1, 2 * p
                v = lambda a, b: self.edge(a, b, t, r)
                d = self.dia[t, r]
                v00 = (
                    d * w(up, i, p)
                    - v(-1, 0)
                    - v(-1, -1) * w(right, i, p - 1)
                    - v(-1, 1) * w(left, i, p)
                    - v(0, -1) * w(beside, i, p - 1)
                    - v(0, 1) * w(here, i, p)
                )
                v10 = (
                    d * w(down, i, p)
                    - v(1, 0)
                    - v(1, -1) * w(right, i + 1, p - 1)
                    - v(1, 1) * w(left, i + 1, p)
                    - v(0, -1) * w(both, i, p - 1)
                    - v(0, 1) * w(below, i, p)
                )
                v01 = -v(-1, 1) * w(right, i, p) - v(0, 1) * w(beside, i, p)
                v11 = -v(1, 1) * w(right, i + 1, p) - v(0, 1) * w(both, i, p)
                v1m = -v(1, -1) * w(left, i + 1, p - 1) - v(0, -1) * w(below, i, p - 1)
                t, r = 2 * i, 2 * p + 1
                h = lambda a, b: self.edge(a, b, t, r)
                d = self.dia[t, r]
                h00 = (
                    d * w(left, i, p)
                    - h(0, -1)
                    - h(-1, -1) * w(down, i - 1, p)
                    - h(1, -1) * w(up, i, p)
                    - h(-1, 0) * w(below, i - 1, p)
                    - h(1, 0) * w(here, i, p)
                )
                h01 = (
                    d * w(right, i, p)
                    - h(0, 1)
                    - h(-1, 1) * w(down, i - 1, p + 1)
                    - h(1, 1) * w(up, i, p + 1)
                    - h(-1, 0) * w(both, i - 1, p)
                    - h(1, 0) * w(beside, i, p)
                )
                h10 = -h(1, -1) * w(down, i, p) - h(1, 0) * w(below, i, p)
                h11 = -h(1, 1) * w(down, i, p + 1) - h(1, 0) * w(both, i, p)
                t, r = 2 * i + 1, 2 * p + 1
                k = lambda a, b: self.edge(a, b, t, r)
                d = self.dia[t, r]
                k00 = (
                    d * w(here, i, p)
                    - k(-1, -1)
                    - k(-1, 0) * w(left, i, p)
                    - k(0, -1) * w(up, i, p)
                )
                k10 = (
                    d * w(below, i, p)
                    - k(1, -1)
                    - k(1, 0) * w(left, i + 1, p)
                    - k(0, -1) * w(down, i, p)
                )
                k01 = (
                    d * w(beside, i, p)
                    - k(-1, 1)
                    - k(-1, 0) * w(right, i, p)
                    - k(0, 1) * w(up, i, p + 1)
                )
                k11 = (
                    d * w(both, i, p)
                    - k(1, 1)
                    - k(1, 0) * w(right, i + 1, p)
                    - k(0, 1) * w(down, i, p + 1)
                )
                wu, wd, wl, wr = (w(index, i, p) for index in (up, down, left, right))
                ch, cd, cr, cb = (w(index, i, p) for index in (here, below, beside, both))
                self.kept[0, i, p] = center + (wu * v00 + wl * h00) + ch * k00
                self.kept[1, i, p] = east + (wu * v01 + wl * h01) + ch * k01
                self.kept[2, i, p] = south + (wu * v10 + wl * h10) + ch * k10
                self.kept[3, i, p] = south_east + (wu * v11 + wl * h11) + ch * k11
                self.kept[4, i, p] = south_west + wu * v1m
                passed = (
                    wd * v10 + cd * k10,
                    wd * v11 + cd * k11,
                    wr * h01 + cr * k01,
                    wr * h11 + cr * k11,
                    wr * h10 + cr * k10,
                    cb * k11,
                )
                for index, x in enumerate(passed):
                    dense.put(self.passed.at[index], i, p, x)

        rows(dense.rows, body, self.per)
        for index in range(6):
            dense.wrap(self.passed.at[index], self.per)

    def give_product(self, coarse):
        dense, grid = DENSE[self.index], coarse.grid

        def body(i):
            for p in range(dense.phases):
                sent = lambda index, di, dp: self.passed[index, i + 1 + di, p + 1 + dp]
                center = (
                    self.kept[0, i, p] + sent(0, -1, 0) + sent(2, 0, -1) + sent(5, -1, -1)
                )
                entries = (
                    self.kept[1, i, p] + sent(1, -1, 0),
                    self.kept[2, i, p] + sent(3, 0, -1),
                    self.kept[3, i, p],
                    self.kept[4, i, p] + sent(4, 0, -1),
                )
                for phase, by in coarse.places(p, dense):
                    coarse.dia[i, phase] = center if by == 0 else turn_lanes(center, by)
                    for index, x in enumerate(entries):
                        x = -x if by == 0 else turn_lanes(-x, by)
                        grid.put(coarse.own.at[index], i, phase, x)

        rows(dense.rows, body, coarse.per)
        for index in range(4):
            grid.wrap(coarse.own.at[index], coarse.per)

        def scaled(u):
            for odd in (0, 1):
                for r in range(grid.phases):
                    t = 2 * u + odd
                    coarse.scale_edges(
                        t, r, [coarse.edge(a, b, t, r) for a, b in AROUND], coarse.dia[t, r]
                    )

        coarse.pairs(scaled)

    def places(self, p, dense):
        if dense.phases == self.grid.phases:
            return ((p, 0),)
        return ((0, 0), (1, -dense.stride))

    def restrict(self, coarse):
        dense, w, res = DENSE[self.index], self.weight, self.residual

        def body(i):
            for p in range(dense.phases):
                f = lambda a, b: res[2 * i + a + 1, 2 * p + b + 1]
                x = (
                    (f(0, 0) + w(0, i, p) * f(1, 0))
                    + (w(1, i - 1, p) * f(-1, 0) + w(2, i, p) * f(0, 1))
                ) + (
                    (w(3, i, p - 1) * f(0, -1) + w(4, i, p) * f(1, 1))
                    + (
                        (w(5, i - 1, p) * f(-1, 1) + w(6, i, p - 1) * f(1, -1))
                        + w(7, i - 1, p - 1) * f(-1, -1)
                    )
                )
                for phase, by in coarse.places(p, dense):
                    y = x if by == 0 else turn_lanes(x, by)
                    coarse.grid.put(coarse.right, i, phase, y * coarse.inv[i, phase])

        rows(dense.rows, body, coarse.per)
        coarse.grid.wrap(coarse.right, coarse.per)

    def prolong(self, coarse):
        grid, dense, w = self.grid, DENSE[self.index], self.weight
        if dense.phases == coarse.grid.phases:
            e = lambda i, p, parity: coarse.now[parity % 2][i + 1, p + 1]
        else:
            lane = lax.broadcasted_iota(jnp.int32, (SUB, LANES), 1)
            even = (lane & dense.stride) == 0
            for i in range(dense.rows):
                first = coarse.now[i % 2][i + 1, 1]
                second = turn_lanes(coarse.now[(i + 1) % 2][i + 1, 2], dense.stride)
                dense.put(self.lifted, i, 0, jnp.where(even, first, second))
            e = lambda i, p, parity: self.lifted[i + 1, p + 1]
        outs = [self.spare(0), self.spare(1)]

        def body(v):
            for odd in (0, 1):
                i = 2 * v + odd
                for p in range(dense.phases):
                    here = e(i, p, odd + p)
                    below = e(i + 1, p, odd + p + 1)
                    beside = e(i, p + 1, odd + p + 1)
                    both = e(i + 1, p + 1, odd + p)
                    changes = (
                        (0, 0, here),
                        (1, 0, w(0, i, p) * here + w(1, i, p) * below),
                        (0, 1, w(2, i, p) * here + w(3, i, p) * beside),
                        (
                            1,
                            1,
                            (w(4, i, p) * here + w(5, i, p) * below)
                            + (w(6, i, p) * beside + w(7, i, p) * both),
                        ),
                    )
                    for a, b, change in changes:
                        colour = (a + b) % 2
                        t, r = 2 * i + a, 2 * p + b
                        grid.put(outs[colour], t, r, self.now[colour][t + 1, r + 1] + change)

        rows(dense.rows // 2, body, self.per)
        for colour in (0, 1):
            grid.wrap(outs[colour], self.per, colour)
            self.now[colour] = outs[colour]


def reorder(x, order):
    high = x.astype(BF16)
    rest = x - high.astype(F32)
    middle = rest.astype(BF16)
    low = (rest - middle.astype(F32)).astype(BF16)
    moved = [jnp.dot(part, order, preferred_element_type=F32) for part in (low, middle, high)]
    return (moved[0] + moved[1]) + moved[2]


def phase_matrix(swap, inverse):
    natural = lax.broadcasted_iota(jnp.int32, (COLS, COLS), 1 if inverse else 0)
    phased = lax.broadcasted_iota(jnp.int32, (COLS, COLS), 0 if inverse else 1)
    phase = natural & 3
    if swap:
        phase = phase ^ 1
    target = phase * 64 + (natural >> 2)
    return jnp.where(phased == target, 1.0, 0.0).astype(BF16)


def spread(field, own, halo, own_order, halo_order, own_out, halo_out):
    for out, x in ((own_out, reorder(own, own_order)), (halo_out, reorder(halo, halo_order))):
        for pair in (0, 1):
            out[field, pair] = x[:, pair * LANES : (pair + 1) * LANES]


def phases_of(field, t, own_out, halo_out, low):
    found = []
    for pair in (0, 1):
        window = (pl.ds(t, SUB, stride=ROWS), slice(None))
        own, halo = own_out.at[field, pair][window], halo_out.at[field, pair][window]
        found.append(jnp.where(low, own, halo))
        found.append(turn_lanes(jnp.where(low, halo, own), 64))
    return found


def fill_edges(level, col_place, own_out, halo_out):
    grid = level.grid
    lane = lax.broadcasted_iota(jnp.int32, (SUB, LANES), 1)
    strip = lax.broadcasted_iota(jnp.int32, (SUB, LANES), 0)
    low = lane < 64
    lane_start = col_place * 64 + jnp.where(lane < 96, lane, lane - LANES)
    count = lax.axis_size("col") * 64
    east_ok = jnp.where((lane_start == count - 1) | (lane_start == -1), 0.0, 1.0)
    west_ok = jnp.where((lane_start == 0) | (lane_start == count), 0.0, 1.0)
    last_strip = strip == SUB - 1

    def body(t):
        south_ok = jnp.where(last_strip & (t == ROWS - 1), 0.0, 1.0)
        for index in range(4):
            phases = phases_of(index, t, own_out, halo_out, low)
            for r, x in enumerate(phases):
                if index != 0:
                    x = x * south_ok
                if index in (0, 2) and r == 3:
                    x = x * east_ok
                if index == 3 and r == 0:
                    x = x * west_ok
                grid.put(level.own.at[index], t, r, x)

    rows(ROWS, body, level.per)
    for index in range(4):
        grid.wrap(level.own.at[index], level.per)

    def scaled(t):
        shift = phases_of(4, t, own_out, halo_out, low)
        for r in range(4):
            edges = [level.edge(a, b, t, r) for a, b in AROUND]
            pairs = [edges[i] + edges[i + 1] for i in range(0, 8, 2)]
            total = (pairs[0] + pairs[1]) + (pairs[2] + pairs[3])
            level.scale_edges(t, r, edges, shift[r] + total)

    rows(ROWS, scaled, level.per)


def fill_right(level, own_out, halo_out):
    grid = level.grid
    vector = level.residual
    lane = lax.broadcasted_iota(jnp.int32, (SUB, LANES), 1)
    low = lane < 64

    def body(t):
        for r, x in enumerate(phases_of(5, t, own_out, halo_out, low)):
            grid.put(vector, t, r, x)

    rows(ROWS, body, level.per)
    grid.wrap(vector, level.per)

    def image(u):
        for odd in (0, 1):
            for r in range(4):
                t = 2 * u + odd
                x = vector[t + 1, r + 1] - level.gathered(t, r, AROUND, lambda a, b: vector)
                grid.put(level.right, t, r, x)

    level.pairs(image)
    grid.wrap(level.right, level.per)


def setup(levels):
    for index in range(3):
        levels[index].find_weights()
        levels[index].find_product()
        levels[index].give_product(levels[index + 1])


def cycle(levels, index):
    level = levels[index]
    level.smooth_from_zero()
    if index == 3:
        return
    level.find_residual()
    level.restrict(levels[index + 1])
    cycle(levels, index + 1)
    level.prolong(levels[index + 1])
    level.smooth()


def total(x):
    return jnp.sum(jnp.sum(x, axis=0, keepdims=True), axis=1, keepdims=True)


def tell(solved, vector, previous):
    target = solved - previous
    length = total(vector * vector)
    projected = total(vector * target)
    near_alpha = jnp.where(length > 0.0, projected / jnp.where(length > 0.0, length, 1.0), 0.0)
    rest = target - near_alpha * vector
    squares = total(rest * rest)
    cross = total(vector * rest)
    inner = total(vector * solved)
    lane = lax.broadcasted_iota(jnp.int32, (1, LANES), 1)
    row = jnp.where(lane < 3, near_alpha, 0.0)
    for place, x in ((3, inner), (64, squares), (65, cross), (66, length)):
        row = jnp.where(lane == place, x, row)
    return row


def conclude(told, cells):
    lane = lax.broadcasted_iota(jnp.int32, told.shape, 1)
    alpha = total(jnp.where(lane == 3, told, 0.0)) / cells
    delta = alpha - told
    sums = pltpu.roll(told, 64, 1)
    weight = jnp.where(lane == 0, 1.0, jnp.where(lane == 1, -2.0 * delta, delta * delta))
    squares = total(jnp.where(lane < 3, weight * sums, 0.0)) / cells
    scale = jnp.sqrt(jnp.maximum(squares, 0.0) + EPSILON)
    return alpha, scale


def spread_edges(own, halo, own_out, halo_out):
    own_order, halo_order = phase_matrix(False, False), phase_matrix(True, False)
    for field in range(5):
        sides = [halo[:, side, field].reshape(SUB * ROWS, LANES) for side in (0, 1)]
        spread(
            field,
            own[:, field].reshape(SUB * ROWS, COLS),
            jnp.concatenate(sides, axis=1),
            own_order,
            halo_order,
            own_out,
            halo_out,
        )


def spread_vector(vector, vector_halo, own_out, halo_out):
    sides = [vector_halo[side].reshape(SUB * ROWS, LANES) for side in (0, 1)]
    spread(
        5,
        vector[...].reshape(SUB * ROWS, COLS),
        jnp.concatenate(sides, axis=1),
        phase_matrix(False, False),
        phase_matrix(True, False),
        own_out,
        halo_out,
    )


def take_solved(level, phased, solved):
    lane = lax.broadcasted_iota(jnp.int32, (SUB, LANES), 1)
    low = lane < 64

    def gather(u):
        for odd in (0, 1):
            t = 2 * u + odd
            x = [level.now[(odd + r) % 2][t + 1, r + 1] for r in range(4)]
            for pair in (0, 1):
                y = jnp.where(low, x[2 * pair], turn_lanes(x[2 * pair + 1], 64))
                phased.at[pair][pl.ds(t, SUB, stride=ROWS), :] = y

    rows(ROWS // 2, gather, level.per)
    result = reorder(
        jnp.concatenate([phased[0], phased[1]], axis=1), phase_matrix(False, True)
    )
    solved[...] = result.reshape(SUB, ROWS, COLS)


def compute(
    col_place, own, halo, vector, vector_halo, previous, solved, told, levels_refs, own_out, halo_out, phased, waits
):
    wait_vectors, wait_previous = waits
    levels = [Level(index, refs, WHOLE) for index, refs in enumerate(levels_refs)]
    spread_edges(own, halo, own_out, halo_out)
    fill_edges(levels[0], col_place, own_out, halo_out)
    setup(levels)
    wait_vectors()
    spread_vector(vector, vector_halo, own_out, halo_out)
    fill_right(levels[0], own_out, halo_out)
    cycle(levels, 0)
    take_solved(levels[0], phased, solved)
    wait_previous()
    whole = (SUB * ROWS, COLS)
    told[...] = tell(
        solved[...].reshape(whole), vector[...].reshape(whole), previous[...].reshape(whole)
    )


def copy_out(source, target, send, receive, grp, col):
    return pltpu.make_async_remote_copy(
        src_ref=source,
        dst_ref=target,
        send_sem=send,
        recv_sem=receive,
        device_id=(grp, col),
        device_id_type=MESH,
    )


def greet(partners):
    barrier = pltpu.get_barrier_semaphore()
    for grp, col in partners:
        pl.semaphore_signal(barrier, inc=1, device_id=(grp, col), device_id_type=MESH)
    pl.semaphore_wait(barrier, len(partners))


def gather_semaphores():
    dma = pltpu.SemaphoreType.DMA
    return [dma((2, 3)), dma((2, 7)), dma((2, 7)), dma((2, 8)), dma((2, 2)), dma((2, 4)), dma((2, 8))]


def gather_sources(g, conductance, shift, vector_in, previous_in, own, vector, previous):
    own[g, 0:4] = conductance[...]
    own[g, 4] = shift[...]
    vector[g] = vector_in[g]
    previous[g] = previous_in[g]


def gather(g, c, vector_in, previous_in, own, halo, vector, vector_halo, previous, semaphores):
    along, of_vector, of_previous, beside, vector_beside, across, halo_across = semaphores
    n_grp, n_col = 8, lax.axis_size("col")
    y, core = g // 2, g % 2
    twin = y * 2 + 1 - core
    mates = [(g + step) % n_grp for step in range(1, n_grp)]
    east, west = (c + 1) % n_col, (c + n_col - 1) % n_col
    started = []

    def start(copy):
        copy.start()
        started.append(copy)
        return copy

    def place(back):
        return ((y + 4 - back) % 4) * 2 + core

    def send_sides(back):
        rows_ = place(back)
        return [
            start(
                copy_out(
                    own.at[rows_, :, :, pl.ds(LANES, LANES)],
                    halo.at[rows_, 1],
                    beside.at[0, back],
                    beside.at[1, back],
                    g,
                    east,
                )
            ),
            start(
                copy_out(
                    own.at[rows_, :, :, pl.ds(0, LANES)],
                    halo.at[rows_, 0],
                    beside.at[0, 4 + back],
                    beside.at[1, 4 + back],
                    g,
                    west,
                )
            ),
        ]

    def send_across(back):
        rows_ = place(back)
        return start(
            copy_out(own.at[rows_], own.at[rows_], across.at[0, back], across.at[1, back], twin, c)
        )

    arriving = []
    for step in range(1, 4):
        to = ((y + step) % 4) * 2 + core
        arriving.append(
            start(
                copy_out(own.at[g], own.at[g], along.at[0, step - 1], along.at[1, step - 1], to, c)
            )
        )
    from_sides = [send_sides(0)]
    from_twin = [send_across(0)]
    vectors = [
        start(
            copy_out(
                vector_in.at[to], vector.at[g], of_vector.at[0, i], of_vector.at[1, i], to, c
            )
        )
        for i, to in enumerate(mates)
    ]
    for back in (1, 3, 2):
        arriving[back - 1].wait_recv()
        from_sides.append(send_sides(back))
        from_twin.append(send_across(back))
    for copy in vectors:
        copy.wait_recv()
    side_vectors = []
    for side, to in ((1, east), (0, west)):
        side_vectors.append(
            start(
                copy_out(
                    vector.at[:, :, pl.ds(side * LANES, LANES)],
                    vector_halo.at[side],
                    vector_beside.at[0, side],
                    vector_beside.at[1, side],
                    g,
                    to,
                )
            )
        )
    previouses = [
        start(
            copy_out(
                previous_in.at[to],
                previous.at[g],
                of_previous.at[0, i],
                of_previous.at[1, i],
                to,
                c,
            )
        )
        for i, to in enumerate(mates)
    ]
    halves = []
    for order, back in enumerate((0, 1, 3, 2)):
        for side in (1, 0):
            from_sides[order][1 - side].wait_recv()
            rows_ = place(back)
            at = side * 4 + back
            halves.append(
                start(
                    copy_out(
                        halo.at[rows_, side],
                        halo.at[rows_, side],
                        halo_across.at[0, at],
                        halo_across.at[1, at],
                        twin,
                        c,
                    )
                )
            )
    for copy in from_twin + halves:
        copy.wait_recv()

    def wait_vectors():
        for copy in side_vectors:
            copy.wait_recv()

    def wait_previous():
        for copy in previouses:
            copy.wait_recv()

    def wait_sends():
        for copy in started:
            copy.wait_send()

    return wait_vectors, wait_previous, wait_sends


def finish_semaphores():
    dma = pltpu.SemaphoreType.DMA
    return [dma((2,)), dma((2, 7)), dma((2,))]


def finish_scratch(n_col):
    return [
        pltpu.VMEM((8, ROWS, COLS), F32),
        pltpu.VMEM((n_col, 1, LANES), F32),
        pltpu.VMEM((8, 2, LANES), F32),
    ]


def conclude_all(g, c, vector_in, previous_in, solved, told, got, heard, verdicts, out, coefficients, semaphores):
    spread_sem, back_sem, verdict_sem = semaphores
    n_grp, n_col = 8, lax.axis_size("col")
    mates = [(g + step) % n_grp for step in range(1, n_grp)]
    heard[c] = told[...]
    telling = []
    for step in range(1, n_col):
        to = (c + step) % n_col
        telling.append(copy_out(told, heard.at[c], spread_sem.at[0], spread_sem.at[1], g, to))
        telling[-1].start()
    back = []
    for i, to in enumerate(mates):
        back.append(copy_out(solved.at[to], got.at[g], back_sem.at[0, i], back_sem.at[1, i], to, c))
        back[-1].start()
    got[g] = solved[g]
    several = heard.at[pl.ds(0, n_col - 1)]
    pltpu.make_async_copy(several, several, spread_sem.at[1]).wait()
    alpha, scale = conclude(heard[...].reshape(n_col, LANES), float(n_grp * ROWS * n_col * COLS))
    which = lax.broadcasted_iota(jnp.int32, (2, LANES), 0)
    verdicts[g] = jnp.where(which == 0, alpha, scale)
    deciding = []
    for to in mates:
        deciding.append(
            copy_out(verdicts.at[g], verdicts.at[g], verdict_sem.at[0], verdict_sem.at[1], to, c)
        )
        deciding[-1].start()
    for copy in back:
        copy.wait_recv()
    others = verdicts.at[pl.ds(0, n_grp - 1)]
    pltpu.make_async_copy(others, others, verdict_sem.at[1]).wait()
    lane = lax.broadcasted_iota(jnp.int32, (2, LANES), 1)
    summary = jnp.zeros((2, LANES), F32)
    for probe in range(n_grp):
        pair = verdicts[probe]
        summary = jnp.where(lane == probe, pair, summary)
        rest = got[probe] - pair[0:1, 0:1] * vector_in[probe] - previous_in[probe]
        out[probe] = rest * (1.0 / pair[1:2, 0:1])
    coefficients[...] = summary[:, 0:n_grp]
    pltpu.make_async_copy(several, several, spread_sem.at[0]).wait()
    pltpu.make_async_copy(others, others, verdict_sem.at[0]).wait()
    for copy in back:
        copy.wait_send()


def flat_levels():
    return jax.tree.flatten(level_scratch())


def spread_scratch():
    return [pltpu.VMEM((6, 2, 8 * ROWS, LANES), F32)] * 2 + [pltpu.VMEM((2, 8 * ROWS, LANES), F32)]


VMEM = pl.BlockSpec(memory_space=pltpu.VMEM)
ANY = pl.BlockSpec(memory_space=pl.ANY)
LIMIT = 48 * 1024 * 1024


def shape(*dims):
    return jax.ShapeDtypeStruct(dims, F32)


def step_kernel(conductance, shift, vector_hbm, previous_hbm, out, coefficients, *scratch):
    leaves, tree = flat_levels()
    count = len(leaves)
    levels_refs = jax.tree.unflatten(tree, scratch[:count])
    (own_out, halo_out, phased, vector_in, previous_in, own, halo, vector, vector_halo, previous, solved, told, got, heard, verdicts, loads) = scratch[count : count + 16]
    semaphores = scratch[count + 16 :]
    g, c = lax.axis_index("grp"), lax.axis_index("col")
    n_col = lax.axis_size("col")
    loading = [
        pltpu.make_async_copy(conductance, own.at[g, pl.ds(0, 4)], loads.at[0]),
        pltpu.make_async_copy(shift, own.at[g, 4], loads.at[1]),
        pltpu.make_async_copy(vector_hbm, vector_in, loads.at[2]),
        pltpu.make_async_copy(previous_hbm, previous_in, loads.at[3]),
    ]
    for copy in loading:
        copy.start()
    barrier = pltpu.get_barrier_semaphore()
    partners = [((g + step) % 8, c) for step in range(1, 8)]
    partners += [(g, (c + step) % n_col) for step in range(1, n_col)]
    for grp, col in partners:
        pl.semaphore_signal(barrier, inc=1, device_id=(grp, col), device_id_type=MESH)
    for copy in loading:
        copy.wait()
    vector[g] = vector_in[g]
    previous[g] = previous_in[g]
    pl.semaphore_wait(barrier, len(partners))
    wait_vectors, wait_previous, wait_sends = gather(
        g, c, vector_in, previous_in, own, halo, vector, vector_halo, previous, semaphores[:7]
    )
    compute(c, own, halo, vector, vector_halo, previous, solved, told, levels_refs, own_out, halo_out, phased, (wait_vectors, wait_previous))
    conclude_all(g, c, vector_in, previous_in, solved, told, got, heard, verdicts, out, coefficients, semaphores[7:])
    wait_sends()


def local(conductance, shift, vector_in, previous_in):
    n_col = lax.axis_size("col")
    leaves, _ = flat_levels()
    tile = (8, ROWS, COLS)
    return pl.pallas_call(
        step_kernel,
        out_shape=(shape(8, ROWS, COLS), shape(2, 8)),
        in_specs=[ANY] * 4,
        out_specs=(VMEM,) * 2,
        scratch_shapes=leaves
        + spread_scratch()
        + [
            pltpu.VMEM(dims, F32)
            for dims in (
                tile,
                tile,
                (8, 5, ROWS, COLS),
                (8, 2, 5, ROWS, LANES),
                tile,
                (2, 8, ROWS, LANES),
                tile,
                tile,
                (1, LANES),
            )
        ]
        + finish_scratch(n_col)
        + [pltpu.SemaphoreType.DMA((4,))]
        + gather_semaphores()
        + finish_semaphores(),
        compiler_params=pltpu.CompilerParams(
            collective_id=0, has_side_effects=True, vmem_limit_bytes=LIMIT
        ),
        name="lanczos_step",
    )(conductance, shift, vector_in, previous_in)


def solution(mesh):
    in_specs = (
        P(None, "grp", "col"),
        P("grp", "col"),
        P(None, "grp", "col"),
        P(None, "grp", "col"),
    )
    out_specs = (P(None, "grp", "col"), P())
    return jax.shard_map(local, mesh=mesh, in_specs=in_specs, out_specs=out_specs, check_vma=False)
```

```python
import jax
import jax.numpy as jnp
from jax import lax
from jax.experimental import pallas as pl
from jax.experimental.pallas import tpu as pltpu
from jax.sharding import PartitionSpec as P

F32 = jnp.float32
BF16 = jnp.bfloat16
EPSILON = 1e-06
LANES = 128
SUB = 8
WHOLE = 99
ROWS = 16
COLS = 256
MESH = pl.DeviceIdType.MESH

LEVEL_ROWS = (16, 8, 4, 2)
LEVEL_PHASES = (4, 2, 2, 2)
LEVEL_STRIDE = (1, 1, 2, 4)
AROUND = ((-1, 0), (1, 0), (0, -1), (0, 1), (-1, -1), (-1, 1), (1, -1), (1, 1))
PLACE = {offset: index for index, offset in enumerate(AROUND)}


def turn_lanes(x, by):
    return pltpu.roll(x, by % LANES, 1)


def turn_strips(x, by):
    return pltpu.roll(x, by % SUB, 0)


def rows(count, body, per):
    if per >= count:
        for index in range(count):
            body(index)
    else:

        def step(index, carry):
            for inner in range(per):
                body(index * per + inner)
            return carry

        lax.fori_loop(0, count // per, step, 0)


class Grid:
    def __init__(self, rows_, phases, stride):
        self.rows, self.phases, self.stride = rows_, phases, stride

    @property
    def ghosted(self):
        return (self.rows + 2, self.phases + 2, SUB, LANES)

    @property
    def bare(self):
        return (self.rows, self.phases, SUB, LANES)

    def put(self, ref, t, r, x):
        places = [(r + 1, x)]
        if r == 0:
            places.append((self.phases + 1, turn_lanes(x, -self.stride)))
        if r == self.phases - 1:
            places.append((0, turn_lanes(x, self.stride)))
        for place, y in places:
            ref[t + 1, place] = y
            if isinstance(t, int) and t == 0:
                ref[self.rows + 1, place] = turn_strips(y, -1)
            if isinstance(t, int) and t == self.rows - 1:
                ref[0, place] = turn_strips(y, 1)

    def wrap(self, ref, per, colour=None):
        if per >= self.rows:
            return
        for r in range(-1, self.phases + 1):
            if colour is None or (self.rows - 1 + r) % 2 == colour:
                ref[0, r + 1] = turn_strips(ref[self.rows, r + 1], 1)
            if colour is None or r % 2 == colour:
                ref[self.rows + 1, r + 1] = turn_strips(ref[1, r + 1], -1)


GRIDS = tuple(Grid(*sizes) for sizes in zip(LEVEL_ROWS, LEVEL_PHASES, LEVEL_STRIDE))
DENSE = tuple(Grid(g.rows // 2, g.phases // 2, g.stride) for g in GRIDS[:3])


def level_scratch():
    shapes = []
    for index, grid in enumerate(GRIDS):
        entry = {
            "own": (4,) + grid.ghosted,
            "dia": grid.bare,
            "inv": grid.bare,
            "near": (8,) + grid.bare,
            "right": grid.ghosted,
            "red0": grid.ghosted,
            "red1": grid.ghosted,
            "black0": grid.ghosted,
            "black1": grid.ghosted,
        }
        if index < 3:
            dense = DENSE[index]
            entry["weights"] = (8,) + dense.ghosted
            entry["passed"] = (6,) + dense.ghosted
            entry["kept"] = (5,) + dense.bare
            entry["residual"] = grid.ghosted
            entry["lifted"] = dense.ghosted
        shapes.append({name: pltpu.VMEM(shape, F32) for name, shape in entry.items()})
    return shapes


class Level:
    def __init__(self, index, refs, per):
        self.index, self.grid, self.per = index, GRIDS[index], per
        for name, ref in refs.items():
            setattr(self, name, ref)
        self.buffers = ((self.red0, self.red1), (self.black0, self.black1))
        self.now = [self.right, None]

    def pairs(self, body):
        rows(self.grid.rows // 2, body, self.per)

    def edge(self, a, b, t, r):
        own = self.own
        if (a, b) == (0, 1):
            return own[0, t + 1, r + 1]
        if (a, b) == (0, -1):
            return own[0, t + 1, r]
        if (a, b) == (1, 0):
            return own[1, t + 1, r + 1]
        if (a, b) == (-1, 0):
            return own[1, t, r + 1]
        if (a, b) == (1, 1):
            return own[2, t + 1, r + 1]
        if (a, b) == (-1, -1):
            return own[2, t, r]
        if (a, b) == (1, -1):
            return own[3, t + 1, r + 1]
        return own[3, t, r + 2]

    def scale_edges(self, t, r, edges, diagonal):
        inverse = 1.0 / diagonal
        self.dia[t, r] = diagonal
        self.inv[t, r] = inverse
        for index, edge in enumerate(edges):
            self.near[index, t, r] = edge * inverse

    def gathered(self, t, r, offsets, source, start=None):
        terms = [
            self.near[PLACE[a, b], t, r] * source(a, b)[t + 1 + a, r + 1 + b] for a, b in offsets
        ]
        if start is not None:
            terms.append(start)
        while len(terms) > 1:
            terms = [
                terms[i] + terms[i + 1] if i + 1 < len(terms) else terms[i]
                for i in range(0, len(terms), 2)
            ]
        return terms[0]

    def spare(self, colour):
        first, second = self.buffers[colour]
        return second if self.now[colour] is first else first

    def half_sweep(self, colour):
        grid, other, same = self.grid, self.now[1 - colour], self.now[colour]
        out = self.spare(colour)
        offsets = AROUND if same is not None else AROUND[:4]

        def body(u):
            for odd in (0, 1):
                for r in range(grid.phases):
                    if (odd + r) % 2 == colour:
                        t = 2 * u + odd
                        x = self.gathered(
                            t,
                            r,
                            offsets,
                            lambda a, b: other if (a + b) % 2 else same,
                            self.right[t + 1, r + 1],
                        )
                        grid.put(out, t, r, x)

        self.pairs(body)
        grid.wrap(out, self.per, colour)
        self.now[colour] = out

    def smooth_from_zero(self):
        self.now = [self.right, None]
        for colour in (1, 0, 1):
            self.half_sweep(colour)

    def smooth(self):
        for colour in (0, 1, 0, 1):
            self.half_sweep(colour)

    def find_residual(self):
        grid = self.grid

        def body(u):
            for odd in (0, 1):
                for r in range(grid.phases):
                    t = 2 * u + odd
                    colour = (odd + r) % 2
                    x = self.gathered(
                        t,
                        r,
                        AROUND,
                        lambda a, b: self.now[(colour + a + b) % 2],
                        self.right[t + 1, r + 1] - self.now[colour][t + 1, r + 1],
                    )
                    grid.put(self.residual, t, r, self.dia[t, r] * x)

        self.pairs(body)
        grid.wrap(self.residual, self.per)

    def find_weights(self):
        grid, dense, edge = self.grid, DENSE[self.index], self.edge

        def edges(i):
            for p in range(dense.phases):
                t, r = 2 * i + 1, 2 * p
                middle = 1.0 / (self.dia[t, r] - edge(0, -1, t, r) - edge(0, 1, t, r))
                up = edge(-1, 0, t, r) + edge(-1, -1, t, r) + edge(-1, 1, t, r)
                down = edge(1, 0, t, r) + edge(1, -1, t, r) + edge(1, 1, t, r)
                dense.put(self.weights.at[0], i, p, up * middle)
                dense.put(self.weights.at[1], i, p, down * middle)
                t, r = 2 * i, 2 * p + 1
                middle = 1.0 / (self.dia[t, r] - edge(-1, 0, t, r) - edge(1, 0, t, r))
                left = edge(0, -1, t, r) + edge(-1, -1, t, r) + edge(1, -1, t, r)
                right = edge(0, 1, t, r) + edge(-1, 1, t, r) + edge(1, 1, t, r)
                dense.put(self.weights.at[2], i, p, left * middle)
                dense.put(self.weights.at[3], i, p, right * middle)

        rows(dense.rows, edges, self.per)
        for index in range(4):
            dense.wrap(self.weights.at[index], self.per)
        w = self.weight

        def corners(i):
            for p in range(dense.phases):
                n = lambda a, b: self.near[PLACE[a, b], 2 * i + 1, 2 * p + 1]
                here = n(-1, -1) + n(0, -1) * w(0, i, p) + n(-1, 0) * w(2, i, p)
                down = n(1, -1) + n(0, -1) * w(1, i, p) + n(1, 0) * w(2, i + 1, p)
                right = n(-1, 1) + n(0, 1) * w(0, i, p + 1) + n(-1, 0) * w(3, i, p)
                both = n(1, 1) + n(0, 1) * w(1, i, p + 1) + n(1, 0) * w(3, i + 1, p)
                for index, x in enumerate((here, down, right, both)):
                    dense.put(self.weights.at[4 + index], i, p, x)

        rows(dense.rows, corners, self.per)
        for index in range(4, 8):
            dense.wrap(self.weights.at[index], self.per)

    def weight(self, index, i, p):
        return self.weights[index, i + 1, p + 1]

    def find_product(self):
        dense, w = DENSE[self.index], self.weight
        up, down, left, right, here, below, beside, both = range(8)

        def body(i):
            for p in range(dense.phases):
                t, r = 2 * i, 2 * p
                c = lambda a, b: self.edge(a, b, t, r)
                center = (
                    self.dia[t, r]
                    - c(-1, 0) * w(down, i - 1, p)
                    - c(1, 0) * w(up, i, p)
                    - c(0, -1) * w(right, i, p - 1)
                    - c(0, 1) * w(left, i, p)
                ) - (
                    c(-1, -1) * w(both, i - 1, p - 1)
                    + c(-1, 1) * w(below, i - 1, p)
                    + c(1, -1) * w(beside, i, p - 1)
                    + c(1, 1) * w(here, i, p)
                )
                east = -(
                    c(0, 1) * w(right, i, p)
                    + c(-1, 1) * w(both, i - 1, p)
                    + c(1, 1) * w(beside, i, p)
                )
                south = -(
                    c(1, 0) * w(down, i, p)
                    + c(1, 1) * w(below, i, p)
                    + c(1, -1) * w(both, i, p - 1)
                )
                south_east = -c(1, 1) * w(both, i, p)
                south_west = -c(1, -1) * w(below, i, p - 1)
                t, r = 2 * i + 1, 2 * p
                v = lambda a, b: self.edge(a, b, t, r)
                d = self.dia[t, r]
                v00 = (
                    d * w(up, i, p)
                    - v(-1, 0)
                    - v(-1, -1) * w(right, i, p - 1)
                    - v(-1, 1) * w(left, i, p)
                    - v(0, -1) * w(beside, i, p - 1)
                    - v(0, 1) * w(here, i, p)
                )
                v10 = (
                    d * w(down, i, p)
                    - v(1, 0)
                    - v(1, -1) * w(right, i + 1, p - 1)
                    - v(1, 1) * w(left, i + 1, p)
                    - v(0, -1) * w(both, i, p - 1)
                    - v(0, 1) * w(below, i, p)
                )
                v01 = -v(-1, 1) * w(right, i, p) - v(0, 1) * w(beside, i, p)
                v11 = -v(1, 1) * w(right, i + 1, p) - v(0, 1) * w(both, i, p)
                v1m = -v(1, -1) * w(left, i + 1, p - 1) - v(0, -1) * w(below, i, p - 1)
                t, r = 2 * i, 2 * p + 1
                h = lambda a, b: self.edge(a, b, t, r)
                d = self.dia[t, r]
                h00 = (
                    d * w(left, i, p)
                    - h(0, -1)
                    - h(-1, -1) * w(down, i - 1, p)
                    - h(1, -1) * w(up, i, p)
                    - h(-1, 0) * w(below, i - 1, p)
                    - h(1, 0) * w(here, i, p)
                )
                h01 = (
                    d * w(right, i, p)
                    - h(0, 1)
                    - h(-1, 1) * w(down, i - 1, p + 1)
                    - h(1, 1) * w(up, i, p + 1)
                    - h(-1, 0) * w(both, i - 1, p)
                    - h(1, 0) * w(beside, i, p)
                )
                h10 = -h(1, -1) * w(down, i, p) - h(1, 0) * w(below, i, p)
                h11 = -h(1, 1) * w(down, i, p + 1) - h(1, 0) * w(both, i, p)
                t, r = 2 * i + 1, 2 * p + 1
                k = lambda a, b: self.edge(a, b, t, r)
                d = self.dia[t, r]
                k00 = (
                    d * w(here, i, p)
                    - k(-1, -1)
                    - k(-1, 0) * w(left, i, p)
                    - k(0, -1) * w(up, i, p)
                )
                k10 = (
                    d * w(below, i, p)
                    - k(1, -1)
                    - k(1, 0) * w(left, i + 1, p)
                    - k(0, -1) * w(down, i, p)
                )
                k01 = (
                    d * w(beside, i, p)
                    - k(-1, 1)
                    - k(-1, 0) * w(right, i, p)
                    - k(0, 1) * w(up, i, p + 1)
                )
                k11 = (
                    d * w(both, i, p)
                    - k(1, 1)
                    - k(1, 0) * w(right, i + 1, p)
                    - k(0, 1) * w(down, i, p + 1)
                )
                wu, wd, wl, wr = (w(index, i, p) for index in (up, down, left, right))
                ch, cd, cr, cb = (w(index, i, p) for index in (here, below, beside, both))
                self.kept[0, i, p] = center + (wu * v00 + wl * h00) + ch * k00
                self.kept[1, i, p] = east + (wu * v01 + wl * h01) + ch * k01
                self.kept[2, i, p] = south + (wu * v10 + wl * h10) + ch * k10
                self.kept[3, i, p] = south_east + (wu * v11 + wl * h11) + ch * k11
                self.kept[4, i, p] = south_west + wu * v1m
                passed = (
                    wd * v10 + cd * k10,
                    wd * v11 + cd * k11,
                    wr * h01 + cr * k01,
                    wr * h11 + cr * k11,
                    wr * h10 + cr * k10,
                    cb * k11,
                )
                for index, x in enumerate(passed):
                    dense.put(self.passed.at[index], i, p, x)

        rows(dense.rows, body, self.per)
        for index in range(6):
            dense.wrap(self.passed.at[index], self.per)

    def give_product(self, coarse):
        dense, grid = DENSE[self.index], coarse.grid

        def body(i):
            for p in range(dense.phases):
                sent = lambda index, di, dp: self.passed[index, i + 1 + di, p + 1 + dp]
                center = (
                    self.kept[0, i, p] + sent(0, -1, 0) + sent(2, 0, -1) + sent(5, -1, -1)
                )
                entries = (
                    self.kept[1, i, p] + sent(1, -1, 0),
                    self.kept[2, i, p] + sent(3, 0, -1),
                    self.kept[3, i, p],
                    self.kept[4, i, p] + sent(4, 0, -1),
                )
                for phase, by in coarse.places(p, dense):
                    coarse.dia[i, phase] = center if by == 0 else turn_lanes(center, by)
                    for index, x in enumerate(entries):
                        x = -x if by == 0 else turn_lanes(-x, by)
                        grid.put(coarse.own.at[index], i, phase, x)

        rows(dense.rows, body, coarse.per)
        for index in range(4):
            grid.wrap(coarse.own.at[index], coarse.per)

        def scaled(u):
            for odd in (0, 1):
                for r in range(grid.phases):
                    t = 2 * u + odd
                    coarse.scale_edges(
                        t, r, [coarse.edge(a, b, t, r) for a, b in AROUND], coarse.dia[t, r]
                    )

        coarse.pairs(scaled)

    def places(self, p, dense):
        if dense.phases == self.grid.phases:
            return ((p, 0),)
        return ((0, 0), (1, -dense.stride))

    def restrict(self, coarse):
        dense, w, res = DENSE[self.index], self.weight, self.residual

        def body(i):
            for p in range(dense.phases):
                f = lambda a, b: res[2 * i + a + 1, 2 * p + b + 1]
                x = (
                    (f(0, 0) + w(0, i, p) * f(1, 0))
                    + (w(1, i - 1, p) * f(-1, 0) + w(2, i, p) * f(0, 1))
                ) + (
                    (w(3, i, p - 1) * f(0, -1) + w(4, i, p) * f(1, 1))
                    + (
                        (w(5, i - 1, p) * f(-1, 1) + w(6, i, p - 1) * f(1, -1))
                        + w(7, i - 1, p - 1) * f(-1, -1)
                    )
                )
                for phase, by in coarse.places(p, dense):
                    y = x if by == 0 else turn_lanes(x, by)
                    coarse.grid.put(coarse.right, i, phase, y * coarse.inv[i, phase])

        rows(dense.rows, body, coarse.per)
        coarse.grid.wrap(coarse.right, coarse.per)

    def prolong(self, coarse):
        grid, dense, w = self.grid, DENSE[self.index], self.weight
        if dense.phases == coarse.grid.phases:
            e = lambda i, p, parity: coarse.now[parity % 2][i + 1, p + 1]
        else:
            lane = lax.broadcasted_iota(jnp.int32, (SUB, LANES), 1)
            even = (lane & dense.stride) == 0
            for i in range(dense.rows):
                first = coarse.now[i % 2][i + 1, 1]
                second = turn_lanes(coarse.now[(i + 1) % 2][i + 1, 2], dense.stride)
                dense.put(self.lifted, i, 0, jnp.where(even, first, second))
            e = lambda i, p, parity: self.lifted[i + 1, p + 1]
        outs = [self.spare(0), self.spare(1)]

        def body(v):
            for odd in (0, 1):
                i = 2 * v + odd
                for p in range(dense.phases):
                    here = e(i, p, odd + p)
                    below = e(i + 1, p, odd + p + 1)
                    beside = e(i, p + 1, odd + p + 1)
                    both = e(i + 1, p + 1, odd + p)
                    changes = (
                        (0, 0, here),
                        (1, 0, w(0, i, p) * here + w(1, i, p) * below),
                        (0, 1, w(2, i, p) * here + w(3, i, p) * beside),
                        (
                            1,
                            1,
                            (w(4, i, p) * here + w(5, i, p) * below)
                            + (w(6, i, p) * beside + w(7, i, p) * both),
                        ),
                    )
                    for a, b, change in changes:
                        colour = (a + b) % 2
                        t, r = 2 * i + a, 2 * p + b
                        grid.put(outs[colour], t, r, self.now[colour][t + 1, r + 1] + change)

        rows(dense.rows // 2, body, self.per)
        for colour in (0, 1):
            grid.wrap(outs[colour], self.per, colour)
            self.now[colour] = outs[colour]


def reorder(x, order):
    high = x.astype(BF16)
    rest = x - high.astype(F32)
    middle = rest.astype(BF16)
    low = (rest - middle.astype(F32)).astype(BF16)
    moved = [jnp.dot(part, order, preferred_element_type=F32) for part in (low, middle, high)]
    return (moved[0] + moved[1]) + moved[2]


def phase_matrix(swap, inverse):
    natural = lax.broadcasted_iota(jnp.int32, (COLS, COLS), 1 if inverse else 0)
    phased = lax.broadcasted_iota(jnp.int32, (COLS, COLS), 0 if inverse else 1)
    phase = natural & 3
    if swap:
        phase = phase ^ 1
    target = phase * 64 + (natural >> 2)
    return jnp.where(phased == target, 1.0, 0.0).astype(BF16)


def reordered(x, order, out):
    moved = reorder(x, order)
    for pair in (0, 1):
        out[pair] = moved[:, pair * LANES : (pair + 1) * LANES]


def phases_of(field, t, own_out, halo_out, low):
    found = []
    for pair in (0, 1):
        window = (pl.ds(t, SUB, stride=ROWS), slice(None))
        own, halo = own_out.at[field, pair][window], halo_out.at[field, pair][window]
        found.append(jnp.where(low, own, halo))
        found.append(turn_lanes(jnp.where(low, halo, own), 64))
    return found


def fill_edges(level, col_place, own_out, halo_out):
    grid = level.grid
    lane = lax.broadcasted_iota(jnp.int32, (SUB, LANES), 1)
    strip = lax.broadcasted_iota(jnp.int32, (SUB, LANES), 0)
    low = lane < 64
    lane_start = col_place * 64 + jnp.where(lane < 96, lane, lane - LANES)
    count = lax.axis_size("col") * 64
    east_ok = jnp.where((lane_start == count - 1) | (lane_start == -1), 0.0, 1.0)
    west_ok = jnp.where((lane_start == 0) | (lane_start == count), 0.0, 1.0)
    last_strip = strip == SUB - 1

    def body(t):
        south_ok = jnp.where(last_strip & (t == ROWS - 1), 0.0, 1.0)
        for index in range(4):
            phases = phases_of(index, t, own_out, halo_out, low)
            for r, x in enumerate(phases):
                if index != 0:
                    x = x * south_ok
                if index in (0, 2) and r == 3:
                    x = x * east_ok
                if index == 3 and r == 0:
                    x = x * west_ok
                grid.put(level.own.at[index], t, r, x)

    rows(ROWS, body, level.per)
    for index in range(4):
        grid.wrap(level.own.at[index], level.per)

    def scaled(t):
        shift = phases_of(4, t, own_out, halo_out, low)
        for r in range(4):
            edges = [level.edge(a, b, t, r) for a, b in AROUND]
            pairs = [edges[i] + edges[i + 1] for i in range(0, 8, 2)]
            total = (pairs[0] + pairs[1]) + (pairs[2] + pairs[3])
            level.scale_edges(t, r, edges, shift[r] + total)

    rows(ROWS, scaled, level.per)


def fill_right(level, own_out, halo_out):
    grid = level.grid
    vector = level.residual
    lane = lax.broadcasted_iota(jnp.int32, (SUB, LANES), 1)
    low = lane < 64

    def body(t):
        for r, x in enumerate(phases_of(5, t, own_out, halo_out, low)):
            grid.put(vector, t, r, x)

    rows(ROWS, body, level.per)
    grid.wrap(vector, level.per)

    def image(u):
        for odd in (0, 1):
            for r in range(4):
                t = 2 * u + odd
                x = vector[t + 1, r + 1] - level.gathered(t, r, AROUND, lambda a, b: vector)
                grid.put(level.right, t, r, x)

    level.pairs(image)
    grid.wrap(level.right, level.per)


def setup(levels):
    for index in range(3):
        levels[index].find_weights()
        levels[index].find_product()
        levels[index].give_product(levels[index + 1])


def cycle(levels, index):
    level = levels[index]
    level.smooth_from_zero()
    if index == 3:
        return
    level.find_residual()
    level.restrict(levels[index + 1])
    cycle(levels, index + 1)
    level.prolong(levels[index + 1])
    level.smooth()


def total(x):
    return jnp.sum(jnp.sum(x, axis=0, keepdims=True), axis=1, keepdims=True)


def tell(solved, vector, previous):
    target = solved - previous
    length = total(vector * vector)
    projected = total(vector * target)
    near_alpha = jnp.where(length > 0.0, projected / jnp.where(length > 0.0, length, 1.0), 0.0)
    rest = target - near_alpha * vector
    squares = total(rest * rest)
    cross = total(vector * rest)
    inner = total(vector * solved)
    lane = lax.broadcasted_iota(jnp.int32, (1, LANES), 1)
    row = jnp.where(lane < 3, near_alpha, 0.0)
    for place, x in ((3, inner), (64, squares), (65, cross), (66, length)):
        row = jnp.where(lane == place, x, row)
    return row


def conclude(told, cells):
    lane = lax.broadcasted_iota(jnp.int32, told.shape, 1)
    alpha = total(jnp.where(lane == 3, told, 0.0)) / cells
    delta = alpha - told
    sums = pltpu.roll(told, 64, 1)
    weight = jnp.where(lane == 0, 1.0, jnp.where(lane == 1, -2.0 * delta, delta * delta))
    squares = total(jnp.where(lane < 3, weight * sums, 0.0)) / cells
    scale = jnp.sqrt(jnp.maximum(squares, 0.0) + EPSILON)
    return alpha, scale


def spread_own(own, own_out):
    order = phase_matrix(False, False)
    for field in range(5):
        reordered(own[:, field].reshape(SUB * ROWS, COLS), order, own_out.at[field])


def spread_halo(halo, halo_out):
    order = phase_matrix(True, False)
    for field in range(5):
        sides = [halo[:, side, field].reshape(SUB * ROWS, LANES) for side in (0, 1)]
        reordered(jnp.concatenate(sides, axis=1), order, halo_out.at[field])


def spread_vector(vector, vector_halo, own_out, halo_out):
    reordered(vector[...].reshape(SUB * ROWS, COLS), phase_matrix(False, False), own_out.at[5])
    sides = [vector_halo[side].reshape(SUB * ROWS, LANES) for side in (0, 1)]
    reordered(jnp.concatenate(sides, axis=1), phase_matrix(True, False), halo_out.at[5])


def pack_solved(level, phased):
    lane = lax.broadcasted_iota(jnp.int32, (SUB, LANES), 1)
    low = lane < 64
    for t in range(ROWS):
        x = [level.now[(t + r) % 2][t + 1, r + 1] for r in range(4)]
        for pair in (0, 1):
            y = jnp.where(low, x[2 * pair], turn_lanes(x[2 * pair + 1], 64))
            phased.at[pair][pl.ds(t, SUB, stride=ROWS), :] = y


def compute(
    col_place, halo, vector, vector_halo, previous, levels_refs, own_out, halo_out, phased, before, waits
):
    wait_vectors, wait_previous = waits
    levels = [Level(index, refs, WHOLE) for index, refs in enumerate(levels_refs)]
    spread_halo(halo, halo_out)
    fill_edges(levels[0], col_place, own_out, halo_out)
    setup(levels)
    wait_vectors()
    spread_vector(vector, vector_halo, own_out, halo_out)
    fill_right(levels[0], own_out, halo_out)
    wait_previous()
    reordered(previous[...].reshape(SUB * ROWS, COLS), phase_matrix(False, False), before)
    cycle(levels, 0)
    pack_solved(levels[0], phased)


def make_told(told, phased, own_out, before):
    flat = (2 * SUB * ROWS, LANES)
    told[...] = tell(phased[...].reshape(flat), own_out[5].reshape(flat), before[...].reshape(flat))


def copy_out(source, target, send, receive, grp, col):
    return pltpu.make_async_remote_copy(
        src_ref=source,
        dst_ref=target,
        send_sem=send,
        recv_sem=receive,
        device_id=(grp, col),
        device_id_type=MESH,
    )


def greet(partners):
    barrier = pltpu.get_barrier_semaphore()
    for grp, col in partners:
        pl.semaphore_signal(barrier, inc=1, device_id=(grp, col), device_id_type=MESH)
    pl.semaphore_wait(barrier, len(partners))


def gather_semaphores():
    dma = pltpu.SemaphoreType.DMA
    return [dma((4,)), dma((2,)), dma((2,)), dma((5,)), dma((2,)), dma((2,)), dma((2,))]


def wait_bytes(ref, semaphore):
    pltpu.make_async_copy(ref, ref, semaphore).wait()


def gather_sources(g, conductance, shift, vector_in, previous_in, own, vector, previous):
    own[g, 0:4] = conductance[...]
    own[g, 4] = shift[...]
    vector[g] = vector_in[g]
    previous[g] = previous_in[g]


def gather(g, c, vector_in, previous_in, own, halo, vector, vector_halo, previous, semaphores, while_waiting):
    along, of_vector, of_previous, beside, vector_beside, across, halo_across = semaphores
    n_grp, n_col = 8, lax.axis_size("col")
    y, core = g // 2, g % 2
    twin = y * 2 + 1 - core
    mates = [(g + step) % n_grp for step in range(1, n_grp)]
    east, west = (c + 1) % n_col, (c + n_col - 1) % n_col

    def place(back):
        return ((y + 4 - back) % 4) * 2 + core

    def send_sides(back):
        row = place(back)
        for side, to in ((1, east), (0, west)):
            copy_out(
                own.at[row, :, :, pl.ds(side * LANES, LANES)],
                halo.at[row, side],
                beside.at[4],
                beside.at[back],
                g,
                to,
            ).start()

    def pass_tile(back):
        row = place(back)
        copy_out(own.at[row], own.at[row], across.at[0], across.at[1], twin, c).start()

    def pass_sides(back):
        row = place(back)
        wait_bytes(halo.at[row], beside.at[back])
        copy_out(halo.at[row], halo.at[row], halo_across.at[0], halo_across.at[1], twin, c).start()

    def transpose(source, target, semaphore):
        for to in mates:
            copy_out(source.at[to], target.at[g], semaphore.at[0], semaphore.at[1], to, c).start()

    for step in (1, 3, 2):
        to = ((y + step) % 4) * 2 + core
        copy_out(own.at[g], own.at[g], along.at[0], along.at[step], to, c).start()
    send_sides(0)
    pass_tile(0)
    transpose(vector_in, vector, of_vector)
    for back in (1, 3, 2):
        row = place(back)
        wait_bytes(own.at[row], along.at[back])
        send_sides(back)
        pass_tile(back)
    wait_bytes(vector.at[pl.ds(0, n_grp - 1)], of_vector.at[1])
    for side, to in ((1, east), (0, west)):
        copy_out(
            vector.at[:, :, pl.ds(side * LANES, LANES)],
            vector_halo.at[side],
            vector_beside.at[0],
            vector_beside.at[1],
            g,
            to,
        ).start()
    transpose(previous_in, previous, of_previous)
    for back in (0, 1, 3):
        pass_sides(back)
    wait_bytes(own.at[pl.ds(0, 4)], across.at[1])
    while_waiting()
    pass_sides(2)
    wait_bytes(halo.at[pl.ds(0, 4)], halo_across.at[1])

    def wait_vectors():
        wait_bytes(vector_halo, vector_beside.at[1])

    def wait_previous():
        wait_bytes(previous.at[pl.ds(0, n_grp - 1)], of_previous.at[1])

    def wait_sends():
        wait_bytes(own.at[pl.ds(0, 3)], along.at[0])
        wait_bytes(halo.at[pl.ds(0, 4)], beside.at[4])
        wait_bytes(own.at[pl.ds(0, 4)], across.at[0])
        wait_bytes(halo.at[pl.ds(0, 4)], halo_across.at[0])
        wait_bytes(vector.at[pl.ds(0, n_grp - 1)], of_vector.at[0])
        wait_bytes(previous.at[pl.ds(0, n_grp - 1)], of_previous.at[0])
        wait_bytes(vector_halo, vector_beside.at[0])

    return wait_vectors, wait_previous, wait_sends


def finish_semaphores():
    dma = pltpu.SemaphoreType.DMA
    return [dma((2,)), dma((2,)), dma((2,)), dma((1,))]


def finish_scratch(n_col):
    return [
        pltpu.VMEM((8, 2, ROWS, LANES), F32),
        pltpu.VMEM((n_col, 1, LANES), F32),
        pltpu.VMEM((8, 2, LANES), F32),
        pltpu.VMEM((8, ROWS, COLS), F32),
    ]


def conclude_all(
    g, c, vector_in, previous_in, phased, told, got, heard, verdicts, out, made, coefficients, semaphores, make_told, wait_sends
):
    spread_sem, back_sem, verdict_sem, out_sem = semaphores
    n_grp, n_col = 8, lax.axis_size("col")
    mates = [(g + step) % n_grp for step in range(1, n_grp)]
    for to in mates:
        strip = phased.at[:, pl.ds(pl.multiple_of(to * ROWS, ROWS), ROWS), :]
        copy_out(strip, got.at[g], back_sem.at[0], back_sem.at[1], to, c).start()
    make_told()
    heard[c] = told[...]
    for step in range(1, n_col):
        to = (c + step) % n_col
        copy_out(told, heard.at[c], spread_sem.at[0], spread_sem.at[1], g, to).start()
    for pair in (0, 1):
        got[g, pair] = phased[pair, pl.ds(pl.multiple_of(g * ROWS, ROWS), ROWS), :]
    wait_sends()
    several = heard.at[pl.ds(0, n_col - 1)]
    others = verdicts.at[pl.ds(0, n_grp - 1)]
    wait_bytes(several, spread_sem.at[1])
    alpha, scale = conclude(heard[...].reshape(n_col, LANES), float(n_grp * ROWS * n_col * COLS))
    which = lax.broadcasted_iota(jnp.int32, (2, LANES), 0)
    verdicts[g] = jnp.where(which == 0, alpha, scale)
    for to in mates:
        copy_out(
            verdicts.at[g], verdicts.at[g], verdict_sem.at[0], verdict_sem.at[1], to, c
        ).start()
    wait_bytes(got.at[pl.ds(0, n_grp - 1)], back_sem.at[1])
    wait_bytes(got.at[pl.ds(0, n_grp - 1)], back_sem.at[0])
    wait_bytes(several, spread_sem.at[0])
    packed = [got[:, pair].reshape(n_grp * ROWS, LANES) for pair in (0, 1)]
    solved = reorder(jnp.concatenate(packed, axis=1), phase_matrix(False, True))
    target = solved.reshape(n_grp, ROWS, COLS) - previous_in[...]
    wait_bytes(others, verdict_sem.at[1])
    lane = lax.broadcasted_iota(jnp.int32, (2, LANES), 1)
    summary = jnp.zeros((2, LANES), F32)
    for probe in range(n_grp):
        pair = verdicts[probe]
        summary = jnp.where(lane == probe, pair, summary)
        rest = target[probe] - pair[0:1, 0:1] * vector_in[probe]
        made[probe] = rest * (1.0 / pair[1:2, 0:1])
    writing = pltpu.make_async_copy(made, out, out_sem.at[0])
    writing.start()
    coefficients[...] = summary[:, 0:n_grp]
    wait_bytes(others, verdict_sem.at[0])
    writing.wait()


def flat_levels():
    return jax.tree.flatten(level_scratch())


def spread_scratch():
    return [pltpu.VMEM((6, 2, 8 * ROWS, LANES), F32)] * 2 + [pltpu.VMEM((2, 8 * ROWS, LANES), F32)] * 2


VMEM = pl.BlockSpec(memory_space=pltpu.VMEM)
HBM = pl.BlockSpec(memory_space=pltpu.HBM)
LIMIT = 127 * 1024 * 512


def shape(*dims):
    return jax.ShapeDtypeStruct(dims, F32)


def step_kernel(conductance, shift, vector_hbm, previous_hbm, out, coefficients, *scratch):
    leaves, tree = flat_levels()
    count = len(leaves)
    levels_refs = jax.tree.unflatten(tree, scratch[:count])
    (own_out, halo_out, phased, before, vector_in, previous_in, own, halo, vector, vector_halo, previous, told, got, heard, verdicts, made, loads) = scratch[count : count + 17]
    semaphores = scratch[count + 17 :]
    g, c = lax.axis_index("grp"), lax.axis_index("col")
    n_col = lax.axis_size("col")
    loading = [
        pltpu.make_async_copy(conductance, own.at[g, pl.ds(0, 4)], loads.at[0]),
        pltpu.make_async_copy(shift, own.at[g, 4], loads.at[1]),
        pltpu.make_async_copy(vector_hbm, vector_in, loads.at[2]),
        pltpu.make_async_copy(previous_hbm, previous_in, loads.at[3]),
    ]
    for copy in loading:
        copy.start()
    barrier = pltpu.get_barrier_semaphore()
    partners = [((g + step) % 8, c) for step in range(1, 8)]
    partners += [(g, (c + step) % n_col) for step in range(1, n_col)]
    for grp, col in partners:
        pl.semaphore_signal(barrier, inc=1, device_id=(grp, col), device_id_type=MESH)
    for copy in loading:
        copy.wait()
    vector[g] = vector_in[g]
    previous[g] = previous_in[g]
    pl.semaphore_wait(barrier, len(partners))
    wait_vectors, wait_previous, wait_sends = gather(
        g, c, vector_in, previous_in, own, halo, vector, vector_halo, previous, semaphores[:7], lambda: spread_own(own, own_out)
    )
    compute(c, halo, vector, vector_halo, previous, levels_refs, own_out, halo_out, phased, before, (wait_vectors, wait_previous))
    conclude_all(g, c, vector_in, previous_in, phased, told, got, heard, verdicts, out, made, coefficients, semaphores[7:], lambda: make_told(told, phased, own_out, before), wait_sends)


def local(conductance, shift, vector_in, previous_in):
    n_col = lax.axis_size("col")
    leaves, _ = flat_levels()
    tile = (8, ROWS, COLS)
    return pl.pallas_call(
        step_kernel,
        out_shape=(shape(8, ROWS, COLS), shape(2, 8)),
        in_specs=[HBM] * 4,
        out_specs=(HBM, VMEM),
        scratch_shapes=leaves
        + spread_scratch()
        + [
            pltpu.VMEM(dims, F32)
            for dims in (
                tile,
                tile,
                (8, 5, ROWS, COLS),
                (8, 2, 5, ROWS, LANES),
                tile,
                (2, 8, ROWS, LANES),
                tile,
                (1, LANES),
            )
        ]
        + finish_scratch(n_col)
        + [pltpu.SemaphoreType.DMA((4,))]
        + gather_semaphores()
        + finish_semaphores(),
        compiler_params=pltpu.CompilerParams(
            collective_id=0, has_side_effects=True, vmem_limit_bytes=LIMIT
        ),
        name="lanczos_step",
    )(conductance, shift, vector_in, previous_in)


def solution(mesh):
    in_specs = (
        P(None, "grp", "col"),
        P("grp", "col"),
        P(None, "grp", "col"),
        P(None, "grp", "col"),
    )
    out_specs = (P(None, "grp", "col"), P())
    return jax.shard_map(local, mesh=mesh, in_specs=in_specs, out_specs=out_specs, check_vma=False)
```

```python
import jax
import jax.numpy as jnp
from jax import lax
from jax.experimental import pallas as pl
from jax.experimental.pallas import tpu as pltpu
from jax.sharding import PartitionSpec as P

F32 = jnp.float32
BF16 = jnp.bfloat16
EPSILON = 1e-06
LANES = 128
SUB = 8
WHOLE = 99
ROWS = 16
COLS = 256
MESH = pl.DeviceIdType.MESH

LEVEL_ROWS = (16, 8, 4, 2)
LEVEL_PHASES = (4, 2, 2, 2)
LEVEL_STRIDE = (1, 1, 2, 4)
AROUND = ((-1, 0), (1, 0), (0, -1), (0, 1), (-1, -1), (-1, 1), (1, -1), (1, 1))
PLACE = {offset: index for index, offset in enumerate(AROUND)}


def turn_lanes(x, by):
    return pltpu.roll(x, by % LANES, 1)


def turn_strips(x, by):
    return pltpu.roll(x, by % SUB, 0)


def rows(count, body, per):
    if per >= count:
        for index in range(count):
            body(index)
    else:

        def step(index, carry):
            for inner in range(per):
                body(index * per + inner)
            return carry

        lax.fori_loop(0, count // per, step, 0)


class Grid:
    def __init__(self, rows_, phases, stride):
        self.rows, self.phases, self.stride = rows_, phases, stride

    @property
    def ghosted(self):
        return (self.rows + 2, self.phases + 2, SUB, LANES)

    @property
    def bare(self):
        return (self.rows, self.phases, SUB, LANES)

    def put(self, ref, t, r, x):
        places = [(r + 1, x)]
        if r == 0:
            places.append((self.phases + 1, turn_lanes(x, -self.stride)))
        if r == self.phases - 1:
            places.append((0, turn_lanes(x, self.stride)))
        for place, y in places:
            ref[t + 1, place] = y
            if isinstance(t, int) and t == 0:
                ref[self.rows + 1, place] = turn_strips(y, -1)
            if isinstance(t, int) and t == self.rows - 1:
                ref[0, place] = turn_strips(y, 1)

    def wrap(self, ref, per, colour=None):
        if per >= self.rows:
            return
        for r in range(-1, self.phases + 1):
            if colour is None or (self.rows - 1 + r) % 2 == colour:
                ref[0, r + 1] = turn_strips(ref[self.rows, r + 1], 1)
            if colour is None or r % 2 == colour:
                ref[self.rows + 1, r + 1] = turn_strips(ref[1, r + 1], -1)


GRIDS = tuple(Grid(*sizes) for sizes in zip(LEVEL_ROWS, LEVEL_PHASES, LEVEL_STRIDE))
DENSE = tuple(Grid(g.rows // 2, g.phases // 2, g.stride) for g in GRIDS[:3])


def level_scratch():
    shapes = []
    for index, grid in enumerate(GRIDS):
        entry = {
            "own": (4,) + grid.ghosted,
            "dia": grid.bare,
            "inv": grid.bare,
            "near": (8,) + grid.bare,
            "right": grid.ghosted,
            "red0": grid.ghosted,
            "red1": grid.ghosted,
            "black0": grid.ghosted,
            "black1": grid.ghosted,
        }
        if index < 3:
            dense = DENSE[index]
            entry["weights"] = (8,) + dense.ghosted
            entry["passed"] = (6,) + dense.ghosted
            entry["kept"] = (5,) + dense.bare
            entry["residual"] = grid.ghosted
            entry["lifted"] = dense.ghosted
        shapes.append({name: pltpu.VMEM(shape, F32) for name, shape in entry.items()})
    return shapes


class Level:
    def __init__(self, index, refs, per):
        self.index, self.grid, self.per = index, GRIDS[index], per
        for name, ref in refs.items():
            setattr(self, name, ref)
        self.buffers = ((self.red0, self.red1), (self.black0, self.black1))
        self.now = [self.right, None]

    def pairs(self, body):
        rows(self.grid.rows // 2, body, self.per)

    def edge(self, a, b, t, r):
        own = self.own
        if (a, b) == (0, 1):
            return own[0, t + 1, r + 1]
        if (a, b) == (0, -1):
            return own[0, t + 1, r]
        if (a, b) == (1, 0):
            return own[1, t + 1, r + 1]
        if (a, b) == (-1, 0):
            return own[1, t, r + 1]
        if (a, b) == (1, 1):
            return own[2, t + 1, r + 1]
        if (a, b) == (-1, -1):
            return own[2, t, r]
        if (a, b) == (1, -1):
            return own[3, t + 1, r + 1]
        return own[3, t, r + 2]

    def scale_edges(self, t, r, edges, diagonal):
        inverse = 1.0 / diagonal
        self.dia[t, r] = diagonal
        self.inv[t, r] = inverse
        for index, edge in enumerate(edges):
            self.near[index, t, r] = edge * inverse

    def gathered(self, t, r, offsets, source, start=None):
        terms = [
            self.near[PLACE[a, b], t, r] * source(a, b)[t + 1 + a, r + 1 + b] for a, b in offsets
        ]
        if start is not None:
            terms.append(start)
        while len(terms) > 1:
            terms = [
                terms[i] + terms[i + 1] if i + 1 < len(terms) else terms[i]
                for i in range(0, len(terms), 2)
            ]
        return terms[0]

    def spare(self, colour):
        first, second = self.buffers[colour]
        return second if self.now[colour] is first else first

    def half_sweep(self, colour):
        grid, other, same = self.grid, self.now[1 - colour], self.now[colour]
        out = self.spare(colour)
        offsets = AROUND if same is not None else AROUND[:4]

        def body(u):
            for odd in (0, 1):
                for r in range(grid.phases):
                    if (odd + r) % 2 == colour:
                        t = 2 * u + odd
                        x = self.gathered(
                            t,
                            r,
                            offsets,
                            lambda a, b: other if (a + b) % 2 else same,
                            self.right[t + 1, r + 1],
                        )
                        grid.put(out, t, r, x)

        self.pairs(body)
        grid.wrap(out, self.per, colour)
        self.now[colour] = out

    def smooth_from_zero(self):
        self.now = [self.right, None]
        for colour in (1, 0, 1):
            self.half_sweep(colour)

    def smooth(self):
        for colour in (0, 1, 0, 1):
            self.half_sweep(colour)

    def find_residual(self):
        grid = self.grid

        def body(u):
            for odd in (0, 1):
                for r in range(grid.phases):
                    t = 2 * u + odd
                    colour = (odd + r) % 2
                    x = self.gathered(
                        t,
                        r,
                        AROUND,
                        lambda a, b: self.now[(colour + a + b) % 2],
                        self.right[t + 1, r + 1] - self.now[colour][t + 1, r + 1],
                    )
                    grid.put(self.residual, t, r, self.dia[t, r] * x)

        self.pairs(body)
        grid.wrap(self.residual, self.per)

    def find_weights(self):
        grid, dense, edge = self.grid, DENSE[self.index], self.edge

        def edges(i):
            for p in range(dense.phases):
                t, r = 2 * i + 1, 2 * p
                middle = 1.0 / (self.dia[t, r] - edge(0, -1, t, r) - edge(0, 1, t, r))
                up = edge(-1, 0, t, r) + edge(-1, -1, t, r) + edge(-1, 1, t, r)
                down = edge(1, 0, t, r) + edge(1, -1, t, r) + edge(1, 1, t, r)
                dense.put(self.weights.at[0], i, p, up * middle)
                dense.put(self.weights.at[1], i, p, down * middle)
                t, r = 2 * i, 2 * p + 1
                middle = 1.0 / (self.dia[t, r] - edge(-1, 0, t, r) - edge(1, 0, t, r))
                left = edge(0, -1, t, r) + edge(-1, -1, t, r) + edge(1, -1, t, r)
                right = edge(0, 1, t, r) + edge(-1, 1, t, r) + edge(1, 1, t, r)
                dense.put(self.weights.at[2], i, p, left * middle)
                dense.put(self.weights.at[3], i, p, right * middle)

        rows(dense.rows, edges, self.per)
        for index in range(4):
            dense.wrap(self.weights.at[index], self.per)
        w = self.weight

        def corners(i):
            for p in range(dense.phases):
                n = lambda a, b: self.near[PLACE[a, b], 2 * i + 1, 2 * p + 1]
                here = n(-1, -1) + n(0, -1) * w(0, i, p) + n(-1, 0) * w(2, i, p)
                down = n(1, -1) + n(0, -1) * w(1, i, p) + n(1, 0) * w(2, i + 1, p)
                right = n(-1, 1) + n(0, 1) * w(0, i, p + 1) + n(-1, 0) * w(3, i, p)
                both = n(1, 1) + n(0, 1) * w(1, i, p + 1) + n(1, 0) * w(3, i + 1, p)
                for index, x in enumerate((here, down, right, both)):
                    dense.put(self.weights.at[4 + index], i, p, x)

        rows(dense.rows, corners, self.per)
        for index in range(4, 8):
            dense.wrap(self.weights.at[index], self.per)

    def weight(self, index, i, p):
        return self.weights[index, i + 1, p + 1]

    def find_product(self):
        dense, w = DENSE[self.index], self.weight
        up, down, left, right, here, below, beside, both = range(8)

        def body(i):
            for p in range(dense.phases):
                t, r = 2 * i, 2 * p
                c = lambda a, b: self.edge(a, b, t, r)
                center = (
                    self.dia[t, r]
                    - c(-1, 0) * w(down, i - 1, p)
                    - c(1, 0) * w(up, i, p)
                    - c(0, -1) * w(right, i, p - 1)
                    - c(0, 1) * w(left, i, p)
                ) - (
                    c(-1, -1) * w(both, i - 1, p - 1)
                    + c(-1, 1) * w(below, i - 1, p)
                    + c(1, -1) * w(beside, i, p - 1)
                    + c(1, 1) * w(here, i, p)
                )
                east = -(
                    c(0, 1) * w(right, i, p)
                    + c(-1, 1) * w(both, i - 1, p)
                    + c(1, 1) * w(beside, i, p)
                )
                south = -(
                    c(1, 0) * w(down, i, p)
                    + c(1, 1) * w(below, i, p)
                    + c(1, -1) * w(both, i, p - 1)
                )
                south_east = -c(1, 1) * w(both, i, p)
                south_west = -c(1, -1) * w(below, i, p - 1)
                t, r = 2 * i + 1, 2 * p
                v = lambda a, b: self.edge(a, b, t, r)
                d = self.dia[t, r]
                v00 = (
                    d * w(up, i, p)
                    - v(-1, 0)
                    - v(-1, -1) * w(right, i, p - 1)
                    - v(-1, 1) * w(left, i, p)
                    - v(0, -1) * w(beside, i, p - 1)
                    - v(0, 1) * w(here, i, p)
                )
                v10 = (
                    d * w(down, i, p)
                    - v(1, 0)
                    - v(1, -1) * w(right, i + 1, p - 1)
                    - v(1, 1) * w(left, i + 1, p)
                    - v(0, -1) * w(both, i, p - 1)
                    - v(0, 1) * w(below, i, p)
                )
                v01 = -v(-1, 1) * w(right, i, p) - v(0, 1) * w(beside, i, p)
                v11 = -v(1, 1) * w(right, i + 1, p) - v(0, 1) * w(both, i, p)
                v1m = -v(1, -1) * w(left, i + 1, p - 1) - v(0, -1) * w(below, i, p - 1)
                t, r = 2 * i, 2 * p + 1
                h = lambda a, b: self.edge(a, b, t, r)
                d = self.dia[t, r]
                h00 = (
                    d * w(left, i, p)
                    - h(0, -1)
                    - h(-1, -1) * w(down, i - 1, p)
                    - h(1, -1) * w(up, i, p)
                    - h(-1, 0) * w(below, i - 1, p)
                    - h(1, 0) * w(here, i, p)
                )
                h01 = (
                    d * w(right, i, p)
                    - h(0, 1)
                    - h(-1, 1) * w(down, i - 1, p + 1)
                    - h(1, 1) * w(up, i, p + 1)
                    - h(-1, 0) * w(both, i - 1, p)
                    - h(1, 0) * w(beside, i, p)
                )
                h10 = -h(1, -1) * w(down, i, p) - h(1, 0) * w(below, i, p)
                h11 = -h(1, 1) * w(down, i, p + 1) - h(1, 0) * w(both, i, p)
                t, r = 2 * i + 1, 2 * p + 1
                k = lambda a, b: self.edge(a, b, t, r)
                d = self.dia[t, r]
                k00 = (
                    d * w(here, i, p)
                    - k(-1, -1)
                    - k(-1, 0) * w(left, i, p)
                    - k(0, -1) * w(up, i, p)
                )
                k10 = (
                    d * w(below, i, p)
                    - k(1, -1)
                    - k(1, 0) * w(left, i + 1, p)
                    - k(0, -1) * w(down, i, p)
                )
                k01 = (
                    d * w(beside, i, p)
                    - k(-1, 1)
                    - k(-1, 0) * w(right, i, p)
                    - k(0, 1) * w(up, i, p + 1)
                )
                k11 = (
                    d * w(both, i, p)
                    - k(1, 1)
                    - k(1, 0) * w(right, i + 1, p)
                    - k(0, 1) * w(down, i, p + 1)
                )
                wu, wd, wl, wr = (w(index, i, p) for index in (up, down, left, right))
                ch, cd, cr, cb = (w(index, i, p) for index in (here, below, beside, both))
                self.kept[0, i, p] = center + (wu * v00 + wl * h00) + ch * k00
                self.kept[1, i, p] = east + (wu * v01 + wl * h01) + ch * k01
                self.kept[2, i, p] = south + (wu * v10 + wl * h10) + ch * k10
                self.kept[3, i, p] = south_east + (wu * v11 + wl * h11) + ch * k11
                self.kept[4, i, p] = south_west + wu * v1m
                passed = (
                    wd * v10 + cd * k10,
                    wd * v11 + cd * k11,
                    wr * h01 + cr * k01,
                    wr * h11 + cr * k11,
                    wr * h10 + cr * k10,
                    cb * k11,
                )
                for index, x in enumerate(passed):
                    dense.put(self.passed.at[index], i, p, x)

        rows(dense.rows, body, self.per)
        for index in range(6):
            dense.wrap(self.passed.at[index], self.per)

    def give_product(self, coarse):
        dense, grid = DENSE[self.index], coarse.grid

        def body(i):
            for p in range(dense.phases):
                sent = lambda index, di, dp: self.passed[index, i + 1 + di, p + 1 + dp]
                center = (
                    self.kept[0, i, p] + sent(0, -1, 0) + sent(2, 0, -1) + sent(5, -1, -1)
                )
                entries = (
                    self.kept[1, i, p] + sent(1, -1, 0),
                    self.kept[2, i, p] + sent(3, 0, -1),
                    self.kept[3, i, p],
                    self.kept[4, i, p] + sent(4, 0, -1),
                )
                for phase, by in coarse.places(p, dense):
                    coarse.dia[i, phase] = center if by == 0 else turn_lanes(center, by)
                    for index, x in enumerate(entries):
                        x = -x if by == 0 else turn_lanes(-x, by)
                        grid.put(coarse.own.at[index], i, phase, x)

        rows(dense.rows, body, coarse.per)
        for index in range(4):
            grid.wrap(coarse.own.at[index], coarse.per)

        def scaled(u):
            for odd in (0, 1):
                for r in range(grid.phases):
                    t = 2 * u + odd
                    coarse.scale_edges(
                        t, r, [coarse.edge(a, b, t, r) for a, b in AROUND], coarse.dia[t, r]
                    )

        coarse.pairs(scaled)

    def places(self, p, dense):
        if dense.phases == self.grid.phases:
            return ((p, 0),)
        return ((0, 0), (1, -dense.stride))

    def restrict(self, coarse):
        dense, w, res = DENSE[self.index], self.weight, self.residual

        def body(i):
            for p in range(dense.phases):
                f = lambda a, b: res[2 * i + a + 1, 2 * p + b + 1]
                x = (
                    (f(0, 0) + w(0, i, p) * f(1, 0))
                    + (w(1, i - 1, p) * f(-1, 0) + w(2, i, p) * f(0, 1))
                ) + (
                    (w(3, i, p - 1) * f(0, -1) + w(4, i, p) * f(1, 1))
                    + (
                        (w(5, i - 1, p) * f(-1, 1) + w(6, i, p - 1) * f(1, -1))
                        + w(7, i - 1, p - 1) * f(-1, -1)
                    )
                )
                for phase, by in coarse.places(p, dense):
                    y = x if by == 0 else turn_lanes(x, by)
                    coarse.grid.put(coarse.right, i, phase, y * coarse.inv[i, phase])

        rows(dense.rows, body, coarse.per)
        coarse.grid.wrap(coarse.right, coarse.per)

    def prolong(self, coarse):
        grid, dense, w = self.grid, DENSE[self.index], self.weight
        if dense.phases == coarse.grid.phases:
            e = lambda i, p, parity: coarse.now[parity % 2][i + 1, p + 1]
        else:
            lane = lax.broadcasted_iota(jnp.int32, (SUB, LANES), 1)
            even = (lane & dense.stride) == 0
            for i in range(dense.rows):
                first = coarse.now[i % 2][i + 1, 1]
                second = turn_lanes(coarse.now[(i + 1) % 2][i + 1, 2], dense.stride)
                dense.put(self.lifted, i, 0, jnp.where(even, first, second))
            e = lambda i, p, parity: self.lifted[i + 1, p + 1]
        outs = [self.spare(0), self.spare(1)]

        def body(v):
            for odd in (0, 1):
                i = 2 * v + odd
                for p in range(dense.phases):
                    here = e(i, p, odd + p)
                    below = e(i + 1, p, odd + p + 1)
                    beside = e(i, p + 1, odd + p + 1)
                    both = e(i + 1, p + 1, odd + p)
                    changes = (
                        (0, 0, here),
                        (1, 0, w(0, i, p) * here + w(1, i, p) * below),
                        (0, 1, w(2, i, p) * here + w(3, i, p) * beside),
                        (
                            1,
                            1,
                            (w(4, i, p) * here + w(5, i, p) * below)
                            + (w(6, i, p) * beside + w(7, i, p) * both),
                        ),
                    )
                    for a, b, change in changes:
                        colour = (a + b) % 2
                        t, r = 2 * i + a, 2 * p + b
                        grid.put(outs[colour], t, r, self.now[colour][t + 1, r + 1] + change)

        rows(dense.rows // 2, body, self.per)
        for colour in (0, 1):
            grid.wrap(outs[colour], self.per, colour)
            self.now[colour] = outs[colour]


def reorder(x, order):
    high = x.astype(BF16)
    rest = x - high.astype(F32)
    middle = rest.astype(BF16)
    low = (rest - middle.astype(F32)).astype(BF16)
    moved = [jnp.dot(part, order, preferred_element_type=F32) for part in (low, middle, high)]
    return (moved[0] + moved[1]) + moved[2]


def phase_matrix(swap, inverse):
    natural = lax.broadcasted_iota(jnp.int32, (COLS, COLS), 1 if inverse else 0)
    phased = lax.broadcasted_iota(jnp.int32, (COLS, COLS), 0 if inverse else 1)
    phase = natural & 3
    if swap:
        phase = phase ^ 1
    target = phase * 64 + (natural >> 2)
    return jnp.where(phased == target, 1.0, 0.0).astype(BF16)


def reordered(x, order, out):
    moved = reorder(x, order)
    for pair in (0, 1):
        out[pair] = moved[:, pair * LANES : (pair + 1) * LANES]


def phases_of(field, t, own_out, halo_out, low):
    found = []
    for pair in (0, 1):
        window = (pl.ds(t, SUB, stride=ROWS), slice(None))
        own, halo = own_out.at[field, pair][window], halo_out.at[field, pair][window]
        found.append(jnp.where(low, own, halo))
        found.append(turn_lanes(jnp.where(low, halo, own), 64))
    return found


def fill_edges(level, col_place, own_out, halo_out):
    grid = level.grid
    lane = lax.broadcasted_iota(jnp.int32, (SUB, LANES), 1)
    strip = lax.broadcasted_iota(jnp.int32, (SUB, LANES), 0)
    low = lane < 64
    lane_start = col_place * 64 + jnp.where(lane < 96, lane, lane - LANES)
    count = lax.axis_size("col") * 64
    east_ok = jnp.where((lane_start == count - 1) | (lane_start == -1), 0.0, 1.0)
    west_ok = jnp.where((lane_start == 0) | (lane_start == count), 0.0, 1.0)
    last_strip = strip == SUB - 1

    def body(t):
        south_ok = jnp.where(last_strip & (t == ROWS - 1), 0.0, 1.0)
        for index in range(4):
            phases = phases_of(index, t, own_out, halo_out, low)
            for r, x in enumerate(phases):
                if index != 0:
                    x = x * south_ok
                if index in (0, 2) and r == 3:
                    x = x * east_ok
                if index == 3 and r == 0:
                    x = x * west_ok
                grid.put(level.own.at[index], t, r, x)

    rows(ROWS, body, level.per)
    for index in range(4):
        grid.wrap(level.own.at[index], level.per)

    def scaled(t):
        shift = phases_of(4, t, own_out, halo_out, low)
        for r in range(4):
            edges = [level.edge(a, b, t, r) for a, b in AROUND]
            pairs = [edges[i] + edges[i + 1] for i in range(0, 8, 2)]
            total = (pairs[0] + pairs[1]) + (pairs[2] + pairs[3])
            level.scale_edges(t, r, edges, shift[r] + total)

    rows(ROWS, scaled, level.per)


def fill_right(level, own_out, halo_out):
    grid = level.grid
    vector = level.residual
    lane = lax.broadcasted_iota(jnp.int32, (SUB, LANES), 1)
    low = lane < 64

    def body(t):
        for r, x in enumerate(phases_of(5, t, own_out, halo_out, low)):
            grid.put(vector, t, r, x)

    rows(ROWS, body, level.per)
    grid.wrap(vector, level.per)

    def image(u):
        for odd in (0, 1):
            for r in range(4):
                t = 2 * u + odd
                x = vector[t + 1, r + 1] - level.gathered(t, r, AROUND, lambda a, b: vector)
                grid.put(level.right, t, r, x)

    level.pairs(image)
    grid.wrap(level.right, level.per)


def setup(levels):
    for index in range(3):
        levels[index].find_weights()
        levels[index].find_product()
        levels[index].give_product(levels[index + 1])


def cycle(levels, index):
    level = levels[index]
    level.smooth_from_zero()
    if index == 3:
        return
    level.find_residual()
    level.restrict(levels[index + 1])
    cycle(levels, index + 1)
    level.prolong(levels[index + 1])
    level.smooth()


def total(x):
    return jnp.sum(jnp.sum(x, axis=0, keepdims=True), axis=1, keepdims=True)


def tell(solved, vector, previous):
    target = solved - previous
    length = total(vector * vector)
    projected = total(vector * target)
    near_alpha = jnp.where(length > 0.0, projected / jnp.where(length > 0.0, length, 1.0), 0.0)
    rest = target - near_alpha * vector
    squares = total(rest * rest)
    cross = total(vector * rest)
    inner = total(vector * solved)
    lane = lax.broadcasted_iota(jnp.int32, (1, LANES), 1)
    row = jnp.where(lane < 3, near_alpha, 0.0)
    for place, x in ((3, inner), (64, squares), (65, cross), (66, length)):
        row = jnp.where(lane == place, x, row)
    return row


def conclude(told, cells):
    lane = lax.broadcasted_iota(jnp.int32, told.shape, 1)
    alpha = total(jnp.where(lane == 3, told, 0.0)) / cells
    delta = alpha - told
    sums = pltpu.roll(told, 64, 1)
    weight = jnp.where(lane == 0, 1.0, jnp.where(lane == 1, -2.0 * delta, delta * delta))
    squares = total(jnp.where(lane < 3, weight * sums, 0.0)) / cells
    scale = jnp.sqrt(jnp.maximum(squares, 0.0) + EPSILON)
    return alpha, scale


def spread_own(own, own_out):
    order = phase_matrix(False, False)
    for field in range(5):
        reordered(own[:, field].reshape(SUB * ROWS, COLS), order, own_out.at[field])


def spread_halo(halo, halo_out):
    order = phase_matrix(True, False)
    for field in range(5):
        sides = [halo[:, side, field].reshape(SUB * ROWS, LANES) for side in (0, 1)]
        reordered(jnp.concatenate(sides, axis=1), order, halo_out.at[field])


def spread_vector(vector, vector_halo, own_out, halo_out):
    reordered(vector[...].reshape(SUB * ROWS, COLS), phase_matrix(False, False), own_out.at[5])
    sides = [vector_halo[side].reshape(SUB * ROWS, LANES) for side in (0, 1)]
    reordered(jnp.concatenate(sides, axis=1), phase_matrix(True, False), halo_out.at[5])


def pack_solved(level, phased):
    lane = lax.broadcasted_iota(jnp.int32, (SUB, LANES), 1)
    low = lane < 64
    for t in range(ROWS):
        x = [level.now[(t + r) % 2][t + 1, r + 1] for r in range(4)]
        for pair in (0, 1):
            y = jnp.where(low, x[2 * pair], turn_lanes(x[2 * pair + 1], 64))
            phased.at[pair][pl.ds(t, SUB, stride=ROWS), :] = y


def compute(
    col_place, halo, vector, vector_halo, previous, levels_refs, own_out, halo_out, phased, before, waits
):
    wait_vectors, wait_previous = waits
    levels = [Level(index, refs, WHOLE) for index, refs in enumerate(levels_refs)]
    spread_halo(halo, halo_out)
    fill_edges(levels[0], col_place, own_out, halo_out)
    setup(levels)
    wait_vectors()
    spread_vector(vector, vector_halo, own_out, halo_out)
    fill_right(levels[0], own_out, halo_out)
    wait_previous()
    reordered(previous[...].reshape(SUB * ROWS, COLS), phase_matrix(False, False), before)
    cycle(levels, 0)
    pack_solved(levels[0], phased)


def make_told(told, phased, own_out, before):
    flat = (2 * SUB * ROWS, LANES)
    told[...] = tell(phased[...].reshape(flat), own_out[5].reshape(flat), before[...].reshape(flat))


def copy_out(source, target, send, receive, grp, col):
    return pltpu.make_async_remote_copy(
        src_ref=source,
        dst_ref=target,
        send_sem=send,
        recv_sem=receive,
        device_id=(grp, col),
        device_id_type=MESH,
    )


def greet(partners):
    barrier = pltpu.get_barrier_semaphore()
    for grp, col in partners:
        pl.semaphore_signal(barrier, inc=1, device_id=(grp, col), device_id_type=MESH)
    pl.semaphore_wait(barrier, len(partners))


def gather_semaphores():
    dma = pltpu.SemaphoreType.DMA
    return [dma((4,)), dma((2,)), dma((2,)), dma((5,)), dma((2,)), dma((2,)), dma((2,))]


def wait_bytes(ref, semaphore):
    pltpu.make_async_copy(ref, ref, semaphore).wait()


def gather_sources(g, conductance, shift, vector_in, previous_in, own, vector, previous):
    own[g, 0:4] = conductance[...]
    own[g, 4] = shift[...]
    vector[g] = vector_in[g]
    previous[g] = previous_in[g]


def gather(g, c, vector_in, previous_in, own, halo, vector, vector_halo, previous, semaphores, while_waiting):
    along, of_vector, of_previous, beside, vector_beside, across, halo_across = semaphores
    n_grp, n_col = 8, lax.axis_size("col")
    y, core = g // 2, g % 2
    twin = y * 2 + 1 - core
    mates = [(g + step) % n_grp for step in range(1, n_grp)]
    east, west = (c + 1) % n_col, (c + n_col - 1) % n_col

    def place(back):
        return ((y + 4 - back) % 4) * 2 + core

    def send_sides(back):
        row = place(back)
        for side, to in ((1, east), (0, west)):
            copy_out(
                own.at[row, :, :, pl.ds(side * LANES, LANES)],
                halo.at[row, side],
                beside.at[4],
                beside.at[back],
                g,
                to,
            ).start()

    def pass_tile(back):
        row = place(back)
        copy_out(own.at[row], own.at[row], across.at[0], across.at[1], twin, c).start()

    def pass_sides(back):
        row = place(back)
        wait_bytes(halo.at[row], beside.at[back])
        copy_out(halo.at[row], halo.at[row], halo_across.at[0], halo_across.at[1], twin, c).start()

    def transpose(source, target, semaphore):
        for to in mates:
            copy_out(source.at[to], target.at[g], semaphore.at[0], semaphore.at[1], to, c).start()

    for step in (1, 3, 2):
        to = ((y + step) % 4) * 2 + core
        copy_out(own.at[g], own.at[g], along.at[0], along.at[step], to, c).start()
    send_sides(0)
    pass_tile(0)
    transpose(vector_in, vector, of_vector)
    for back in (1, 3, 2):
        row = place(back)
        wait_bytes(own.at[row], along.at[back])
        send_sides(back)
        pass_tile(back)
    wait_bytes(vector.at[pl.ds(0, n_grp - 1)], of_vector.at[1])
    for side, to in ((1, east), (0, west)):
        copy_out(
            vector.at[:, :, pl.ds(side * LANES, LANES)],
            vector_halo.at[side],
            vector_beside.at[0],
            vector_beside.at[1],
            g,
            to,
        ).start()
    transpose(previous_in, previous, of_previous)
    for back in (0, 1, 3):
        pass_sides(back)
    wait_bytes(own.at[pl.ds(0, 4)], across.at[1])
    while_waiting()
    pass_sides(2)
    wait_bytes(halo.at[pl.ds(0, 4)], halo_across.at[1])

    def wait_vectors():
        wait_bytes(vector_halo, vector_beside.at[1])

    def wait_previous():
        wait_bytes(previous.at[pl.ds(0, n_grp - 1)], of_previous.at[1])

    def wait_sends():
        wait_bytes(own.at[pl.ds(0, 3)], along.at[0])
        wait_bytes(halo.at[pl.ds(0, 4)], beside.at[4])
        wait_bytes(own.at[pl.ds(0, 4)], across.at[0])
        wait_bytes(halo.at[pl.ds(0, 4)], halo_across.at[0])
        wait_bytes(vector.at[pl.ds(0, n_grp - 1)], of_vector.at[0])
        wait_bytes(previous.at[pl.ds(0, n_grp - 1)], of_previous.at[0])
        wait_bytes(vector_halo, vector_beside.at[0])

    return wait_vectors, wait_previous, wait_sends


def finish_semaphores():
    dma = pltpu.SemaphoreType.DMA
    return [dma((2,)), dma((2,)), dma((2,))]


def finish_scratch(n_col):
    return [
        pltpu.VMEM((8, 2, ROWS, LANES), F32),
        pltpu.VMEM((n_col, 1, LANES), F32),
        pltpu.VMEM((8, 2, LANES), F32),
    ]


def conclude_all(
    g, c, vector_in, previous_in, phased, told, got, heard, verdicts, out, coefficients, semaphores, make_told, wait_sends
):
    spread_sem, back_sem, verdict_sem = semaphores
    n_grp, n_col = 8, lax.axis_size("col")
    mates = [(g + step) % n_grp for step in range(1, n_grp)]
    for to in mates:
        strip = phased.at[:, pl.ds(pl.multiple_of(to * ROWS, ROWS), ROWS), :]
        copy_out(strip, got.at[g], back_sem.at[0], back_sem.at[1], to, c).start()
    make_told()
    heard[c] = told[...]
    for step in range(1, n_col):
        to = (c + step) % n_col
        copy_out(told, heard.at[c], spread_sem.at[0], spread_sem.at[1], g, to).start()
    for pair in (0, 1):
        got[g, pair] = phased[pair, pl.ds(pl.multiple_of(g * ROWS, ROWS), ROWS), :]
    wait_sends()
    several = heard.at[pl.ds(0, n_col - 1)]
    others = verdicts.at[pl.ds(0, n_grp - 1)]
    wait_bytes(several, spread_sem.at[1])
    alpha, scale = conclude(heard[...].reshape(n_col, LANES), float(n_grp * ROWS * n_col * COLS))
    which = lax.broadcasted_iota(jnp.int32, (2, LANES), 0)
    verdicts[g] = jnp.where(which == 0, alpha, scale)
    for to in mates:
        copy_out(
            verdicts.at[g], verdicts.at[g], verdict_sem.at[0], verdict_sem.at[1], to, c
        ).start()
    wait_bytes(got.at[pl.ds(0, n_grp - 1)], back_sem.at[1])
    wait_bytes(got.at[pl.ds(0, n_grp - 1)], back_sem.at[0])
    wait_bytes(several, spread_sem.at[0])
    packed = [got[:, pair].reshape(n_grp * ROWS, LANES) for pair in (0, 1)]
    solved = reorder(jnp.concatenate(packed, axis=1), phase_matrix(False, True))
    target = solved.reshape(n_grp, ROWS, COLS) - previous_in[...]
    wait_bytes(others, verdict_sem.at[1])
    lane = lax.broadcasted_iota(jnp.int32, (2, LANES), 1)
    summary = jnp.zeros((2, LANES), F32)
    for probe in range(n_grp):
        pair = verdicts[probe]
        summary = jnp.where(lane == probe, pair, summary)
        rest = target[probe] - pair[0:1, 0:1] * vector_in[probe]
        made = rest * (1.0 / pair[1:2, 0:1])
        for half in (0, 1):
            out[2 * probe + half][...] = made[half * SUB : (half + 1) * SUB]
    coefficients[...] = summary[:, 0:n_grp]
    wait_bytes(others, verdict_sem.at[0])


def flat_levels():
    return jax.tree.flatten(level_scratch())


def spread_scratch():
    return [pltpu.VMEM((6, 2, 8 * ROWS, LANES), F32)] * 2 + [pltpu.VMEM((2, 8 * ROWS, LANES), F32)] * 2


VMEM = pl.BlockSpec(memory_space=pltpu.VMEM)
HBM = pl.BlockSpec(memory_space=pltpu.HBM)
LIMIT = 55091 * 1024


PIECES = 16


def shape(*dims):
    return jax.ShapeDtypeStruct(dims, F32)


def step_kernel(conductance, shift, vector_hbm, previous_hbm, *rest):
    out, coefficients, scratch = rest[:PIECES], rest[PIECES], rest[PIECES + 1 :]
    leaves, tree = flat_levels()
    count = len(leaves)
    levels_refs = jax.tree.unflatten(tree, scratch[:count])
    (own_out, halo_out, phased, before, vector_in, previous_in, own, halo, vector, vector_halo, previous, told, got, heard, verdicts, loads) = scratch[count : count + 16]
    semaphores = scratch[count + 16 :]
    g, c = lax.axis_index("grp"), lax.axis_index("col")
    n_col = lax.axis_size("col")
    loading = [
        pltpu.make_async_copy(conductance, own.at[g, pl.ds(0, 4)], loads.at[0]),
        pltpu.make_async_copy(shift, own.at[g, 4], loads.at[1]),
        pltpu.make_async_copy(vector_hbm, vector_in, loads.at[2]),
        pltpu.make_async_copy(previous_hbm, previous_in, loads.at[3]),
    ]
    for copy in loading:
        copy.start()
    barrier = pltpu.get_barrier_semaphore()
    partners = [((g + step) % 8, c) for step in range(1, 8)]
    partners += [(g, (c + step) % n_col) for step in range(1, n_col)]
    for grp, col in partners:
        pl.semaphore_signal(barrier, inc=1, device_id=(grp, col), device_id_type=MESH)
    for copy in loading:
        copy.wait()
    vector[g] = vector_in[g]
    previous[g] = previous_in[g]
    pl.semaphore_wait(barrier, len(partners))
    wait_vectors, wait_previous, wait_sends = gather(
        g, c, vector_in, previous_in, own, halo, vector, vector_halo, previous, semaphores[:7], lambda: spread_own(own, own_out)
    )
    compute(c, halo, vector, vector_halo, previous, levels_refs, own_out, halo_out, phased, before, (wait_vectors, wait_previous))
    conclude_all(g, c, vector_in, previous_in, phased, told, got, heard, verdicts, out, coefficients, semaphores[7:], lambda: make_told(told, phased, own_out, before), wait_sends)


def store_kernel(*refs):
    made, told = refs[:PIECES], refs[PIECES]
    out, coefficients, semaphores = refs[PIECES + 1 :]
    copies = [pltpu.make_async_copy(told, coefficients, semaphores.at[PIECES])]
    for piece in range(PIECES):
        strip = out.at[piece // 2, pl.ds(piece % 2 * SUB, SUB)]
        copies.append(pltpu.make_async_copy(made[piece], strip, semaphores.at[piece]))
    for copy in copies:
        copy.start()
    for copy in copies:
        copy.wait()


def local(conductance, shift, vector_in, previous_in):
    n_col = lax.axis_size("col")
    leaves, _ = flat_levels()
    tile = (8, ROWS, COLS)
    made = pl.pallas_call(
        step_kernel,
        out_shape=(shape(SUB, COLS),) * PIECES + (shape(2, 8),),
        in_specs=[HBM] * 4,
        out_specs=(VMEM,) * (PIECES + 1),
        scratch_shapes=leaves
        + spread_scratch()
        + [
            pltpu.VMEM(dims, F32)
            for dims in (
                tile,
                tile,
                (8, 5, ROWS, COLS),
                (8, 2, 5, ROWS, LANES),
                tile,
                (2, 8, ROWS, LANES),
                tile,
                (1, LANES),
            )
        ]
        + finish_scratch(n_col)
        + [pltpu.SemaphoreType.DMA((4,))]
        + gather_semaphores()
        + finish_semaphores(),
        compiler_params=pltpu.CompilerParams(
            collective_id=0, has_side_effects=True, vmem_limit_bytes=LIMIT
        ),
        name="lanczos_step",
    )(conductance, shift, vector_in, previous_in)
    return pl.pallas_call(
        store_kernel,
        out_shape=(shape(8, ROWS, COLS), shape(2, 8)),
        in_specs=[VMEM] * (PIECES + 1),
        out_specs=(HBM, HBM),
        scratch_shapes=[pltpu.SemaphoreType.DMA((PIECES + 1,))],
        compiler_params=pltpu.CompilerParams(vmem_limit_bytes=1024 * 1024),
        name="store",
    )(*made)


def solution(mesh):
    in_specs = (
        P(None, "grp", "col"),
        P("grp", "col"),
        P(None, "grp", "col"),
        P(None, "grp", "col"),
    )
    out_specs = (P(None, "grp", "col"), P())
    return jax.shard_map(local, mesh=mesh, in_specs=in_specs, out_specs=out_specs, check_vma=False)
```

```python
import jax
import jax.numpy as jnp
from jax import lax
from jax.experimental import pallas as pl
from jax.experimental.pallas import tpu as pltpu
from jax.sharding import PartitionSpec as P

F32 = jnp.float32
BF16 = jnp.bfloat16
EPSILON = 1e-06
LANES = 128
SUB = 8
WHOLE = 99
ROWS = 16
COLS = 256
MESH = pl.DeviceIdType.MESH

LEVEL_ROWS = (16, 8, 4, 2)
LEVEL_PHASES = (4, 2, 2, 2)
LEVEL_STRIDE = (1, 1, 2, 4)
AROUND = ((-1, 0), (1, 0), (0, -1), (0, 1), (-1, -1), (-1, 1), (1, -1), (1, 1))
PLACE = {offset: index for index, offset in enumerate(AROUND)}


def turn_lanes(x, by):
    return pltpu.roll(x, by % LANES, 1)


def turn_strips(x, by):
    return pltpu.roll(x, by % SUB, 0)


def rows(count, body, per):
    if per >= count:
        for index in range(count):
            body(index)
    else:

        def step(index, carry):
            for inner in range(per):
                body(index * per + inner)
            return carry

        lax.fori_loop(0, count // per, step, 0)


class Grid:
    def __init__(self, rows_, phases, stride):
        self.rows, self.phases, self.stride = rows_, phases, stride

    @property
    def ghosted(self):
        return (self.rows + 2, self.phases + 2, SUB, LANES)

    @property
    def bare(self):
        return (self.rows, self.phases, SUB, LANES)

    def put(self, ref, t, r, x):
        places = [(r + 1, x)]
        if r == 0:
            places.append((self.phases + 1, turn_lanes(x, -self.stride)))
        if r == self.phases - 1:
            places.append((0, turn_lanes(x, self.stride)))
        for place, y in places:
            ref[t + 1, place] = y
            if isinstance(t, int) and t == 0:
                ref[self.rows + 1, place] = turn_strips(y, -1)
            if isinstance(t, int) and t == self.rows - 1:
                ref[0, place] = turn_strips(y, 1)

    def wrap(self, ref, per, colour=None):
        if per >= self.rows:
            return
        for r in range(-1, self.phases + 1):
            if colour is None or (self.rows - 1 + r) % 2 == colour:
                ref[0, r + 1] = turn_strips(ref[self.rows, r + 1], 1)
            if colour is None or r % 2 == colour:
                ref[self.rows + 1, r + 1] = turn_strips(ref[1, r + 1], -1)


GRIDS = tuple(Grid(*sizes) for sizes in zip(LEVEL_ROWS, LEVEL_PHASES, LEVEL_STRIDE))
DENSE = tuple(Grid(g.rows // 2, g.phases // 2, g.stride) for g in GRIDS[:3])


def level_scratch():
    shapes = []
    for index, grid in enumerate(GRIDS):
        entry = {
            "own": (4,) + grid.ghosted,
            "dia": grid.bare,
            "inv": grid.bare,
            "near": (8,) + grid.bare,
            "right": grid.ghosted,
            "red0": grid.ghosted,
            "red1": grid.ghosted,
            "black0": grid.ghosted,
            "black1": grid.ghosted,
        }
        if index < 3:
            dense = DENSE[index]
            entry["weights"] = (8,) + dense.ghosted
            entry["passed"] = (6,) + dense.ghosted
            entry["kept"] = (5,) + dense.bare
            entry["residual"] = grid.ghosted
            entry["lifted"] = dense.ghosted
        shapes.append({name: pltpu.VMEM(shape, F32) for name, shape in entry.items()})
    return shapes


class Level:
    def __init__(self, index, refs, per):
        self.index, self.grid, self.per = index, GRIDS[index], per
        for name, ref in refs.items():
            setattr(self, name, ref)
        self.buffers = ((self.red0, self.red1), (self.black0, self.black1))
        self.now = [self.right, None]

    def pairs(self, body):
        rows(self.grid.rows // 2, body, self.per)

    def edge(self, a, b, t, r):
        own = self.own
        if (a, b) == (0, 1):
            return own[0, t + 1, r + 1]
        if (a, b) == (0, -1):
            return own[0, t + 1, r]
        if (a, b) == (1, 0):
            return own[1, t + 1, r + 1]
        if (a, b) == (-1, 0):
            return own[1, t, r + 1]
        if (a, b) == (1, 1):
            return own[2, t + 1, r + 1]
        if (a, b) == (-1, -1):
            return own[2, t, r]
        if (a, b) == (1, -1):
            return own[3, t + 1, r + 1]
        return own[3, t, r + 2]

    def scale_edges(self, t, r, edges, diagonal):
        inverse = 1.0 / diagonal
        self.dia[t, r] = diagonal
        self.inv[t, r] = inverse
        for index, edge in enumerate(edges):
            self.near[index, t, r] = edge * inverse

    def gathered(self, t, r, offsets, source, start=None):
        terms = [
            self.near[PLACE[a, b], t, r] * source(a, b)[t + 1 + a, r + 1 + b] for a, b in offsets
        ]
        if start is not None:
            terms.append(start)
        while len(terms) > 1:
            terms = [
                terms[i] + terms[i + 1] if i + 1 < len(terms) else terms[i]
                for i in range(0, len(terms), 2)
            ]
        return terms[0]

    def spare(self, colour):
        first, second = self.buffers[colour]
        return second if self.now[colour] is first else first

    def half_sweep(self, colour):
        grid, other, same = self.grid, self.now[1 - colour], self.now[colour]
        out = self.spare(colour)
        offsets = AROUND if same is not None else AROUND[:4]

        def body(u):
            for odd in (0, 1):
                for r in range(grid.phases):
                    if (odd + r) % 2 == colour:
                        t = 2 * u + odd
                        x = self.gathered(
                            t,
                            r,
                            offsets,
                            lambda a, b: other if (a + b) % 2 else same,
                            self.right[t + 1, r + 1],
                        )
                        grid.put(out, t, r, x)

        self.pairs(body)
        grid.wrap(out, self.per, colour)
        self.now[colour] = out

    def smooth_from_zero(self):
        self.now = [self.right, None]
        for colour in (1, 0, 1):
            self.half_sweep(colour)

    def smooth(self):
        for colour in (0, 1, 0, 1):
            self.half_sweep(colour)

    def find_residual(self):
        grid = self.grid

        def body(u):
            for odd in (0, 1):
                for r in range(grid.phases):
                    t = 2 * u + odd
                    colour = (odd + r) % 2
                    x = self.gathered(
                        t,
                        r,
                        AROUND,
                        lambda a, b: self.now[(colour + a + b) % 2],
                        self.right[t + 1, r + 1] - self.now[colour][t + 1, r + 1],
                    )
                    grid.put(self.residual, t, r, self.dia[t, r] * x)

        self.pairs(body)
        grid.wrap(self.residual, self.per)

    def find_weights(self):
        grid, dense, edge = self.grid, DENSE[self.index], self.edge

        def edges(i):
            for p in range(dense.phases):
                t, r = 2 * i + 1, 2 * p
                middle = 1.0 / (self.dia[t, r] - edge(0, -1, t, r) - edge(0, 1, t, r))
                up = edge(-1, 0, t, r) + edge(-1, -1, t, r) + edge(-1, 1, t, r)
                down = edge(1, 0, t, r) + edge(1, -1, t, r) + edge(1, 1, t, r)
                dense.put(self.weights.at[0], i, p, up * middle)
                dense.put(self.weights.at[1], i, p, down * middle)
                t, r = 2 * i, 2 * p + 1
                middle = 1.0 / (self.dia[t, r] - edge(-1, 0, t, r) - edge(1, 0, t, r))
                left = edge(0, -1, t, r) + edge(-1, -1, t, r) + edge(1, -1, t, r)
                right = edge(0, 1, t, r) + edge(-1, 1, t, r) + edge(1, 1, t, r)
                dense.put(self.weights.at[2], i, p, left * middle)
                dense.put(self.weights.at[3], i, p, right * middle)

        rows(dense.rows, edges, self.per)
        for index in range(4):
            dense.wrap(self.weights.at[index], self.per)
        w = self.weight

        def corners(i):
            for p in range(dense.phases):
                n = lambda a, b: self.near[PLACE[a, b], 2 * i + 1, 2 * p + 1]
                here = n(-1, -1) + n(0, -1) * w(0, i, p) + n(-1, 0) * w(2, i, p)
                down = n(1, -1) + n(0, -1) * w(1, i, p) + n(1, 0) * w(2, i + 1, p)
                right = n(-1, 1) + n(0, 1) * w(0, i, p + 1) + n(-1, 0) * w(3, i, p)
                both = n(1, 1) + n(0, 1) * w(1, i, p + 1) + n(1, 0) * w(3, i + 1, p)
                for index, x in enumerate((here, down, right, both)):
                    dense.put(self.weights.at[4 + index], i, p, x)

        rows(dense.rows, corners, self.per)
        for index in range(4, 8):
            dense.wrap(self.weights.at[index], self.per)

    def weight(self, index, i, p):
        return self.weights[index, i + 1, p + 1]

    def find_product(self):
        dense, w = DENSE[self.index], self.weight
        up, down, left, right, here, below, beside, both = range(8)

        def body(i):
            for p in range(dense.phases):
                t, r = 2 * i, 2 * p
                c = lambda a, b: self.edge(a, b, t, r)
                center = (
                    self.dia[t, r]
                    - c(-1, 0) * w(down, i - 1, p)
                    - c(1, 0) * w(up, i, p)
                    - c(0, -1) * w(right, i, p - 1)
                    - c(0, 1) * w(left, i, p)
                ) - (
                    c(-1, -1) * w(both, i - 1, p - 1)
                    + c(-1, 1) * w(below, i - 1, p)
                    + c(1, -1) * w(beside, i, p - 1)
                    + c(1, 1) * w(here, i, p)
                )
                east = -(
                    c(0, 1) * w(right, i, p)
                    + c(-1, 1) * w(both, i - 1, p)
                    + c(1, 1) * w(beside, i, p)
                )
                south = -(
                    c(1, 0) * w(down, i, p)
                    + c(1, 1) * w(below, i, p)
                    + c(1, -1) * w(both, i, p - 1)
                )
                south_east = -c(1, 1) * w(both, i, p)
                south_west = -c(1, -1) * w(below, i, p - 1)
                t, r = 2 * i + 1, 2 * p
                v = lambda a, b: self.edge(a, b, t, r)
                d = self.dia[t, r]
                v00 = (
                    d * w(up, i, p)
                    - v(-1, 0)
                    - v(-1, -1) * w(right, i, p - 1)
                    - v(-1, 1) * w(left, i, p)
                    - v(0, -1) * w(beside, i, p - 1)
                    - v(0, 1) * w(here, i, p)
                )
                v10 = (
                    d * w(down, i, p)
                    - v(1, 0)
                    - v(1, -1) * w(right, i + 1, p - 1)
                    - v(1, 1) * w(left, i + 1, p)
                    - v(0, -1) * w(both, i, p - 1)
                    - v(0, 1) * w(below, i, p)
                )
                v01 = -v(-1, 1) * w(right, i, p) - v(0, 1) * w(beside, i, p)
                v11 = -v(1, 1) * w(right, i + 1, p) - v(0, 1) * w(both, i, p)
                v1m = -v(1, -1) * w(left, i + 1, p - 1) - v(0, -1) * w(below, i, p - 1)
                t, r = 2 * i, 2 * p + 1
                h = lambda a, b: self.edge(a, b, t, r)
                d = self.dia[t, r]
                h00 = (
                    d * w(left, i, p)
                    - h(0, -1)
                    - h(-1, -1) * w(down, i - 1, p)
                    - h(1, -1) * w(up, i, p)
                    - h(-1, 0) * w(below, i - 1, p)
                    - h(1, 0) * w(here, i, p)
                )
                h01 = (
                    d * w(right, i, p)
                    - h(0, 1)
                    - h(-1, 1) * w(down, i - 1, p + 1)
                    - h(1, 1) * w(up, i, p + 1)
                    - h(-1, 0) * w(both, i - 1, p)
                    - h(1, 0) * w(beside, i, p)
                )
                h10 = -h(1, -1) * w(down, i, p) - h(1, 0) * w(below, i, p)
                h11 = -h(1, 1) * w(down, i, p + 1) - h(1, 0) * w(both, i, p)
                t, r = 2 * i + 1, 2 * p + 1
                k = lambda a, b: self.edge(a, b, t, r)
                d = self.dia[t, r]
                k00 = (
                    d * w(here, i, p)
                    - k(-1, -1)
                    - k(-1, 0) * w(left, i, p)
                    - k(0, -1) * w(up, i, p)
                )
                k10 = (
                    d * w(below, i, p)
                    - k(1, -1)
                    - k(1, 0) * w(left, i + 1, p)
                    - k(0, -1) * w(down, i, p)
                )
                k01 = (
                    d * w(beside, i, p)
                    - k(-1, 1)
                    - k(-1, 0) * w(right, i, p)
                    - k(0, 1) * w(up, i, p + 1)
                )
                k11 = (
                    d * w(both, i, p)
                    - k(1, 1)
                    - k(1, 0) * w(right, i + 1, p)
                    - k(0, 1) * w(down, i, p + 1)
                )
                wu, wd, wl, wr = (w(index, i, p) for index in (up, down, left, right))
                ch, cd, cr, cb = (w(index, i, p) for index in (here, below, beside, both))
                self.kept[0, i, p] = center + (wu * v00 + wl * h00) + ch * k00
                self.kept[1, i, p] = east + (wu * v01 + wl * h01) + ch * k01
                self.kept[2, i, p] = south + (wu * v10 + wl * h10) + ch * k10
                self.kept[3, i, p] = south_east + (wu * v11 + wl * h11) + ch * k11
                self.kept[4, i, p] = south_west + wu * v1m
                passed = (
                    wd * v10 + cd * k10,
                    wd * v11 + cd * k11,
                    wr * h01 + cr * k01,
                    wr * h11 + cr * k11,
                    wr * h10 + cr * k10,
                    cb * k11,
                )
                for index, x in enumerate(passed):
                    dense.put(self.passed.at[index], i, p, x)

        rows(dense.rows, body, self.per)
        for index in range(6):
            dense.wrap(self.passed.at[index], self.per)

    def give_product(self, coarse):
        dense, grid = DENSE[self.index], coarse.grid

        def body(i):
            for p in range(dense.phases):
                sent = lambda index, di, dp: self.passed[index, i + 1 + di, p + 1 + dp]
                center = (
                    self.kept[0, i, p] + sent(0, -1, 0) + sent(2, 0, -1) + sent(5, -1, -1)
                )
                entries = (
                    self.kept[1, i, p] + sent(1, -1, 0),
                    self.kept[2, i, p] + sent(3, 0, -1),
                    self.kept[3, i, p],
                    self.kept[4, i, p] + sent(4, 0, -1),
                )
                for phase, by in coarse.places(p, dense):
                    coarse.dia[i, phase] = center if by == 0 else turn_lanes(center, by)
                    for index, x in enumerate(entries):
                        x = -x if by == 0 else turn_lanes(-x, by)
                        grid.put(coarse.own.at[index], i, phase, x)

        rows(dense.rows, body, coarse.per)
        for index in range(4):
            grid.wrap(coarse.own.at[index], coarse.per)

        def scaled(u):
            for odd in (0, 1):
                for r in range(grid.phases):
                    t = 2 * u + odd
                    coarse.scale_edges(
                        t, r, [coarse.edge(a, b, t, r) for a, b in AROUND], coarse.dia[t, r]
                    )

        coarse.pairs(scaled)

    def places(self, p, dense):
        if dense.phases == self.grid.phases:
            return ((p, 0),)
        return ((0, 0), (1, -dense.stride))

    def restrict(self, coarse):
        dense, w, res = DENSE[self.index], self.weight, self.residual

        def body(i):
            for p in range(dense.phases):
                f = lambda a, b: res[2 * i + a + 1, 2 * p + b + 1]
                x = (
                    (f(0, 0) + w(0, i, p) * f(1, 0))
                    + (w(1, i - 1, p) * f(-1, 0) + w(2, i, p) * f(0, 1))
                ) + (
                    (w(3, i, p - 1) * f(0, -1) + w(4, i, p) * f(1, 1))
                    + (
                        (w(5, i - 1, p) * f(-1, 1) + w(6, i, p - 1) * f(1, -1))
                        + w(7, i - 1, p - 1) * f(-1, -1)
                    )
                )
                for phase, by in coarse.places(p, dense):
                    y = x if by == 0 else turn_lanes(x, by)
                    coarse.grid.put(coarse.right, i, phase, y * coarse.inv[i, phase])

        rows(dense.rows, body, coarse.per)
        coarse.grid.wrap(coarse.right, coarse.per)

    def prolong(self, coarse):
        grid, dense, w = self.grid, DENSE[self.index], self.weight
        if dense.phases == coarse.grid.phases:
            e = lambda i, p, parity: coarse.now[parity % 2][i + 1, p + 1]
        else:
            lane = lax.broadcasted_iota(jnp.int32, (SUB, LANES), 1)
            even = (lane & dense.stride) == 0
            for i in range(dense.rows):
                first = coarse.now[i % 2][i + 1, 1]
                second = turn_lanes(coarse.now[(i + 1) % 2][i + 1, 2], dense.stride)
                dense.put(self.lifted, i, 0, jnp.where(even, first, second))
            e = lambda i, p, parity: self.lifted[i + 1, p + 1]
        outs = [self.spare(0), self.spare(1)]

        def body(v):
            for odd in (0, 1):
                i = 2 * v + odd
                for p in range(dense.phases):
                    here = e(i, p, odd + p)
                    below = e(i + 1, p, odd + p + 1)
                    beside = e(i, p + 1, odd + p + 1)
                    both = e(i + 1, p + 1, odd + p)
                    changes = (
                        (0, 0, here),
                        (1, 0, w(0, i, p) * here + w(1, i, p) * below),
                        (0, 1, w(2, i, p) * here + w(3, i, p) * beside),
                        (
                            1,
                            1,
                            (w(4, i, p) * here + w(5, i, p) * below)
                            + (w(6, i, p) * beside + w(7, i, p) * both),
                        ),
                    )
                    for a, b, change in changes:
                        colour = (a + b) % 2
                        t, r = 2 * i + a, 2 * p + b
                        grid.put(outs[colour], t, r, self.now[colour][t + 1, r + 1] + change)

        rows(dense.rows // 2, body, self.per)
        for colour in (0, 1):
            grid.wrap(outs[colour], self.per, colour)
            self.now[colour] = outs[colour]


def reorder(x, order):
    high = x.astype(BF16)
    rest = x - high.astype(F32)
    middle = rest.astype(BF16)
    low = (rest - middle.astype(F32)).astype(BF16)
    moved = [jnp.dot(part, order, preferred_element_type=F32) for part in (low, middle, high)]
    return (moved[0] + moved[1]) + moved[2]


def phase_matrix(swap, inverse):
    natural = lax.broadcasted_iota(jnp.int32, (COLS, COLS), 1 if inverse else 0)
    phased = lax.broadcasted_iota(jnp.int32, (COLS, COLS), 0 if inverse else 1)
    phase = natural & 3
    if swap:
        phase = phase ^ 1
    target = phase * 64 + (natural >> 2)
    return jnp.where(phased == target, 1.0, 0.0).astype(BF16)


def reordered(x, order, out):
    moved = reorder(x, order)
    for pair in (0, 1):
        out[pair] = moved[:, pair * LANES : (pair + 1) * LANES]


def phases_of(field, t, own_out, halo_out, low):
    found = []
    for pair in (0, 1):
        window = (pl.ds(t, SUB, stride=ROWS), slice(None))
        own, halo = own_out.at[field, pair][window], halo_out.at[field, pair][window]
        found.append(jnp.where(low, own, halo))
        found.append(turn_lanes(jnp.where(low, halo, own), 64))
    return found


def fill_edges(level, col_place, own_out, halo_out):
    grid = level.grid
    lane = lax.broadcasted_iota(jnp.int32, (SUB, LANES), 1)
    strip = lax.broadcasted_iota(jnp.int32, (SUB, LANES), 0)
    low = lane < 64
    lane_start = col_place * 64 + jnp.where(lane < 96, lane, lane - LANES)
    count = lax.axis_size("col") * 64
    east_ok = jnp.where((lane_start == count - 1) | (lane_start == -1), 0.0, 1.0)
    west_ok = jnp.where((lane_start == 0) | (lane_start == count), 0.0, 1.0)
    last_strip = strip == SUB - 1

    def body(t):
        south_ok = jnp.where(last_strip & (t == ROWS - 1), 0.0, 1.0)
        for index in range(4):
            phases = phases_of(index, t, own_out, halo_out, low)
            for r, x in enumerate(phases):
                if index != 0:
                    x = x * south_ok
                if index in (0, 2) and r == 3:
                    x = x * east_ok
                if index == 3 and r == 0:
                    x = x * west_ok
                grid.put(level.own.at[index], t, r, x)

    rows(ROWS, body, level.per)
    for index in range(4):
        grid.wrap(level.own.at[index], level.per)

    def scaled(t):
        shift = phases_of(4, t, own_out, halo_out, low)
        for r in range(4):
            edges = [level.edge(a, b, t, r) for a, b in AROUND]
            pairs = [edges[i] + edges[i + 1] for i in range(0, 8, 2)]
            total = (pairs[0] + pairs[1]) + (pairs[2] + pairs[3])
            level.scale_edges(t, r, edges, shift[r] + total)

    rows(ROWS, scaled, level.per)


def fill_right(level, own_out, halo_out):
    grid = level.grid
    vector = level.residual
    lane = lax.broadcasted_iota(jnp.int32, (SUB, LANES), 1)
    low = lane < 64

    def body(t):
        for r, x in enumerate(phases_of(5, t, own_out, halo_out, low)):
            grid.put(vector, t, r, x)

    rows(ROWS, body, level.per)
    grid.wrap(vector, level.per)

    def image(u):
        for odd in (0, 1):
            for r in range(4):
                t = 2 * u + odd
                x = vector[t + 1, r + 1] - level.gathered(t, r, AROUND, lambda a, b: vector)
                grid.put(level.right, t, r, x)

    level.pairs(image)
    grid.wrap(level.right, level.per)


def setup(levels):
    for index in range(3):
        levels[index].find_weights()
        levels[index].find_product()
        levels[index].give_product(levels[index + 1])


def cycle(levels, index):
    level = levels[index]
    level.smooth_from_zero()
    if index == 3:
        return
    level.find_residual()
    level.restrict(levels[index + 1])
    cycle(levels, index + 1)
    level.prolong(levels[index + 1])
    level.smooth()


def total(x):
    return jnp.sum(jnp.sum(x, axis=0, keepdims=True), axis=1, keepdims=True)


def tell(solved, vector, previous):
    target = solved - previous
    length = total(vector * vector)
    projected = total(vector * target)
    near_alpha = jnp.where(length > 0.0, projected / jnp.where(length > 0.0, length, 1.0), 0.0)
    rest = target - near_alpha * vector
    squares = total(rest * rest)
    cross = total(vector * rest)
    inner = total(vector * solved)
    lane = lax.broadcasted_iota(jnp.int32, (1, LANES), 1)
    row = jnp.where(lane < 3, near_alpha, 0.0)
    for place, x in ((3, inner), (64, squares), (65, cross), (66, length)):
        row = jnp.where(lane == place, x, row)
    return row


def conclude(told, cells):
    lane = lax.broadcasted_iota(jnp.int32, told.shape, 1)
    alpha = total(jnp.where(lane == 3, told, 0.0)) / cells
    delta = alpha - told
    sums = pltpu.roll(told, 64, 1)
    weight = jnp.where(lane == 0, 1.0, jnp.where(lane == 1, -2.0 * delta, delta * delta))
    squares = total(jnp.where(lane < 3, weight * sums, 0.0)) / cells
    scale = jnp.sqrt(jnp.maximum(squares, 0.0) + EPSILON)
    return alpha, scale


def spread_own(own, own_out):
    order = phase_matrix(False, False)
    for field in range(5):
        reordered(own[:, field].reshape(SUB * ROWS, COLS), order, own_out.at[field])


def spread_halo(halo, halo_out):
    order = phase_matrix(True, False)
    for field in range(5):
        sides = [halo[:, side, field].reshape(SUB * ROWS, LANES) for side in (0, 1)]
        reordered(jnp.concatenate(sides, axis=1), order, halo_out.at[field])


def spread_vector(vector, vector_halo, own_out, halo_out):
    reordered(vector[...].reshape(SUB * ROWS, COLS), phase_matrix(False, False), own_out.at[5])
    sides = [vector_halo[side].reshape(SUB * ROWS, LANES) for side in (0, 1)]
    reordered(jnp.concatenate(sides, axis=1), phase_matrix(True, False), halo_out.at[5])


def pack_solved(level, phased):
    lane = lax.broadcasted_iota(jnp.int32, (SUB, LANES), 1)
    low = lane < 64
    for t in range(ROWS):
        x = [level.now[(t + r) % 2][t + 1, r + 1] for r in range(4)]
        for pair in (0, 1):
            y = jnp.where(low, x[2 * pair], turn_lanes(x[2 * pair + 1], 64))
            phased.at[pair][pl.ds(t, SUB, stride=ROWS), :] = y


def compute(
    col_place, halo, vector, vector_halo, previous, levels_refs, own_out, halo_out, phased, before, waits
):
    wait_vectors, wait_previous = waits
    levels = [Level(index, refs, WHOLE) for index, refs in enumerate(levels_refs)]
    spread_halo(halo, halo_out)
    fill_edges(levels[0], col_place, own_out, halo_out)
    setup(levels)
    wait_vectors()
    spread_vector(vector, vector_halo, own_out, halo_out)
    fill_right(levels[0], own_out, halo_out)
    wait_previous()
    reordered(previous[...].reshape(SUB * ROWS, COLS), phase_matrix(False, False), before)
    cycle(levels, 0)
    pack_solved(levels[0], phased)


def make_told(told, phased, own_out, before):
    flat = (2 * SUB * ROWS, LANES)
    told[...] = tell(phased[...].reshape(flat), own_out[5].reshape(flat), before[...].reshape(flat))


def copy_out(source, target, send, receive, grp, col):
    return pltpu.make_async_remote_copy(
        src_ref=source,
        dst_ref=target,
        send_sem=send,
        recv_sem=receive,
        device_id=(grp, col),
        device_id_type=MESH,
    )


def group_mates(g):
    y, core = g // 2, g % 2
    mates = [((y + step) % 4) * 2 + k for step in (2, 1, 3) for k in (core, 1 - core)]
    return mates + [y * 2 + 1 - core]


def column_mates(c):
    steps = [(dz, dx) for dz in range(8) for dx in range(4) if dz or dx]
    steps.sort(key=lambda step: -min(step[0], 8 - step[0]) - min(step[1], 4 - step[1]))
    return [((c // 4 + dz) % 8) * 4 + (c + dx) % 4 for dz, dx in steps]


def gather_semaphores():
    dma = pltpu.SemaphoreType.DMA
    return [dma((4,)), dma((2,)), dma((2,)), dma((5,)), dma((2,)), dma((2,)), dma((2,))]


def wait_bytes(ref, semaphore):
    pltpu.make_async_copy(ref, ref, semaphore).wait()


def gather_sources(g, conductance, shift, vector_in, previous_in, own, vector, previous):
    own[g, 0:4] = conductance[...]
    own[g, 4] = shift[...]
    vector[g] = vector_in[g]
    previous[g] = previous_in[g]


def gather(g, c, vector_in, previous_in, own, halo, vector, vector_halo, previous, semaphores, vectors_loaded, while_waiting):
    along, of_vector, of_previous, beside, vector_beside, across, halo_across = semaphores
    n_grp, n_col = 8, lax.axis_size("col")
    y, core = g // 2, g % 2
    twin = y * 2 + 1 - core
    mates = group_mates(g)
    east, west = (c + 1) % n_col, (c + n_col - 1) % n_col

    def place(back):
        return ((y + 4 - back) % 4) * 2 + core

    def send_sides(back):
        row = place(back)
        for side, to in ((1, east), (0, west)):
            copy_out(
                own.at[row, :, :, pl.ds(side * LANES, LANES)],
                halo.at[row, side],
                beside.at[4],
                beside.at[back],
                g,
                to,
            ).start()

    def pass_tile(back):
        row = place(back)
        copy_out(own.at[row], own.at[row], across.at[0], across.at[1], twin, c).start()

    def pass_sides(back):
        row = place(back)
        wait_bytes(halo.at[row], beside.at[back])
        copy_out(halo.at[row], halo.at[row], halo_across.at[0], halo_across.at[1], twin, c).start()

    def transpose(source, target, semaphore):
        for to in mates:
            copy_out(source.at[to], target.at[g], semaphore.at[0], semaphore.at[1], to, c).start()

    for step in (1, 3, 2):
        to = ((y + step) % 4) * 2 + core
        copy_out(own.at[g], own.at[g], along.at[0], along.at[step], to, c).start()
    send_sides(0)
    pass_tile(0)
    vectors_loaded()
    transpose(vector_in, vector, of_vector)
    for back in (1, 3, 2):
        row = place(back)
        if back == 2:
            pass_sides(0)
        wait_bytes(own.at[row], along.at[back])
        send_sides(back)
        pass_tile(back)
    wait_bytes(vector.at[pl.ds(0, n_grp - 1)], of_vector.at[1])
    for side, to in ((1, east), (0, west)):
        copy_out(
            vector.at[:, :, pl.ds(side * LANES, LANES)],
            vector_halo.at[side],
            vector_beside.at[0],
            vector_beside.at[1],
            g,
            to,
        ).start()
    transpose(previous_in, previous, of_previous)
    for back in (1, 3):
        pass_sides(back)
    wait_bytes(own.at[pl.ds(0, 4)], across.at[1])
    while_waiting()
    pass_sides(2)
    wait_bytes(halo.at[pl.ds(0, 4)], halo_across.at[1])

    def wait_vectors():
        wait_bytes(vector_halo, vector_beside.at[1])

    def wait_previous():
        wait_bytes(previous.at[pl.ds(0, n_grp - 1)], of_previous.at[1])

    def wait_sends():
        wait_bytes(own.at[pl.ds(0, 3)], along.at[0])
        wait_bytes(halo.at[pl.ds(0, 4)], beside.at[4])
        wait_bytes(own.at[pl.ds(0, 4)], across.at[0])
        wait_bytes(halo.at[pl.ds(0, 4)], halo_across.at[0])
        wait_bytes(vector.at[pl.ds(0, n_grp - 1)], of_vector.at[0])
        wait_bytes(previous.at[pl.ds(0, n_grp - 1)], of_previous.at[0])
        wait_bytes(vector_halo, vector_beside.at[0])

    return wait_vectors, wait_previous, wait_sends


def finish_semaphores():
    dma = pltpu.SemaphoreType.DMA
    return [dma((2,)), dma((2,)), dma((2,))]


def finish_scratch(n_col):
    return [
        pltpu.VMEM((8, 2, ROWS, LANES), F32),
        pltpu.VMEM((n_col, 1, LANES), F32),
        pltpu.VMEM((8, 2, LANES), F32),
    ]


def conclude_all(
    g, c, vector_in, previous_in, phased, told, got, heard, verdicts, out, coefficients, semaphores, make_told, wait_sends
):
    spread_sem, back_sem, verdict_sem = semaphores
    n_grp, n_col = 8, lax.axis_size("col")
    mates = group_mates(g)
    make_told()
    heard[c] = told[...]
    for to in column_mates(c):
        copy_out(told, heard.at[c], spread_sem.at[0], spread_sem.at[1], g, to).start()
    for to in mates:
        strip = phased.at[:, pl.ds(pl.multiple_of(to * ROWS, ROWS), ROWS), :]
        copy_out(strip, got.at[g], back_sem.at[0], back_sem.at[1], to, c).start()
    for pair in (0, 1):
        got[g, pair] = phased[pair, pl.ds(pl.multiple_of(g * ROWS, ROWS), ROWS), :]
    wait_sends()
    several = heard.at[pl.ds(0, n_col - 1)]
    others = verdicts.at[pl.ds(0, n_grp - 1)]
    wait_bytes(several, spread_sem.at[1])
    alpha, scale = conclude(heard[...].reshape(n_col, LANES), float(n_grp * ROWS * n_col * COLS))
    which = lax.broadcasted_iota(jnp.int32, (2, LANES), 0)
    verdicts[g] = jnp.where(which == 0, alpha, scale)
    for to in mates:
        copy_out(
            verdicts.at[g], verdicts.at[g], verdict_sem.at[0], verdict_sem.at[1], to, c
        ).start()
    wait_bytes(got.at[pl.ds(0, n_grp - 1)], back_sem.at[1])
    wait_bytes(got.at[pl.ds(0, n_grp - 1)], back_sem.at[0])
    wait_bytes(several, spread_sem.at[0])
    packed = [got[:, pair].reshape(n_grp * ROWS, LANES) for pair in (0, 1)]
    solved = reorder(jnp.concatenate(packed, axis=1), phase_matrix(False, True))
    target = solved.reshape(n_grp, ROWS, COLS) - previous_in[...]
    wait_bytes(others, verdict_sem.at[1])
    lane = lax.broadcasted_iota(jnp.int32, (2, LANES), 1)
    summary = jnp.zeros((2, LANES), F32)
    for probe in range(n_grp):
        pair = verdicts[probe]
        summary = jnp.where(lane == probe, pair, summary)
        rest = target[probe] - pair[0:1, 0:1] * vector_in[probe]
        made = rest * (1.0 / pair[1:2, 0:1])
        for half in (0, 1):
            out[2 * probe + half][...] = made[half * SUB : (half + 1) * SUB]
    coefficients[...] = summary[:, 0:n_grp]
    wait_bytes(others, verdict_sem.at[0])


def flat_levels():
    return jax.tree.flatten(level_scratch())


def spread_scratch():
    return [pltpu.VMEM((6, 2, 8 * ROWS, LANES), F32)] * 2 + [pltpu.VMEM((2, 8 * ROWS, LANES), F32)] * 2


VMEM = pl.BlockSpec(memory_space=pltpu.VMEM)
HBM = pl.BlockSpec(memory_space=pltpu.HBM)
LIMIT = 55091 * 1024


PIECES = 16


def shape(*dims):
    return jax.ShapeDtypeStruct(dims, F32)


def step_kernel(conductance, shift, vector_hbm, previous_hbm, *rest):
    out, coefficients, scratch = rest[:PIECES], rest[PIECES], rest[PIECES + 1 :]
    leaves, tree = flat_levels()
    count = len(leaves)
    levels_refs = jax.tree.unflatten(tree, scratch[:count])
    (own_out, halo_out, phased, before, vector_in, previous_in, own, halo, vector, vector_halo, previous, told, got, heard, verdicts, loads) = scratch[count : count + 16]
    semaphores = scratch[count + 16 :]
    g, c = lax.axis_index("grp"), lax.axis_index("col")
    n_col = lax.axis_size("col")
    loading = [
        pltpu.make_async_copy(conductance, own.at[g, pl.ds(0, 4)], loads.at[0]),
        pltpu.make_async_copy(shift, own.at[g, 4], loads.at[1]),
        pltpu.make_async_copy(vector_hbm, vector_in, loads.at[2]),
        pltpu.make_async_copy(previous_hbm, previous_in, loads.at[3]),
    ]
    for copy in loading:
        copy.start()
    barrier = pltpu.get_barrier_semaphore()
    partners = [(g, to) for to in column_mates(c)] + [(to, c) for to in group_mates(g)]
    for grp, col in partners:
        pl.semaphore_signal(barrier, inc=1, device_id=(grp, col), device_id_type=MESH)
    for copy in loading[:2]:
        copy.wait()

    def vectors_loaded():
        for copy in loading[2:]:
            copy.wait()
        vector[g] = vector_in[g]
        previous[g] = previous_in[g]

    pl.semaphore_wait(barrier, len(partners))
    wait_vectors, wait_previous, wait_sends = gather(
        g, c, vector_in, previous_in, own, halo, vector, vector_halo, previous, semaphores[:7], vectors_loaded, lambda: spread_own(own, own_out)
    )
    compute(c, halo, vector, vector_halo, previous, levels_refs, own_out, halo_out, phased, before, (wait_vectors, wait_previous))
    conclude_all(g, c, vector_in, previous_in, phased, told, got, heard, verdicts, out, coefficients, semaphores[7:], lambda: make_told(told, phased, own_out, before), wait_sends)


def store_kernel(*refs):
    made, told = refs[:PIECES], refs[PIECES]
    out, coefficients, semaphores = refs[PIECES + 1 :]
    copies = [pltpu.make_async_copy(told, coefficients, semaphores.at[PIECES])]
    for piece in range(PIECES):
        strip = out.at[piece // 2, pl.ds(piece % 2 * SUB, SUB)]
        copies.append(pltpu.make_async_copy(made[piece], strip, semaphores.at[piece]))
    for copy in copies:
        copy.start()
    for copy in copies:
        copy.wait()


def local(conductance, shift, vector_in, previous_in):
    n_col = lax.axis_size("col")
    leaves, _ = flat_levels()
    tile = (8, ROWS, COLS)
    made = pl.pallas_call(
        step_kernel,
        out_shape=(shape(SUB, COLS),) * PIECES + (shape(2, 8),),
        in_specs=[HBM] * 4,
        out_specs=(VMEM,) * (PIECES + 1),
        scratch_shapes=leaves
        + spread_scratch()
        + [
            pltpu.VMEM(dims, F32)
            for dims in (
                tile,
                tile,
                (8, 5, ROWS, COLS),
                (8, 2, 5, ROWS, LANES),
                tile,
                (2, 8, ROWS, LANES),
                tile,
                (1, LANES),
            )
        ]
        + finish_scratch(n_col)
        + [pltpu.SemaphoreType.DMA((4,))]
        + gather_semaphores()
        + finish_semaphores(),
        compiler_params=pltpu.CompilerParams(
            collective_id=0, has_side_effects=True, vmem_limit_bytes=LIMIT
        ),
        name="lanczos_step",
    )(conductance, shift, vector_in, previous_in)
    return pl.pallas_call(
        store_kernel,
        out_shape=(shape(8, ROWS, COLS), shape(2, 8)),
        in_specs=[VMEM] * (PIECES + 1),
        out_specs=(HBM, HBM),
        scratch_shapes=[pltpu.SemaphoreType.DMA((PIECES + 1,))],
        compiler_params=pltpu.CompilerParams(vmem_limit_bytes=1024 * 1024),
        name="store",
    )(*made)


def solution(mesh):
    in_specs = (
        P(None, "grp", "col"),
        P("grp", "col"),
        P(None, "grp", "col"),
        P(None, "grp", "col"),
    )
    out_specs = (P(None, "grp", "col"), P())
    return jax.shard_map(local, mesh=mesh, in_specs=in_specs, out_specs=out_specs, check_vma=False)
```

```python
import jax
import jax.numpy as jnp
from jax import lax
from jax.experimental import pallas as pl
from jax.experimental.pallas import tpu as pltpu
from jax.sharding import PartitionSpec as P

F32 = jnp.float32
BF16 = jnp.bfloat16
EPSILON = 1e-06
LANES = 128
SUB = 8
WHOLE = 99
ROWS = 16
COLS = 256
MESH = pl.DeviceIdType.MESH

LEVEL_ROWS = (16, 8, 4, 2)
LEVEL_PHASES = (4, 2, 2, 2)
LEVEL_STRIDE = (1, 1, 2, 4)
AROUND = ((-1, 0), (1, 0), (0, -1), (0, 1), (-1, -1), (-1, 1), (1, -1), (1, 1))
PLACE = {offset: index for index, offset in enumerate(AROUND)}


def turn_lanes(x, by):
    return pltpu.roll(x, by % LANES, 1)


def turn_strips(x, by):
    return pltpu.roll(x, by % SUB, 0)


def rows(count, body, per):
    if per >= count:
        for index in range(count):
            body(index)
    else:

        def step(index, carry):
            for inner in range(per):
                body(index * per + inner)
            return carry

        lax.fori_loop(0, count // per, step, 0)


class Grid:
    def __init__(self, rows_, phases, stride):
        self.rows, self.phases, self.stride = rows_, phases, stride

    @property
    def ghosted(self):
        return (self.rows + 2, self.phases + 2, SUB, LANES)

    @property
    def bare(self):
        return (self.rows, self.phases, SUB, LANES)

    def put(self, ref, t, r, x):
        places = [(r + 1, x)]
        if r == 0:
            places.append((self.phases + 1, turn_lanes(x, -self.stride)))
        if r == self.phases - 1:
            places.append((0, turn_lanes(x, self.stride)))
        for place, y in places:
            ref[t + 1, place] = y
            if isinstance(t, int) and t == 0:
                ref[self.rows + 1, place] = turn_strips(y, -1)
            if isinstance(t, int) and t == self.rows - 1:
                ref[0, place] = turn_strips(y, 1)

    def wrap(self, ref, per, colour=None):
        if per >= self.rows:
            return
        for r in range(-1, self.phases + 1):
            if colour is None or (self.rows - 1 + r) % 2 == colour:
                ref[0, r + 1] = turn_strips(ref[self.rows, r + 1], 1)
            if colour is None or r % 2 == colour:
                ref[self.rows + 1, r + 1] = turn_strips(ref[1, r + 1], -1)


GRIDS = tuple(Grid(*sizes) for sizes in zip(LEVEL_ROWS, LEVEL_PHASES, LEVEL_STRIDE))
DENSE = tuple(Grid(g.rows // 2, g.phases // 2, g.stride) for g in GRIDS[:3])


def level_scratch():
    shapes = []
    for index, grid in enumerate(GRIDS):
        entry = {
            "own": (4,) + grid.ghosted,
            "dia": grid.bare,
            "inv": grid.bare,
            "near": (8,) + grid.bare,
            "right": grid.ghosted,
            "red0": grid.ghosted,
            "red1": grid.ghosted,
            "black0": grid.ghosted,
            "black1": grid.ghosted,
        }
        if index < 3:
            dense = DENSE[index]
            entry["weights"] = (8,) + dense.ghosted
            entry["passed"] = (6,) + dense.ghosted
            entry["kept"] = (5,) + dense.bare
            entry["residual"] = grid.ghosted
            entry["lifted"] = dense.ghosted
        shapes.append({name: pltpu.VMEM(shape, F32) for name, shape in entry.items()})
    return shapes


class Level:
    def __init__(self, index, refs, per):
        self.index, self.grid, self.per = index, GRIDS[index], per
        for name, ref in refs.items():
            setattr(self, name, ref)
        self.buffers = ((self.red0, self.red1), (self.black0, self.black1))
        self.now = [self.right, None]

    def pairs(self, body):
        rows(self.grid.rows // 2, body, self.per)

    def edge(self, a, b, t, r):
        own = self.own
        if (a, b) == (0, 1):
            return own[0, t + 1, r + 1]
        if (a, b) == (0, -1):
            return own[0, t + 1, r]
        if (a, b) == (1, 0):
            return own[1, t + 1, r + 1]
        if (a, b) == (-1, 0):
            return own[1, t, r + 1]
        if (a, b) == (1, 1):
            return own[2, t + 1, r + 1]
        if (a, b) == (-1, -1):
            return own[2, t, r]
        if (a, b) == (1, -1):
            return own[3, t + 1, r + 1]
        return own[3, t, r + 2]

    def scale_edges(self, t, r, edges, diagonal):
        inverse = 1.0 / diagonal
        self.dia[t, r] = diagonal
        self.inv[t, r] = inverse
        for index, edge in enumerate(edges):
            self.near[index, t, r] = edge * inverse

    def gathered(self, t, r, offsets, source, start=None):
        terms = [
            self.near[PLACE[a, b], t, r] * source(a, b)[t + 1 + a, r + 1 + b] for a, b in offsets
        ]
        if start is not None:
            terms.append(start)
        while len(terms) > 1:
            terms = [
                terms[i] + terms[i + 1] if i + 1 < len(terms) else terms[i]
                for i in range(0, len(terms), 2)
            ]
        return terms[0]

    def spare(self, colour):
        first, second = self.buffers[colour]
        return second if self.now[colour] is first else first

    def half_sweep(self, colour):
        grid, other, same = self.grid, self.now[1 - colour], self.now[colour]
        out = self.spare(colour)
        offsets = AROUND if same is not None else AROUND[:4]

        def body(u):
            for odd in (0, 1):
                for r in range(grid.phases):
                    if (odd + r) % 2 == colour:
                        t = 2 * u + odd
                        x = self.gathered(
                            t,
                            r,
                            offsets,
                            lambda a, b: other if (a + b) % 2 else same,
                            self.right[t + 1, r + 1],
                        )
                        grid.put(out, t, r, x)

        self.pairs(body)
        grid.wrap(out, self.per, colour)
        self.now[colour] = out

    def smooth_from_zero(self):
        self.now = [self.right, None]
        for colour in (1, 0, 1):
            self.half_sweep(colour)

    def smooth(self):
        for colour in (0, 1, 0, 1):
            self.half_sweep(colour)

    def find_residual(self):
        grid = self.grid

        def body(u):
            for odd in (0, 1):
                for r in range(grid.phases):
                    t = 2 * u + odd
                    colour = (odd + r) % 2
                    x = self.gathered(
                        t,
                        r,
                        AROUND,
                        lambda a, b: self.now[(colour + a + b) % 2],
                        self.right[t + 1, r + 1] - self.now[colour][t + 1, r + 1],
                    )
                    grid.put(self.residual, t, r, self.dia[t, r] * x)

        self.pairs(body)
        grid.wrap(self.residual, self.per)

    def find_weights(self):
        grid, dense, edge = self.grid, DENSE[self.index], self.edge

        def edges(i):
            for p in range(dense.phases):
                t, r = 2 * i + 1, 2 * p
                middle = 1.0 / (self.dia[t, r] - edge(0, -1, t, r) - edge(0, 1, t, r))
                up = edge(-1, 0, t, r) + edge(-1, -1, t, r) + edge(-1, 1, t, r)
                down = edge(1, 0, t, r) + edge(1, -1, t, r) + edge(1, 1, t, r)
                dense.put(self.weights.at[0], i, p, up * middle)
                dense.put(self.weights.at[1], i, p, down * middle)
                t, r = 2 * i, 2 * p + 1
                middle = 1.0 / (self.dia[t, r] - edge(-1, 0, t, r) - edge(1, 0, t, r))
                left = edge(0, -1, t, r) + edge(-1, -1, t, r) + edge(1, -1, t, r)
                right = edge(0, 1, t, r) + edge(-1, 1, t, r) + edge(1, 1, t, r)
                dense.put(self.weights.at[2], i, p, left * middle)
                dense.put(self.weights.at[3], i, p, right * middle)

        rows(dense.rows, edges, self.per)
        for index in range(4):
            dense.wrap(self.weights.at[index], self.per)
        w = self.weight

        def corners(i):
            for p in range(dense.phases):
                n = lambda a, b: self.near[PLACE[a, b], 2 * i + 1, 2 * p + 1]
                here = n(-1, -1) + n(0, -1) * w(0, i, p) + n(-1, 0) * w(2, i, p)
                down = n(1, -1) + n(0, -1) * w(1, i, p) + n(1, 0) * w(2, i + 1, p)
                right = n(-1, 1) + n(0, 1) * w(0, i, p + 1) + n(-1, 0) * w(3, i, p)
                both = n(1, 1) + n(0, 1) * w(1, i, p + 1) + n(1, 0) * w(3, i + 1, p)
                for index, x in enumerate((here, down, right, both)):
                    dense.put(self.weights.at[4 + index], i, p, x)

        rows(dense.rows, corners, self.per)
        for index in range(4, 8):
            dense.wrap(self.weights.at[index], self.per)

    def weight(self, index, i, p):
        return self.weights[index, i + 1, p + 1]

    def find_product(self):
        dense, w = DENSE[self.index], self.weight
        up, down, left, right, here, below, beside, both = range(8)

        def body(i):
            for p in range(dense.phases):
                t, r = 2 * i, 2 * p
                c = lambda a, b: self.edge(a, b, t, r)
                center = (
                    self.dia[t, r]
                    - c(-1, 0) * w(down, i - 1, p)
                    - c(1, 0) * w(up, i, p)
                    - c(0, -1) * w(right, i, p - 1)
                    - c(0, 1) * w(left, i, p)
                ) - (
                    c(-1, -1) * w(both, i - 1, p - 1)
                    + c(-1, 1) * w(below, i - 1, p)
                    + c(1, -1) * w(beside, i, p - 1)
                    + c(1, 1) * w(here, i, p)
                )
                east = -(
                    c(0, 1) * w(right, i, p)
                    + c(-1, 1) * w(both, i - 1, p)
                    + c(1, 1) * w(beside, i, p)
                )
                south = -(
                    c(1, 0) * w(down, i, p)
                    + c(1, 1) * w(below, i, p)
                    + c(1, -1) * w(both, i, p - 1)
                )
                south_east = -c(1, 1) * w(both, i, p)
                south_west = -c(1, -1) * w(below, i, p - 1)
                t, r = 2 * i + 1, 2 * p
                v = lambda a, b: self.edge(a, b, t, r)
                d = self.dia[t, r]
                v00 = (
                    d * w(up, i, p)
                    - v(-1, 0)
                    - v(-1, -1) * w(right, i, p - 1)
                    - v(-1, 1) * w(left, i, p)
                    - v(0, -1) * w(beside, i, p - 1)
                    - v(0, 1) * w(here, i, p)
                )
                v10 = (
                    d * w(down, i, p)
                    - v(1, 0)
                    - v(1, -1) * w(right, i + 1, p - 1)
                    - v(1, 1) * w(left, i + 1, p)
                    - v(0, -1) * w(both, i, p - 1)
                    - v(0, 1) * w(below, i, p)
                )
                v01 = -v(-1, 1) * w(right, i, p) - v(0, 1) * w(beside, i, p)
                v11 = -v(1, 1) * w(right, i + 1, p) - v(0, 1) * w(both, i, p)
                v1m = -v(1, -1) * w(left, i + 1, p - 1) - v(0, -1) * w(below, i, p - 1)
                t, r = 2 * i, 2 * p + 1
                h = lambda a, b: self.edge(a, b, t, r)
                d = self.dia[t, r]
                h00 = (
                    d * w(left, i, p)
                    - h(0, -1)
                    - h(-1, -1) * w(down, i - 1, p)
                    - h(1, -1) * w(up, i, p)
                    - h(-1, 0) * w(below, i - 1, p)
                    - h(1, 0) * w(here, i, p)
                )
                h01 = (
                    d * w(right, i, p)
                    - h(0, 1)
                    - h(-1, 1) * w(down, i - 1, p + 1)
                    - h(1, 1) * w(up, i, p + 1)
                    - h(-1, 0) * w(both, i - 1, p)
                    - h(1, 0) * w(beside, i, p)
                )
                h10 = -h(1, -1) * w(down, i, p) - h(1, 0) * w(below, i, p)
                h11 = -h(1, 1) * w(down, i, p + 1) - h(1, 0) * w(both, i, p)
                t, r = 2 * i + 1, 2 * p + 1
                k = lambda a, b: self.edge(a, b, t, r)
                d = self.dia[t, r]
                k00 = (
                    d * w(here, i, p)
                    - k(-1, -1)
                    - k(-1, 0) * w(left, i, p)
                    - k(0, -1) * w(up, i, p)
                )
                k10 = (
                    d * w(below, i, p)
                    - k(1, -1)
                    - k(1, 0) * w(left, i + 1, p)
                    - k(0, -1) * w(down, i, p)
                )
                k01 = (
                    d * w(beside, i, p)
                    - k(-1, 1)
                    - k(-1, 0) * w(right, i, p)
                    - k(0, 1) * w(up, i, p + 1)
                )
                k11 = (
                    d * w(both, i, p)
                    - k(1, 1)
                    - k(1, 0) * w(right, i + 1, p)
                    - k(0, 1) * w(down, i, p + 1)
                )
                wu, wd, wl, wr = (w(index, i, p) for index in (up, down, left, right))
                ch, cd, cr, cb = (w(index, i, p) for index in (here, below, beside, both))
                self.kept[0, i, p] = center + (wu * v00 + wl * h00) + ch * k00
                self.kept[1, i, p] = east + (wu * v01 + wl * h01) + ch * k01
                self.kept[2, i, p] = south + (wu * v10 + wl * h10) + ch * k10
                self.kept[3, i, p] = south_east + (wu * v11 + wl * h11) + ch * k11
                self.kept[4, i, p] = south_west + wu * v1m
                passed = (
                    wd * v10 + cd * k10,
                    wd * v11 + cd * k11,
                    wr * h01 + cr * k01,
                    wr * h11 + cr * k11,
                    wr * h10 + cr * k10,
                    cb * k11,
                )
                for index, x in enumerate(passed):
                    dense.put(self.passed.at[index], i, p, x)

        rows(dense.rows, body, self.per)
        for index in range(6):
            dense.wrap(self.passed.at[index], self.per)

    def give_product(self, coarse):
        dense, grid = DENSE[self.index], coarse.grid

        def body(i):
            for p in range(dense.phases):
                sent = lambda index, di, dp: self.passed[index, i + 1 + di, p + 1 + dp]
                center = (
                    self.kept[0, i, p] + sent(0, -1, 0) + sent(2, 0, -1) + sent(5, -1, -1)
                )
                entries = (
                    self.kept[1, i, p] + sent(1, -1, 0),
                    self.kept[2, i, p] + sent(3, 0, -1),
                    self.kept[3, i, p],
                    self.kept[4, i, p] + sent(4, 0, -1),
                )
                for phase, by in coarse.places(p, dense):
                    coarse.dia[i, phase] = center if by == 0 else turn_lanes(center, by)
                    for index, x in enumerate(entries):
                        x = -x if by == 0 else turn_lanes(-x, by)
                        grid.put(coarse.own.at[index], i, phase, x)

        rows(dense.rows, body, coarse.per)
        for index in range(4):
            grid.wrap(coarse.own.at[index], coarse.per)

        def scaled(u):
            for odd in (0, 1):
                for r in range(grid.phases):
                    t = 2 * u + odd
                    coarse.scale_edges(
                        t, r, [coarse.edge(a, b, t, r) for a, b in AROUND], coarse.dia[t, r]
                    )

        coarse.pairs(scaled)

    def places(self, p, dense):
        if dense.phases == self.grid.phases:
            return ((p, 0),)
        return ((0, 0), (1, -dense.stride))

    def restrict(self, coarse):
        dense, w, res = DENSE[self.index], self.weight, self.residual

        def body(i):
            for p in range(dense.phases):
                f = lambda a, b: res[2 * i + a + 1, 2 * p + b + 1]
                x = (
                    (f(0, 0) + w(0, i, p) * f(1, 0))
                    + (w(1, i - 1, p) * f(-1, 0) + w(2, i, p) * f(0, 1))
                ) + (
                    (w(3, i, p - 1) * f(0, -1) + w(4, i, p) * f(1, 1))
                    + (
                        (w(5, i - 1, p) * f(-1, 1) + w(6, i, p - 1) * f(1, -1))
                        + w(7, i - 1, p - 1) * f(-1, -1)
                    )
                )
                for phase, by in coarse.places(p, dense):
                    y = x if by == 0 else turn_lanes(x, by)
                    coarse.grid.put(coarse.right, i, phase, y * coarse.inv[i, phase])

        rows(dense.rows, body, coarse.per)
        coarse.grid.wrap(coarse.right, coarse.per)

    def prolong(self, coarse):
        grid, dense, w = self.grid, DENSE[self.index], self.weight
        if dense.phases == coarse.grid.phases:
            e = lambda i, p, parity: coarse.now[parity % 2][i + 1, p + 1]
        else:
            lane = lax.broadcasted_iota(jnp.int32, (SUB, LANES), 1)
            even = (lane & dense.stride) == 0
            for i in range(dense.rows):
                first = coarse.now[i % 2][i + 1, 1]
                second = turn_lanes(coarse.now[(i + 1) % 2][i + 1, 2], dense.stride)
                dense.put(self.lifted, i, 0, jnp.where(even, first, second))
            e = lambda i, p, parity: self.lifted[i + 1, p + 1]
        outs = [self.spare(0), self.spare(1)]

        def body(v):
            for odd in (0, 1):
                i = 2 * v + odd
                for p in range(dense.phases):
                    here = e(i, p, odd + p)
                    below = e(i + 1, p, odd + p + 1)
                    beside = e(i, p + 1, odd + p + 1)
                    both = e(i + 1, p + 1, odd + p)
                    changes = (
                        (0, 0, here),
                        (1, 0, w(0, i, p) * here + w(1, i, p) * below),
                        (0, 1, w(2, i, p) * here + w(3, i, p) * beside),
                        (
                            1,
                            1,
                            (w(4, i, p) * here + w(5, i, p) * below)
                            + (w(6, i, p) * beside + w(7, i, p) * both),
                        ),
                    )
                    for a, b, change in changes:
                        colour = (a + b) % 2
                        t, r = 2 * i + a, 2 * p + b
                        grid.put(outs[colour], t, r, self.now[colour][t + 1, r + 1] + change)

        rows(dense.rows // 2, body, self.per)
        for colour in (0, 1):
            grid.wrap(outs[colour], self.per, colour)
            self.now[colour] = outs[colour]


def reorder(x, order):
    high = x.astype(BF16)
    rest = x - high.astype(F32)
    middle = rest.astype(BF16)
    low = (rest - middle.astype(F32)).astype(BF16)
    moved = [jnp.dot(part, order, preferred_element_type=F32) for part in (low, middle, high)]
    return (moved[0] + moved[1]) + moved[2]


def phase_matrix(swap, inverse):
    natural = lax.broadcasted_iota(jnp.int32, (COLS, COLS), 1 if inverse else 0)
    phased = lax.broadcasted_iota(jnp.int32, (COLS, COLS), 0 if inverse else 1)
    phase = natural & 3
    if swap:
        phase = phase ^ 1
    target = phase * 64 + (natural >> 2)
    return jnp.where(phased == target, 1.0, 0.0).astype(BF16)


def reordered(x, order, out):
    moved = reorder(x, order)
    for pair in (0, 1):
        out[pair] = moved[:, pair * LANES : (pair + 1) * LANES]


def phases_of(field, t, own_out, halo_out, low):
    found = []
    for pair in (0, 1):
        window = (pl.ds(t, SUB, stride=ROWS), slice(None))
        own, halo = own_out.at[field, pair][window], halo_out.at[field, pair][window]
        found.append(jnp.where(low, own, halo))
        found.append(turn_lanes(jnp.where(low, halo, own), 64))
    return found


def fill_edges(level, col_place, own_out, halo_out):
    grid = level.grid
    lane = lax.broadcasted_iota(jnp.int32, (SUB, LANES), 1)
    strip = lax.broadcasted_iota(jnp.int32, (SUB, LANES), 0)
    low = lane < 64
    lane_start = col_place * 64 + jnp.where(lane < 96, lane, lane - LANES)
    count = lax.axis_size("col") * 64
    east_ok = jnp.where((lane_start == count - 1) | (lane_start == -1), 0.0, 1.0)
    west_ok = jnp.where((lane_start == 0) | (lane_start == count), 0.0, 1.0)
    last_strip = strip == SUB - 1

    def body(t):
        south_ok = jnp.where(last_strip & (t == ROWS - 1), 0.0, 1.0)
        for index in range(4):
            phases = phases_of(index, t, own_out, halo_out, low)
            for r, x in enumerate(phases):
                if index != 0:
                    x = x * south_ok
                if index in (0, 2) and r == 3:
                    x = x * east_ok
                if index == 3 and r == 0:
                    x = x * west_ok
                grid.put(level.own.at[index], t, r, x)

    rows(ROWS, body, level.per)
    for index in range(4):
        grid.wrap(level.own.at[index], level.per)

    def scaled(t):
        shift = phases_of(4, t, own_out, halo_out, low)
        for r in range(4):
            edges = [level.edge(a, b, t, r) for a, b in AROUND]
            pairs = [edges[i] + edges[i + 1] for i in range(0, 8, 2)]
            total = (pairs[0] + pairs[1]) + (pairs[2] + pairs[3])
            level.scale_edges(t, r, edges, shift[r] + total)

    rows(ROWS, scaled, level.per)


def fill_right(level, own_out, halo_out):
    grid = level.grid
    vector = level.residual
    lane = lax.broadcasted_iota(jnp.int32, (SUB, LANES), 1)
    low = lane < 64

    def body(t):
        for r, x in enumerate(phases_of(5, t, own_out, halo_out, low)):
            grid.put(vector, t, r, x)

    rows(ROWS, body, level.per)
    grid.wrap(vector, level.per)

    def image(u):
        for odd in (0, 1):
            for r in range(4):
                t = 2 * u + odd
                x = vector[t + 1, r + 1] - level.gathered(t, r, AROUND, lambda a, b: vector)
                grid.put(level.right, t, r, x)

    level.pairs(image)
    grid.wrap(level.right, level.per)


def setup(levels):
    for index in range(3):
        levels[index].find_weights()
        levels[index].find_product()
        levels[index].give_product(levels[index + 1])


def cycle(levels, index):
    level = levels[index]
    level.smooth_from_zero()
    if index == 3:
        return
    level.find_residual()
    level.restrict(levels[index + 1])
    cycle(levels, index + 1)
    level.prolong(levels[index + 1])
    level.smooth()


def total(x):
    while x.shape[0] > SUB:
        half = x.shape[0] // 2
        x = x[:half] + x[half:]
    return jnp.sum(jnp.sum(x, axis=0, keepdims=True), axis=1, keepdims=True)


def tell(solved, vector, previous):
    target = solved - previous
    length = total(vector * vector)
    projected = total(vector * target)
    near_alpha = jnp.where(length > 0.0, projected / jnp.where(length > 0.0, length, 1.0), 0.0)
    rest = target - near_alpha * vector
    squares = total(rest * rest)
    cross = total(vector * rest)
    inner = total(vector * solved)
    lane = lax.broadcasted_iota(jnp.int32, (1, LANES), 1)
    row = jnp.where(lane < 3, near_alpha, 0.0)
    for place, x in ((3, inner), (64, squares), (65, cross), (66, length)):
        row = jnp.where(lane == place, x, row)
    return row


def conclude(told, cells):
    lane = lax.broadcasted_iota(jnp.int32, told.shape, 1)
    alpha = total(jnp.where(lane == 3, told, 0.0)) / cells
    delta = alpha - told
    sums = pltpu.roll(told, 64, 1)
    weight = jnp.where(lane == 0, 1.0, jnp.where(lane == 1, -2.0 * delta, delta * delta))
    squares = total(jnp.where(lane < 3, weight * sums, 0.0)) / cells
    scale = jnp.sqrt(jnp.maximum(squares, 0.0) + EPSILON)
    return alpha, scale


def spread_own(own, own_out):
    order = phase_matrix(False, False)
    for field in range(5):
        reordered(own[:, field].reshape(SUB * ROWS, COLS), order, own_out.at[field])


def spread_halo(halo, halo_out):
    order = phase_matrix(True, False)
    for field in range(5):
        sides = [halo[:, side, field].reshape(SUB * ROWS, LANES) for side in (0, 1)]
        reordered(jnp.concatenate(sides, axis=1), order, halo_out.at[field])


def spread_vector(vector, vector_halo, own_out, halo_out):
    reordered(vector[...].reshape(SUB * ROWS, COLS), phase_matrix(False, False), own_out.at[5])
    sides = [vector_halo[side].reshape(SUB * ROWS, LANES) for side in (0, 1)]
    reordered(jnp.concatenate(sides, axis=1), phase_matrix(True, False), halo_out.at[5])


def pack_solved(level, phased):
    lane = lax.broadcasted_iota(jnp.int32, (SUB, LANES), 1)
    low = lane < 64
    for t in range(ROWS):
        x = [level.now[(t + r) % 2][t + 1, r + 1] for r in range(4)]
        for pair in (0, 1):
            y = jnp.where(low, x[2 * pair], turn_lanes(x[2 * pair + 1], 64))
            phased.at[pair][pl.ds(t, SUB, stride=ROWS), :] = y


def compute(
    col_place, halo, vector, vector_halo, previous, levels_refs, own_out, halo_out, phased, before, waits
):
    wait_vectors, wait_previous = waits
    levels = [Level(index, refs, WHOLE) for index, refs in enumerate(levels_refs)]
    spread_halo(halo, halo_out)
    fill_edges(levels[0], col_place, own_out, halo_out)
    setup(levels)
    wait_vectors()
    spread_vector(vector, vector_halo, own_out, halo_out)
    fill_right(levels[0], own_out, halo_out)
    wait_previous()
    reordered(previous[...].reshape(SUB * ROWS, COLS), phase_matrix(False, False), before)
    cycle(levels, 0)
    pack_solved(levels[0], phased)


def make_told(told, phased, own_out, before):
    flat = (2 * SUB * ROWS, LANES)
    told[...] = tell(phased[...].reshape(flat), own_out[5].reshape(flat), before[...].reshape(flat))


def copy_out(source, target, send, receive, grp, col):
    return pltpu.make_async_remote_copy(
        src_ref=source,
        dst_ref=target,
        send_sem=send,
        recv_sem=receive,
        device_id=(grp, col),
        device_id_type=MESH,
    )


def group_mates(g):
    y, core = g // 2, g % 2
    mates = [((y + step) % 4) * 2 + k for step in (2, 1, 3) for k in (core, 1 - core)]
    return mates + [y * 2 + 1 - core]


def column_mates(c):
    steps = [(dz, dx) for dz in range(8) for dx in range(4) if dz or dx]
    steps.sort(key=lambda step: -min(step[0], 8 - step[0]) - min(step[1], 4 - step[1]))
    return [((c // 4 + dz) % 8) * 4 + (c + dx) % 4 for dz, dx in steps]


def gather_semaphores():
    dma = pltpu.SemaphoreType.DMA
    return [dma((4,)), dma((2,)), dma((2,)), dma((5,)), dma((2,)), dma((2,)), dma((2,))]


def wait_bytes(ref, semaphore):
    pltpu.make_async_copy(ref, ref, semaphore).wait()


def gather_sources(g, conductance, shift, vector_in, previous_in, own, vector, previous):
    own[g, 0:4] = conductance[...]
    own[g, 4] = shift[...]
    vector[g] = vector_in[g]
    previous[g] = previous_in[g]


def gather(g, c, vector_in, previous_in, own, halo, vector, vector_halo, previous, semaphores, vectors_loaded, while_waiting):
    along, of_vector, of_previous, beside, vector_beside, across, halo_across = semaphores
    n_grp, n_col = 8, lax.axis_size("col")
    y, core = g // 2, g % 2
    twin = y * 2 + 1 - core
    mates = group_mates(g)
    east, west = (c + 1) % n_col, (c + n_col - 1) % n_col

    def place(back):
        return ((y + 4 - back) % 4) * 2 + core

    def send_sides(back):
        row = place(back)
        for side, to in ((1, east), (0, west)):
            copy_out(
                own.at[row, :, :, pl.ds(side * LANES, LANES)],
                halo.at[row, side],
                beside.at[4],
                beside.at[back],
                g,
                to,
            ).start()

    def pass_tile(back):
        row = place(back)
        copy_out(own.at[row], own.at[row], across.at[0], across.at[1], twin, c).start()

    def pass_sides(back):
        row = place(back)
        wait_bytes(halo.at[row], beside.at[back])
        copy_out(halo.at[row], halo.at[row], halo_across.at[0], halo_across.at[1], twin, c).start()

    def transpose(source, target, semaphore):
        for to in mates:
            copy_out(source.at[to], target.at[g], semaphore.at[0], semaphore.at[1], to, c).start()

    for step in (1, 3, 2):
        to = ((y + step) % 4) * 2 + core
        copy_out(own.at[g], own.at[g], along.at[0], along.at[step], to, c).start()
    send_sides(0)
    pass_tile(0)
    vectors_loaded()
    transpose(vector_in, vector, of_vector)
    for back in (1, 3, 2):
        row = place(back)
        if back == 2:
            pass_sides(0)
        wait_bytes(own.at[row], along.at[back])
        send_sides(back)
        pass_tile(back)
    wait_bytes(vector.at[pl.ds(0, n_grp - 1)], of_vector.at[1])
    for side, to in ((1, east), (0, west)):
        copy_out(
            vector.at[:, :, pl.ds(side * LANES, LANES)],
            vector_halo.at[side],
            vector_beside.at[0],
            vector_beside.at[1],
            g,
            to,
        ).start()
    transpose(previous_in, previous, of_previous)
    for back in (1, 3):
        pass_sides(back)
    wait_bytes(own.at[pl.ds(0, 4)], across.at[1])
    while_waiting()
    pass_sides(2)
    wait_bytes(halo.at[pl.ds(0, 4)], halo_across.at[1])

    def wait_vectors():
        wait_bytes(vector_halo, vector_beside.at[1])

    def wait_previous():
        wait_bytes(previous.at[pl.ds(0, n_grp - 1)], of_previous.at[1])

    def wait_sends():
        wait_bytes(own.at[pl.ds(0, 3)], along.at[0])
        wait_bytes(halo.at[pl.ds(0, 4)], beside.at[4])
        wait_bytes(own.at[pl.ds(0, 4)], across.at[0])
        wait_bytes(halo.at[pl.ds(0, 4)], halo_across.at[0])
        wait_bytes(vector.at[pl.ds(0, n_grp - 1)], of_vector.at[0])
        wait_bytes(previous.at[pl.ds(0, n_grp - 1)], of_previous.at[0])
        wait_bytes(vector_halo, vector_beside.at[0])

    return wait_vectors, wait_previous, wait_sends


def finish_semaphores():
    dma = pltpu.SemaphoreType.DMA
    return [dma((2,)), dma((2,)), dma((2,))]


def finish_scratch(n_col):
    return [
        pltpu.VMEM((8, 2, ROWS, LANES), F32),
        pltpu.VMEM((n_col, 1, LANES), F32),
        pltpu.VMEM((8, 2, LANES), F32),
    ]


def conclude_all(
    g, c, vector_in, previous_in, phased, told, got, heard, verdicts, out, coefficients, semaphores, make_told, wait_sends
):
    spread_sem, back_sem, verdict_sem = semaphores
    n_grp, n_col = 8, lax.axis_size("col")
    mates = group_mates(g)
    make_told()
    heard[c] = told[...]
    for to in column_mates(c):
        copy_out(told, heard.at[c], spread_sem.at[0], spread_sem.at[1], g, to).start()
    for to in mates:
        strip = phased.at[:, pl.ds(pl.multiple_of(to * ROWS, ROWS), ROWS), :]
        copy_out(strip, got.at[g], back_sem.at[0], back_sem.at[1], to, c).start()
    for pair in (0, 1):
        got[g, pair] = phased[pair, pl.ds(pl.multiple_of(g * ROWS, ROWS), ROWS), :]
    wait_sends()
    several = heard.at[pl.ds(0, n_col - 1)]
    others = verdicts.at[pl.ds(0, n_grp - 1)]
    wait_bytes(several, spread_sem.at[1])
    alpha, scale = conclude(heard[...].reshape(n_col, LANES), float(n_grp * ROWS * n_col * COLS))
    which = lax.broadcasted_iota(jnp.int32, (2, LANES), 0)
    verdicts[g] = jnp.where(which == 0, alpha, scale)
    for to in mates:
        copy_out(
            verdicts.at[g], verdicts.at[g], verdict_sem.at[0], verdict_sem.at[1], to, c
        ).start()
    wait_bytes(got.at[pl.ds(0, n_grp - 1)], back_sem.at[1])
    wait_bytes(got.at[pl.ds(0, n_grp - 1)], back_sem.at[0])
    wait_bytes(several, spread_sem.at[0])
    packed = [got[:, pair].reshape(n_grp * ROWS, LANES) for pair in (0, 1)]
    solved = reorder(jnp.concatenate(packed, axis=1), phase_matrix(False, True))
    target = solved.reshape(n_grp, ROWS, COLS) - previous_in[...]
    wait_bytes(others, verdict_sem.at[1])
    lane = lax.broadcasted_iota(jnp.int32, (2, LANES), 1)
    summary = jnp.zeros((2, LANES), F32)
    for probe in range(n_grp):
        pair = verdicts[probe]
        summary = jnp.where(lane == probe, pair, summary)
        rest = target[probe] - pair[0:1, 0:1] * vector_in[probe]
        made = rest * (1.0 / pair[1:2, 0:1])
        for half in (0, 1):
            out[2 * probe + half][...] = made[half * SUB : (half + 1) * SUB]
    coefficients[...] = summary[:, 0:n_grp]
    wait_bytes(others, verdict_sem.at[0])


def flat_levels():
    return jax.tree.flatten(level_scratch())


def spread_scratch():
    return [pltpu.VMEM((6, 2, 8 * ROWS, LANES), F32)] * 2 + [pltpu.VMEM((2, 8 * ROWS, LANES), F32)] * 2


VMEM = pl.BlockSpec(memory_space=pltpu.VMEM)
HBM = pl.BlockSpec(memory_space=pltpu.HBM)
LIMIT = 55091 * 1024


PIECES = 16


def shape(*dims):
    return jax.ShapeDtypeStruct(dims, F32)


def step_kernel(conductance, shift, vector_hbm, previous_hbm, *rest):
    out, coefficients, scratch = rest[:PIECES], rest[PIECES], rest[PIECES + 1 :]
    leaves, tree = flat_levels()
    count = len(leaves)
    levels_refs = jax.tree.unflatten(tree, scratch[:count])
    (own_out, halo_out, phased, before, vector_in, previous_in, own, halo, vector, vector_halo, previous, told, got, heard, verdicts, loads) = scratch[count : count + 16]
    semaphores = scratch[count + 16 :]
    g, c = lax.axis_index("grp"), lax.axis_index("col")
    n_col = lax.axis_size("col")
    loading = [
        pltpu.make_async_copy(conductance, own.at[g, pl.ds(0, 4)], loads.at[0]),
        pltpu.make_async_copy(shift, own.at[g, 4], loads.at[1]),
        pltpu.make_async_copy(vector_hbm, vector_in, loads.at[2]),
        pltpu.make_async_copy(previous_hbm, previous_in, loads.at[3]),
    ]
    for copy in loading:
        copy.start()
    barrier = pltpu.get_barrier_semaphore()
    partners = [(g, to) for to in column_mates(c)] + [(to, c) for to in group_mates(g)]
    for grp, col in partners:
        pl.semaphore_signal(barrier, inc=1, device_id=(grp, col), device_id_type=MESH)
    for copy in loading[:2]:
        copy.wait()

    def vectors_loaded():
        for copy in loading[2:]:
            copy.wait()
        vector[g] = vector_in[g]
        previous[g] = previous_in[g]

    pl.semaphore_wait(barrier, len(partners))
    wait_vectors, wait_previous, wait_sends = gather(
        g, c, vector_in, previous_in, own, halo, vector, vector_halo, previous, semaphores[:7], vectors_loaded, lambda: spread_own(own, own_out)
    )
    compute(c, halo, vector, vector_halo, previous, levels_refs, own_out, halo_out, phased, before, (wait_vectors, wait_previous))
    conclude_all(g, c, vector_in, previous_in, phased, told, got, heard, verdicts, out, coefficients, semaphores[7:], lambda: make_told(told, phased, own_out, before), wait_sends)


def store_kernel(*refs):
    made, told = refs[:PIECES], refs[PIECES]
    out, coefficients, semaphores = refs[PIECES + 1 :]
    copies = [pltpu.make_async_copy(told, coefficients, semaphores.at[PIECES])]
    for piece in range(PIECES):
        strip = out.at[piece // 2, pl.ds(piece % 2 * SUB, SUB)]
        copies.append(pltpu.make_async_copy(made[piece], strip, semaphores.at[piece]))
    for copy in copies:
        copy.start()
    for copy in copies:
        copy.wait()


def local(conductance, shift, vector_in, previous_in):
    n_col = lax.axis_size("col")
    leaves, _ = flat_levels()
    tile = (8, ROWS, COLS)
    made = pl.pallas_call(
        step_kernel,
        out_shape=(shape(SUB, COLS),) * PIECES + (shape(2, 8),),
        in_specs=[HBM] * 4,
        out_specs=(VMEM,) * (PIECES + 1),
        scratch_shapes=leaves
        + spread_scratch()
        + [
            pltpu.VMEM(dims, F32)
            for dims in (
                tile,
                tile,
                (8, 5, ROWS, COLS),
                (8, 2, 5, ROWS, LANES),
                tile,
                (2, 8, ROWS, LANES),
                tile,
                (1, LANES),
            )
        ]
        + finish_scratch(n_col)
        + [pltpu.SemaphoreType.DMA((4,))]
        + gather_semaphores()
        + finish_semaphores(),
        compiler_params=pltpu.CompilerParams(
            collective_id=0, has_side_effects=True, vmem_limit_bytes=LIMIT
        ),
        name="lanczos_step",
    )(conductance, shift, vector_in, previous_in)
    return pl.pallas_call(
        store_kernel,
        out_shape=(shape(8, ROWS, COLS), shape(2, 8)),
        in_specs=[VMEM] * (PIECES + 1),
        out_specs=(HBM, HBM),
        scratch_shapes=[pltpu.SemaphoreType.DMA((PIECES + 1,))],
        compiler_params=pltpu.CompilerParams(vmem_limit_bytes=1024 * 1024),
        name="store",
    )(*made)


def solution(mesh):
    in_specs = (
        P(None, "grp", "col"),
        P("grp", "col"),
        P(None, "grp", "col"),
        P(None, "grp", "col"),
    )
    out_specs = (P(None, "grp", "col"), P())
    return jax.shard_map(local, mesh=mesh, in_specs=in_specs, out_specs=out_specs, check_vma=False)
```
